32 devices in a mesh: tm: 4 (over z), det: 8 (over y, x, core).
Axes of the slice: x: 2, y: 2, z: 4, core: 2. Of those that a mesh axis runs over, the one named last changes fastest.
Arguments:
- noise: float32 [512, 16384], P('det', 'tm'), may hold values from -6 to 6
- factor: float32 [8, 512, 512], P('det', 'tm'), may hold values from -8 to 8, as said below
Outputs:
- correlated: float32 [512, 16384], P('det', 'tm')
The draws below stay inside these ranges and needn't reach their ends.
Inputs may be any that keep to these rules, and one draw needn't show every extreme that they name: factor[b] is lower triangular with a positive diagonal, and factor[b] equals factor[7 - b].
All inputs are finite; a program needn't handle non-finite values.
Results may differ from the reference program's by a relative error of at most 0.00007.
Values sent between devices are 32-bit elements; how exact they have to be, the bound alone decides.
No kernel may reach another device: no remote copies, remote signals or barrier semaphores. Data moves between devices by JAX's collectives and lax.ppermute only.
A program may use at most 64 MiB of HBM per device.

```python
import math
import jax
import jax.numpy as jnp
from jax import lax

DET = 512
BW = 2048
NB = 8
NSAMP = 16384


def draw_factor(key, part):
    key_lower, key_diag = jax.random.split(key)
    half = NB // 2
    lower = jnp.clip(jax.random.normal(key_lower, (half, DET, DET), jnp.float32), -6.0, 6.0)
    diagonal = jax.random.uniform(key_diag, (half, DET), jnp.float32, 0.6, 1.4)
    lower = jnp.tril(lower, -1) * (0.8 / math.sqrt(DET))
    bands = jnp.arange(half, dtype=jnp.int32)
    folded = (bands + 1).astype(jnp.float32)
    amplitude = jnp.sqrt(NB / (2.0 * folded))
    matrix = lower + jnp.eye(DET, dtype=jnp.float32)[None, :, :] * diagonal[:, :, None]
    matrix = matrix * amplitude[:, None, None]
    return jnp.concatenate([matrix, matrix[::-1]], axis=0)


def level_of(own_key, extent, shards, least, high):
    factor_of, own = 1.0, jax.random.fold_in(own_key, 6)
    for dim, shards_of in shards:
        steps = jnp.exp(jax.random.uniform(jax.random.fold_in(own, dim), (shards_of,), jnp.float32, least / len(shards), high / len(shards)))
        factor_of = factor_of * jnp.repeat(steps, extent[dim] // shards_of).reshape([-1 if axis == dim else 1 for axis in range(len(extent))])
    return factor_of


def gaussian(key, dims, width, limit, shards=(), kind=jnp.bfloat16):
    entries = jax.random.normal(key, dims, jnp.float32) * width
    if len(shards) > 0:
        entries = level_of(key, dims, shards, -0.22, 0.18) * entries
    return jnp.clip(entries, min=-limit, max=limit).astype(kind)


def setup_inputs(seed: int = 0) -> dict:
    seeds = jax.random.split(jax.random.key(seed), 3)
    noise = gaussian(seeds[0], (DET, NSAMP), 1.0, 6.0, ((0, 8), (1, 4)), jnp.float32)
    factor = draw_factor(jax.random.fold_in(seeds[2], 71), 0)
    return dict(noise=noise, factor=factor)


def shift_phase(count):
    steps = jnp.arange(count, dtype=jnp.int32)
    return jnp.exp(-1j * jnp.pi * steps / count)


def forward_rows(values):
    count = values.shape[1]
    spectrum = jnp.fft.fft(values * shift_phase(count)[None, :], axis=1)
    return jnp.real(spectrum) - jnp.imag(spectrum)


def inverse_rows(values):
    count = values.shape[1]
    spectrum = jnp.fft.fft(values, axis=1) * shift_phase(count)[None, :]
    return (jnp.real(spectrum) - jnp.imag(spectrum)) / count


def reference(noise, factor):
    spectrum = forward_rows(noise).astype(jnp.float32)
    blocks = spectrum.reshape(DET, NB, BW)
    mixed = jnp.einsum('bij,jbk->ibk', factor, blocks, precision=lax.Precision.HIGHEST).reshape(DET, NSAMP)
    return inverse_rows(mixed).astype(jnp.float32)
```

```python
import math

import jax
import jax.numpy as jnp
import ml_dtypes
import numpy as np
from jax import lax
from jax.experimental import pallas as pl
from jax.experimental.pallas import tpu as pltpu
from jax.sharding import PartitionSpec as P


LANES = 128
VMEM_LIMIT = 48 * 1024 * 1024


def fourier_matrix(n2, planes):
    share = n2 // (2 * planes)
    order = []
    for plane in range(planes):
        low = np.arange(plane * share, (plane + 1) * share)
        order.append(np.concatenate([low, n2 - 1 - low[::-1]]))
    order = np.stack(order)
    angle = 2.0 * np.pi / n2 * (np.arange(n2)[:, None, None] * order[None] % n2)
    cosine, sine = np.cos(angle), np.sin(angle)
    matrix = np.stack([np.stack([cosine, -sine], 2), np.stack([sine, cosine], 2)])
    matrix = matrix.reshape(2 * n2, 2 * n2).astype(np.float32)
    high = matrix.astype(ml_dtypes.bfloat16)
    low = (matrix - high.astype(np.float32)).astype(ml_dtypes.bfloat16)
    return high, low


def twiddles(n1, n2):
    angle = 2.0 * np.pi / (n1 * n2) * (np.arange(n1)[:, None] + 0.25) * np.arange(n2)[None, :]
    return np.cos(angle).astype(np.float32), np.sin(angle).astype(np.float32)


def forward_butterflies(parts, shift):
    count = len(parts)
    if count == 1:
        return parts
    half = count // 2
    turn_re, turn_im = math.cos(math.pi * shift), -math.sin(math.pi * shift)
    even, odd = [], []
    for (a_re, a_im), (b_re, b_im) in zip(parts[:half], parts[half:]):
        c_re = b_re * turn_re - b_im * turn_im
        c_im = b_re * turn_im + b_im * turn_re
        even.append((a_re + c_re, a_im + c_im))
        odd.append((a_re - c_re, a_im - c_im))
    even = forward_butterflies(even, shift / 2)
    odd = forward_butterflies(odd, (1 + shift) / 2)
    return [part for pair in zip(even, odd) for part in pair]


def inverse_butterflies(parts, shift):
    if len(parts) == 1:
        return parts
    turn_re, turn_im = math.cos(math.pi * shift), math.sin(math.pi * shift)
    even = inverse_butterflies(parts[0::2], shift / 2)
    odd = inverse_butterflies(parts[1::2], (1 + shift) / 2)
    first, second = [], []
    for (a_re, a_im), (b_re, b_im) in zip(even, odd):
        d_re, d_im = a_re - b_re, a_im - b_im
        first.append((a_re + b_re, a_im + b_im))
        second.append((d_re * turn_re - d_im * turn_im, d_re * turn_im + d_im * turn_re))
    return first + second


def split(value):
    high = value.astype(jnp.bfloat16)
    return high, (value - high.astype(jnp.float32)).astype(jnp.bfloat16)


def product(left, right, contract=((1,), (0,))):
    def dot(a, b):
        return lax.dot_general(a, b, (contract, ((), ())), preferred_element_type=jnp.float32)

    return dot(left[0], right[0]) + (dot(left[0], right[1]) + dot(left[1], right[0]))


def tiles(rows, lanes):
    step = min(8, rows)
    for row in range(0, rows, step):
        for lane in range(0, lanes, LANES):
            yield slice(row, row + step), lane


def forward_kernel(n1, n2, x_ref, cos_ref, sin_ref, high_ref, low_ref, out_ref, mid_ref):
    blocks, dets, span = x_ref.shape
    per = span // n2
    for rows, lane in tiles(dets, n2):

        def load(index):
            start = (index % per) * n2 + lane
            return x_ref[index // per, rows, start : start + LANES]

        parts = [(load(t1), -load(t1 + n1)) for t1 in range(n1)]
        for k1, (re, im) in enumerate(forward_butterflies(parts, 0.25)):
            cosine = cos_ref[k1 : k1 + 1, lane : lane + LANES]
            sine = sin_ref[k1 : k1 + 1, lane : lane + LANES]
            place = slice(k1 * dets + rows.start, k1 * dets + rows.stop)
            mid_ref[place, lane : lane + LANES] = re * cosine + im * sine
            mid_ref[place, n2 + lane : n2 + lane + LANES] = im * cosine - re * sine
    spectrum = product(split(mid_ref[...]), (high_ref[...], low_ref[...]))
    planes, _, width = out_ref.shape
    for plane in range(planes):
        out_ref[plane] = spectrum[:, plane * width : (plane + 1) * width]


def inverse_kernel(n1, n2, y_ref, cos_ref, sin_ref, high_ref, low_ref, out_ref, mid_ref):
    blocks, dets, span = out_ref.shape
    per = span // n2
    scale = 1.0 / (n1 * n2)
    bins = jnp.concatenate([y_ref[plane] for plane in range(y_ref.shape[0])], axis=1)
    mid_ref[...] = product(split(bins), (high_ref[...], low_ref[...]), ((1,), (1,)))
    for rows, lane in tiles(dets, n2):
        parts = []
        for k1 in range(n1):
            cosine = cos_ref[k1 : k1 + 1, lane : lane + LANES] * scale
            sine = sin_ref[k1 : k1 + 1, lane : lane + LANES] * scale
            place = slice(k1 * dets + rows.start, k1 * dets + rows.stop)
            re = mid_ref[place, lane : lane + LANES]
            im = mid_ref[place, n2 + lane : n2 + lane + LANES]
            parts.append((re * cosine - im * sine, im * cosine + re * sine))
        for t1, (re, im) in enumerate(inverse_butterflies(parts, 0.25)):
            for index, value in ((t1, re), (t1 + n1, -im)):
                start = (index % per) * n2 + lane
                out_ref[index // per, rows, start : start + LANES] = value


def mix_kernel(x_ref, factor_ref, out_ref, x_mid, y_mid):
    planes, groups, pieces, dets, width = x_ref.shape
    places = [
        (plane, group, piece, slice((group * planes + plane) * dets, (group * planes + plane + 1) * dets),
         slice(piece * width, (piece + 1) * width))
        for plane in range(planes) for group in range(groups) for piece in range(pieces)
    ]
    for plane, group, piece, rows, lanes in places:
        x_mid[rows, lanes] = x_ref[plane, group, piece]
    count = factor_ref.shape[0]
    half = count // 2
    f_high, f_low = split(factor_ref[...])
    x_high, x_low = split(x_mid[...])
    y_mid[:half] = product((f_high[:half, :half], f_low[:half, :half]), (x_high[:half], x_low[:half]))
    y_mid[half:] = product((f_high[half:], f_low[half:]), (x_high, x_low))
    for plane, group, piece, rows, lanes in places:
        out_ref[plane, group, piece] = y_mid[rows, lanes]


def call(kernel, out_shape, scratch, flops, *args):
    whole = pl.BlockSpec(memory_space=pltpu.VMEM)
    count = sum(math.prod(arg.shape) * arg.dtype.itemsize for arg in args) + math.prod(out_shape) * 4
    return pl.pallas_call(
        kernel,
        out_shape=jax.ShapeDtypeStruct(out_shape, jnp.float32),
        in_specs=[whole] * len(args),
        out_specs=whole,
        scratch_shapes=[pltpu.VMEM(shape, jnp.float32) for shape in scratch],
        compiler_params=pltpu.CompilerParams(vmem_limit_bytes=VMEM_LIMIT),
        cost_estimate=pl.CostEstimate(flops=flops, bytes_accessed=count, transcendentals=0),
    )(*args)


def band_factor(factor, planes, groups):
    half = factor.shape[1] // 2
    upper = lax.axis_index("det") >= groups // 2
    mine = lax.dynamic_slice_in_dim(factor[0], jnp.where(upper, half, 0), half, 0)
    pairs = []
    for plane in range(planes):
        for group in range(groups):
            target = min(group, groups - 1 - group)
            pairs.append((plane * groups + group, target * groups + 2 * plane + (group >= groups // 2)))
    share = lax.ppermute(mine, ("tm", "det"), pairs)
    return lax.all_gather(share, "det", axis=0, tiled=True)


def local(noise, factor):
    planes = lax.axis_size("tm")
    groups = lax.axis_size("det")
    rows, span = noise.shape
    dets = rows // planes
    n2 = LANES // 2 * planes
    n1 = span * planes // 2 // n2
    pieces = n1 // groups
    high, low = fourier_matrix(n2, planes)
    cosine, sine = twiddles(n1, n2)
    flops = 3 * 2 * n1 * dets * (2 * n2) ** 2

    matrix = band_factor(factor, planes, groups)
    series = lax.all_to_all(noise, "tm", split_axis=0, concat_axis=0, tiled=True).reshape(planes, dets, span)
    spectrum = call(
        lambda *refs: forward_kernel(n1, n2, *refs), (planes, n1 * dets, LANES), [(n1 * dets, 2 * n2)], flops,
        series, cosine, sine, high, low,
    )
    spread = lax.all_to_all(
        spectrum.reshape(planes * groups, pieces * dets, LANES), ("tm", "det"), split_axis=0, concat_axis=0, tiled=True
    )
    count = matrix.shape[0]
    mixed = call(
        mix_kernel, (planes, groups, pieces, dets, LANES), [(count, pieces * LANES)] * 2,
        2 * 3 * count * count * pieces * LANES,
        spread.reshape(planes, groups, pieces, dets, LANES), matrix,
    )
    back = lax.all_to_all(
        mixed.reshape(planes * groups, pieces * dets, LANES), ("tm", "det"), split_axis=0, concat_axis=0, tiled=True
    )
    signal = call(
        lambda *refs: inverse_kernel(n1, n2, *refs), (planes, dets, span), [(n1 * dets, 2 * n2)], flops,
        back.reshape(planes, n1 * dets, LANES), cosine, sine, high, low,
    )
    return lax.all_to_all(signal.reshape(rows, span), "tm", split_axis=0, concat_axis=0, tiled=True)


def solution(mesh):
    in_specs = (P("det", "tm"), P("det", "tm", None))
    return jax.shard_map(local, mesh=mesh, in_specs=in_specs, out_specs=P("det", "tm"), check_vma=False)
```

```python
import math

import jax
import jax.numpy as jnp
import ml_dtypes
import numpy as np
from jax import lax
from jax.experimental import pallas as pl
from jax.experimental.pallas import tpu as pltpu
from jax.sharding import PartitionSpec as P


LANES = 128
VMEM_LIMIT = 48 * 1024 * 1024


def fourier_matrix(n2, planes):
    share = n2 // (2 * planes)
    order = []
    for plane in range(planes):
        low = np.arange(plane * share, (plane + 1) * share)
        order.append(np.concatenate([low, n2 - 1 - low[::-1]]))
    order = np.stack(order)
    angle = 2.0 * np.pi / n2 * (np.arange(n2)[:, None, None] * order[None] % n2)
    cosine, sine = np.cos(angle), np.sin(angle)
    matrix = np.stack([np.stack([cosine, -sine], 2), np.stack([sine, cosine], 2)])
    matrix = matrix.reshape(2 * n2, 2 * n2).astype(np.float32)
    high = matrix.astype(ml_dtypes.bfloat16)
    low = (matrix - high.astype(np.float32)).astype(ml_dtypes.bfloat16)
    return high, low


def twiddles(n1, n2):
    angle = 2.0 * np.pi / (n1 * n2) * (np.arange(n1)[:, None] + 0.25) * np.arange(n2)[None, :]
    return np.cos(angle).astype(np.float32), np.sin(angle).astype(np.float32)


def forward_butterflies(parts, shift):
    count = len(parts)
    if count == 1:
        return parts
    half = count // 2
    turn_re, turn_im = math.cos(math.pi * shift), -math.sin(math.pi * shift)
    even, odd = [], []
    for (a_re, a_im), (b_re, b_im) in zip(parts[:half], parts[half:]):
        c_re = b_re * turn_re - b_im * turn_im
        c_im = b_re * turn_im + b_im * turn_re
        even.append((a_re + c_re, a_im + c_im))
        odd.append((a_re - c_re, a_im - c_im))
    even = forward_butterflies(even, shift / 2)
    odd = forward_butterflies(odd, (1 + shift) / 2)
    return [part for pair in zip(even, odd) for part in pair]


def inverse_butterflies(parts, shift):
    if len(parts) == 1:
        return parts
    turn_re, turn_im = math.cos(math.pi * shift), math.sin(math.pi * shift)
    even = inverse_butterflies(parts[0::2], shift / 2)
    odd = inverse_butterflies(parts[1::2], (1 + shift) / 2)
    first, second = [], []
    for (a_re, a_im), (b_re, b_im) in zip(even, odd):
        d_re, d_im = a_re - b_re, a_im - b_im
        first.append((a_re + b_re, a_im + b_im))
        second.append((d_re * turn_re - d_im * turn_im, d_re * turn_im + d_im * turn_re))
    return first + second


def split(value):
    high = value.astype(jnp.bfloat16)
    return high, (value - high.astype(jnp.float32)).astype(jnp.bfloat16)


def product(left, right, contract=((1,), (0,))):
    def dot(a, b):
        return lax.dot_general(a, b, (contract, ((), ())), preferred_element_type=jnp.float32)

    return dot(left[0], right[0]) + (dot(left[0], right[1]) + dot(left[1], right[0]))


def tiles(rows, lanes):
    step = min(8, rows)
    for row in range(0, rows, step):
        for lane in range(0, lanes, LANES):
            yield slice(row, row + step), lane


def forward_kernel(n1, n2, noise_ref, *refs):
    here = lax.axis_index("tm")
    blocks, dets, span = noise_ref.shape
    others, (cos_ref, sin_ref, high_ref, low_ref, out_ref, x_ref, mid_ref) = refs[: blocks - 1], refs[blocks - 1 :]
    x_ref[here] = noise_ref[here]
    for step, other in enumerate(others, 1):
        x_ref[here ^ step] = other[...]
    per = span // n2
    for rows, lane in tiles(dets, n2):

        def load(index):
            start = (index % per) * n2 + lane
            return x_ref[index // per, rows, start : start + LANES]

        parts = [(load(t1), -load(t1 + n1)) for t1 in range(n1)]
        for k1, (re, im) in enumerate(forward_butterflies(parts, 0.25)):
            cosine = cos_ref[k1 : k1 + 1, lane : lane + LANES]
            sine = sin_ref[k1 : k1 + 1, lane : lane + LANES]
            place = slice(k1 * dets + rows.start, k1 * dets + rows.stop)
            mid_ref[place, lane : lane + LANES] = re * cosine + im * sine
            mid_ref[place, n2 + lane : n2 + lane + LANES] = im * cosine - re * sine
    spectrum = product(split(mid_ref[...]), (high_ref[...], low_ref[...]))
    planes, _, width = out_ref.shape
    for plane in range(planes):
        out_ref[plane] = spectrum[:, plane * width : (plane + 1) * width]


def inverse_kernel(n1, n2, y_ref, cos_ref, sin_ref, high_ref, low_ref, *refs):
    here = lax.axis_index("tm")
    outs, (out_ref, mid_ref) = refs[:-2], refs[-2:]
    blocks, dets, span = out_ref.shape
    per = span // n2
    scale = 1.0 / (n1 * n2)
    bins = jnp.concatenate([y_ref[plane] for plane in range(y_ref.shape[0])], axis=1)
    mid_ref[...] = product(split(bins), (high_ref[...], low_ref[...]), ((1,), (1,)))
    for rows, lane in tiles(dets, n2):
        parts = []
        for k1 in range(n1):
            cosine = cos_ref[k1 : k1 + 1, lane : lane + LANES] * scale
            sine = sin_ref[k1 : k1 + 1, lane : lane + LANES] * scale
            place = slice(k1 * dets + rows.start, k1 * dets + rows.stop)
            re = mid_ref[place, lane : lane + LANES]
            im = mid_ref[place, n2 + lane : n2 + lane + LANES]
            parts.append((re * cosine - im * sine, im * cosine + re * sine))
        for t1, (re, im) in enumerate(inverse_butterflies(parts, 0.25)):
            for index, value in ((t1, re), (t1 + n1, -im)):
                start = (index % per) * n2 + lane
                out_ref[index // per, rows, start : start + LANES] = value
    for step, out in enumerate(outs):
        out[...] = out_ref[here ^ step]


def factor_kernel(masks, factor_ref, high_ref, low_ref):
    here = lax.axis_index("det")
    shares, rows, _ = factor_ref.shape
    for share in range(shares):
        source = here
        for bit, mask in enumerate(masks):
            source = source ^ (mask if share >> bit & 1 else 0)
        place = pl.ds(pl.multiple_of(source * rows, rows), rows)
        high_ref[place], low_ref[place] = split(factor_ref[share])


def mix_kernel(x_ref, f_high, f_low, out_ref, x_mid, y_mid):
    planes, groups, pieces, dets, width = x_ref.shape
    places = [
        (plane, group, piece, slice((group * planes + plane) * dets, (group * planes + plane + 1) * dets),
         slice(piece * width, (piece + 1) * width))
        for plane in range(planes) for group in range(groups) for piece in range(pieces)
    ]
    for plane, group, piece, rows, lanes in places:
        x_mid[rows, lanes] = x_ref[plane, group, piece]
    half = f_high.shape[0] // 2
    x_high, x_low = split(x_mid[...])
    y_mid[:half] = product((f_high[:half, :half], f_low[:half, :half]), (x_high[:half], x_low[:half]))
    y_mid[half:] = product((f_high[half:, :], f_low[half:, :]), (x_high, x_low))
    for plane, group, piece, rows, lanes in places:
        out_ref[plane, group, piece] = y_mid[rows, lanes]


def call(kernel, outs, scratch, flops, *args):
    whole = pl.BlockSpec(memory_space=pltpu.VMEM)
    count = sum(math.prod(arg.shape) * arg.dtype.itemsize for arg in (*args, *outs))
    return pl.pallas_call(
        kernel,
        out_shape=outs,
        in_specs=[whole] * len(args),
        out_specs=[whole] * len(outs),
        scratch_shapes=[pltpu.VMEM(shape, jnp.float32) for shape in scratch],
        compiler_params=pltpu.CompilerParams(vmem_limit_bytes=VMEM_LIMIT),
        cost_estimate=pl.CostEstimate(flops=flops, bytes_accessed=count, transcendentals=0),
    )(*args)


def array(*shape, dtype=jnp.float32):
    return jax.ShapeDtypeStruct(shape, dtype)


def swap(value, axis, mask):
    return lax.ppermute(value, axis, [(place, place ^ mask) for place in range(lax.axis_size(axis))])


def band_factor(factor, planes, groups):
    half = factor.shape[1] // 2
    upper = lax.axis_index("det") >= groups // 2
    mine = lax.dynamic_slice_in_dim(factor[0], jnp.where(upper, half, 0), half, 0)
    pairs = []
    for plane in range(planes):
        for group in range(groups):
            target = min(group, groups - 1 - group)
            pairs.append((plane * groups + group, target * groups + 2 * plane + (group >= groups // 2)))
    share = lax.ppermute(mine, ("tm", "det"), pairs)[None]
    masks = [2**bit for bit in range(1, groups.bit_length() - 1)] + [1]
    for mask in masks:
        share = jnp.concatenate([share, swap(share, "det", mask)])
    whole = array(groups * half, factor.shape[2], dtype=jnp.bfloat16)
    return call(lambda *refs: factor_kernel(masks, *refs), [whole, whole], [], 0, share)


def local(noise, factor):
    planes = lax.axis_size("tm")
    groups = lax.axis_size("det")
    here = lax.axis_index("tm")
    rows, span = noise.shape
    dets = rows // planes
    n2 = LANES // 2 * planes
    n1 = span * planes // 2 // n2
    pieces = n1 // groups
    high, low = fourier_matrix(n2, planes)
    cosine, sine = twiddles(n1, n2)
    flops = 3 * 2 * n1 * dets * (2 * n2) ** 2
    series = (planes, dets, span)
    middle = (n1 * dets, 2 * n2)

    blocks = noise.reshape(series)
    others = [swap(lax.dynamic_index_in_dim(blocks, here ^ step, keepdims=False), "tm", step) for step in range(1, planes)]
    f_high, f_low = band_factor(factor, planes, groups)
    (spectrum,) = call(
        lambda *refs: forward_kernel(n1, n2, *refs), [array(planes, n1 * dets, LANES)], [series, middle], flops,
        blocks, *others, cosine, sine, high, low,
    )
    spread = lax.all_to_all(
        spectrum.reshape(planes * groups, pieces * dets, LANES), ("tm", "det"), split_axis=0, concat_axis=0, tiled=True
    )
    count = f_high.shape[0]
    (mixed,) = call(
        mix_kernel, [array(planes, groups, pieces, dets, LANES)], [(count, pieces * LANES)] * 2,
        2 * 3 * count * count * pieces * LANES,
        spread.reshape(planes, groups, pieces, dets, LANES), f_high, f_low,
    )
    back = lax.all_to_all(
        mixed.reshape(planes * groups, pieces * dets, LANES), ("tm", "det"), split_axis=0, concat_axis=0, tiled=True
    )
    parts = call(
        lambda *refs: inverse_kernel(n1, n2, *refs), [array(dets, span)] * planes, [series, middle], flops,
        back.reshape(planes, n1 * dets, LANES), cosine, sine, high, low,
    )
    result = jnp.zeros(series, jnp.float32)
    for step, part in enumerate(parts):
        part = swap(part, "tm", step) if step else part
        result = lax.dynamic_update_index_in_dim(result, part, here ^ step, 0)
    return result.reshape(rows, span)


def solution(mesh):
    in_specs = (P("det", "tm"), P("det", "tm", None))
    return jax.shard_map(local, mesh=mesh, in_specs=in_specs, out_specs=P("det", "tm"), check_vma=False)
```

```python
import math

import jax
import jax.numpy as jnp
import ml_dtypes
import numpy as np
from jax import lax
from jax.experimental import pallas as pl
from jax.experimental.pallas import tpu as pltpu
from jax.sharding import PartitionSpec as P


LANES = 128
VMEM_LIMIT = 48 * 1024 * 1024
CHUNKS = 1


def fourier_matrix(n2, planes):
    share = n2 // (2 * planes)
    order = []
    for plane in range(planes):
        low = np.arange(plane * share, (plane + 1) * share)
        order.append(np.concatenate([low, n2 - 1 - low[::-1]]))
    order = np.stack(order)
    angle = 2.0 * np.pi / n2 * (np.arange(n2)[:, None, None] * order[None] % n2)
    cosine, sine = np.cos(angle), np.sin(angle)
    matrix = np.stack([np.stack([cosine, -sine], 2), np.stack([sine, cosine], 2)])
    matrix = matrix.reshape(2 * n2, 2 * n2).astype(np.float32)
    high = matrix.astype(ml_dtypes.bfloat16)
    low = (matrix - high.astype(np.float32)).astype(ml_dtypes.bfloat16)
    return high, low


def twiddles(n1, n2):
    angle = 2.0 * np.pi / (n1 * n2) * (np.arange(n1)[:, None] + 0.25) * np.arange(n2)[None, :]
    return np.stack([np.cos(angle), np.sin(angle)]).astype(np.float32)


def forward_butterflies(parts, shift):
    count = len(parts)
    if count == 1:
        return parts
    half = count // 2
    turn_re, turn_im = math.cos(math.pi * shift), -math.sin(math.pi * shift)
    even, odd = [], []
    for (a_re, a_im), (b_re, b_im) in zip(parts[:half], parts[half:]):
        c_re = b_re * turn_re - b_im * turn_im
        c_im = b_re * turn_im + b_im * turn_re
        even.append((a_re + c_re, a_im + c_im))
        odd.append((a_re - c_re, a_im - c_im))
    even = forward_butterflies(even, shift / 2)
    odd = forward_butterflies(odd, (1 + shift) / 2)
    return [part for pair in zip(even, odd) for part in pair]


def inverse_butterflies(parts, shift):
    if len(parts) == 1:
        return parts
    turn_re, turn_im = math.cos(math.pi * shift), math.sin(math.pi * shift)
    even = inverse_butterflies(parts[0::2], shift / 2)
    odd = inverse_butterflies(parts[1::2], (1 + shift) / 2)
    first, second = [], []
    for (a_re, a_im), (b_re, b_im) in zip(even, odd):
        d_re, d_im = a_re - b_re, a_im - b_im
        first.append((a_re + b_re, a_im + b_im))
        second.append((d_re * turn_re - d_im * turn_im, d_re * turn_im + d_im * turn_re))
    return first + second


def split(value):
    high = value.astype(jnp.bfloat16)
    return high, (value - high.astype(jnp.float32)).astype(jnp.bfloat16)


def product(left, right, contract=((1,), (0,))):
    def dot(a, b):
        return lax.dot_general(a, b, (contract, ((), ())), preferred_element_type=jnp.float32)

    return dot(left[0], right[0]) + (dot(left[0], right[1]) + dot(left[1], right[0]))


def tiles(rows, lanes):
    step = min(8, rows)
    for row in range(0, rows, step):
        for lane in range(0, lanes, LANES):
            yield slice(row, row + step), lane


def slice_kernel(chunk, noise_ref, *refs):
    here = lax.axis_index("tm")
    outs, sem = refs[:-1], refs[-1]
    copies = [
        pltpu.make_async_copy(noise_ref.at[here ^ step, chunk], out, sem.at[step]) for step, out in enumerate(outs)
    ]
    for copy in copies:
        copy.start()
    for copy in copies:
        copy.wait()


def hold_kernel(*refs):
    count = len(refs) // 2
    sem = refs[-1]
    copies = [pltpu.make_async_copy(refs[at], refs[count + at], sem.at[at]) for at in range(count)]
    for copy in copies:
        copy.start()
    for copy in copies:
        copy.wait()


def forward_kernel(n1, n2, chunk, planes, *refs):
    here = lax.axis_index("tm")
    blocks, (turn_ref, high_ref, low_ref) = refs[:planes], refs[planes : planes + 3]
    out_ref, x_ref, mid_ref, stage_ref, sem = refs[-5:]
    _, dets, span = x_ref.shape
    _, groups, pieces, _, width = stage_ref.shape
    per = span // n2
    for step, block in enumerate(blocks):
        x_ref[here ^ step] = block[...]
    for rows, lane in tiles(dets, n2):

        def load(index):
            start = (index % per) * n2 + lane
            return x_ref[index // per, rows, start : start + LANES]

        parts = [(load(t1), -load(t1 + n1)) for t1 in range(n1)]
        for k1, (re, im) in enumerate(forward_butterflies(parts, 0.25)):
            cosine = turn_ref[0, k1 : k1 + 1, lane : lane + LANES]
            sine = turn_ref[1, k1 : k1 + 1, lane : lane + LANES]
            place = slice(k1 * dets + rows.start, k1 * dets + rows.stop)
            mid_ref[place, lane : lane + LANES] = re * cosine + im * sine
            mid_ref[place, n2 + lane : n2 + lane + LANES] = im * cosine - re * sine
    copies = []
    share = groups // 2
    for part in range(2):
        count = share * pieces * dets
        spectrum = product(split(mid_ref[part * count : (part + 1) * count]), (high_ref[...], low_ref[...]))
        these = pl.ds(part * share, share)
        for plane in range(planes):
            value = spectrum[:, plane * width : (plane + 1) * width]
            stage_ref[plane, these] = value.reshape(share, pieces, dets, width)
        copies.append(pltpu.make_async_copy(stage_ref.at[:, these], out_ref.at[:, these, chunk], sem.at[part]))
        copies[-1].start()
    for copy in copies:
        copy.wait()


def inverse_kernel(n1, n2, chunk, y_ref, turn_ref, high_ref, low_ref, *refs):
    here = lax.axis_index("tm")
    outs, (x_ref, mid_ref) = refs[:-2], refs[-2:]
    _, dets, span = x_ref.shape
    planes, _, _, _, _, width = y_ref.shape
    per = span // n2
    scale = 1.0 / (n1 * n2)
    bins = jnp.concatenate([y_ref[plane, :, chunk].reshape(n1 * dets, width) for plane in range(planes)], axis=1)
    mid_ref[...] = product(split(bins), (high_ref[...], low_ref[...]), ((1,), (1,)))
    for rows, lane in tiles(dets, n2):
        parts = []
        for k1 in range(n1):
            cosine = turn_ref[0, k1 : k1 + 1, lane : lane + LANES] * scale
            sine = turn_ref[1, k1 : k1 + 1, lane : lane + LANES] * scale
            place = slice(k1 * dets + rows.start, k1 * dets + rows.stop)
            re = mid_ref[place, lane : lane + LANES]
            im = mid_ref[place, n2 + lane : n2 + lane + LANES]
            parts.append((re * cosine - im * sine, im * cosine + re * sine))
        for t1, (re, im) in enumerate(inverse_butterflies(parts, 0.25)):
            for index, value in ((t1, re), (t1 + n1, -im)):
                start = (index % per) * n2 + lane
                x_ref[index // per, rows, start : start + LANES] = value
    for step, out in enumerate(outs):
        out[...] = x_ref[here ^ step]


def place_kernel(chunk, *refs):
    here = lax.axis_index("tm")
    out_ref, sem = refs[-2:]
    copies = [
        pltpu.make_async_copy(refs[step], out_ref.at[here ^ step, chunk], sem.at[step])
        for step in range(out_ref.shape[0])
    ]
    for copy in copies:
        copy.start()
    for copy in copies:
        copy.wait()


def factor_kernel(masks, factor_ref, high_ref, low_ref):
    here = lax.axis_index("det")
    shares, rows, _ = factor_ref.shape
    for share in range(shares):
        source = here
        for bit, mask in enumerate(masks):
            source = source ^ (mask if share >> bit & 1 else 0)
        place = pl.ds(pl.multiple_of(source * rows, rows), rows)
        high_ref[place], low_ref[place] = split(factor_ref[share])


def mix_kernel(x_ref, f_high, f_low, out_ref, x_mid, stage_ref, sem):
    planes, groups, chunks, pieces, dets, width = x_ref.shape

    def rows_of(group, plane, chunk):
        start = ((group * planes + plane) * chunks + chunk) * dets
        return slice(start, start + dets)

    places = [
        (plane, group, chunk, piece)
        for group in range(groups) for plane in range(planes) for chunk in range(chunks) for piece in range(pieces)
    ]
    for plane, group, chunk, piece in places:
        x_mid[rows_of(group, plane, chunk), piece * width : (piece + 1) * width] = x_ref[plane, group, chunk, piece]
    x_high, x_low = split(x_mid[...])
    steps = 4
    count, share = f_high.shape[0] // steps, groups // steps
    copies = []
    for step in range(steps):
        rows, reach = slice(step * count, (step + 1) * count), (step + 1) * count
        value = product((f_high[rows, :reach], f_low[rows, :reach]), (x_high[:reach], x_low[:reach]))
        for plane, group, chunk, piece in places:
            if group // share == step:
                own = rows_of(group - step * share, plane, chunk)
                stage_ref[plane, group, chunk, piece] = value[own, piece * width : (piece + 1) * width]
        these = pl.ds(step * share, share)
        copies.append(pltpu.make_async_copy(stage_ref.at[:, these], out_ref.at[:, these], sem.at[step]))
        copies[-1].start()
    for copy in copies:
        copy.wait()


def call(kernel, outs, scratch, flops, *args, spaces=None, out_space=pltpu.VMEM, aliases=None):
    spaces = spaces or [pltpu.VMEM] * len(args)
    count = sum(math.prod(arg.shape) * arg.dtype.itemsize for arg in (*args, *outs))
    return pl.pallas_call(
        kernel,
        out_shape=outs,
        in_specs=[pl.BlockSpec(memory_space=space) for space in spaces],
        out_specs=[pl.BlockSpec(memory_space=out_space)] * len(outs),
        scratch_shapes=[pltpu.VMEM(item, jnp.float32) if isinstance(item, tuple) else item for item in scratch],
        compiler_params=pltpu.CompilerParams(vmem_limit_bytes=VMEM_LIMIT),
        cost_estimate=pl.CostEstimate(flops=flops, bytes_accessed=count, transcendentals=0),
        input_output_aliases=aliases or {},
    )(*args)


def array(*shape, dtype=jnp.float32):
    return jax.ShapeDtypeStruct(shape, dtype)


def dma(count):
    return pltpu.SemaphoreType.DMA((count,))


def swap(value, axis, mask):
    return lax.ppermute(value, axis, [(place, place ^ mask) for place in range(lax.axis_size(axis))])


def band_factor(factor, planes, groups):
    half = factor.shape[1] // 2
    upper = lax.axis_index("det") >= groups // 2
    mine = lax.dynamic_slice_in_dim(factor[0], jnp.where(upper, half, 0), half, 0)
    pairs = []
    for plane in range(planes):
        for group in range(groups):
            target = min(group, groups - 1 - group)
            pairs.append((plane * groups + group, target * groups + 2 * plane + (group >= groups // 2)))
    share = lax.ppermute(mine, ("tm", "det"), pairs)[None]
    masks = [2**bit for bit in range(1, groups.bit_length() - 1)] + [1]
    for mask in masks:
        share = jnp.concatenate([share, swap(share, "det", mask)])
    whole = array(groups * half, factor.shape[2], dtype=jnp.bfloat16)
    return call(lambda *refs: factor_kernel(masks, *refs), [whole, whole], [], 0, share)


def bind(kernel, *static):
    return lambda *refs: kernel(*static, *refs)


def local(noise, factor):
    planes = lax.axis_size("tm")
    groups = lax.axis_size("det")
    rows, span = noise.shape
    n2 = LANES // 2 * planes
    n1 = span * planes // 2 // n2
    pieces = n1 // groups
    chunks = CHUNKS if rows // planes % (8 * CHUNKS) == 0 else 1
    dets = rows // planes // chunks
    flops = 3 * 2 * n1 * dets * (2 * n2) ** 2
    block, series, middle = array(dets, span), (planes, dets, span), (n1 * dets, 2 * n2)
    layout = (planes, groups, chunks, pieces, dets, LANES)
    tables = (twiddles(n1, n2), *fourier_matrix(n2, planes))

    noise = noise.reshape(planes, chunks, dets, span)
    arrived = []
    for chunk in range(chunks):
        parts = call(bind(slice_kernel, chunk), [block] * planes, [dma(planes)], 0, noise, spaces=[pl.ANY])
        arrived.append([swap(part, "tm", step) if step else part for step, part in enumerate(parts)])
    f_high, f_low = band_factor(factor, planes, groups)
    tables = call(
        hold_kernel, [array(*table.shape, dtype=table.dtype) for table in tables], [dma(len(tables))], 0, *tables,
        spaces=[pl.ANY] * len(tables),
    )
    arrived, f_high, f_low = lax.optimization_barrier((arrived, f_high, f_low))
    buffer = []
    for chunk in range(chunks):
        buffer = call(
            bind(forward_kernel, n1, n2, chunk, planes), [array(*layout)],
            [series, middle, (planes, groups, pieces, dets, LANES), dma(2)], flops,
            *arrived[chunk], *tables, *buffer,
            spaces=[pltpu.VMEM] * (planes + len(tables)) + [pl.ANY] * len(buffer),
            out_space=pl.ANY, aliases={planes + len(tables): 0} if buffer else None,
        )

    def exchange(value):
        value = value.reshape(planes * groups, chunks * pieces * dets, LANES)
        return lax.all_to_all(value, ("tm", "det"), split_axis=0, concat_axis=0, tiled=True).reshape(layout)

    count = f_high.shape[0]
    (mixed,) = call(
        mix_kernel, [array(*layout)], [(count, pieces * LANES), layout, dma(4)],
        2 * 3 * count * count * pieces * LANES,
        exchange(buffer[0]), f_high, f_low, out_space=pl.ANY,
    )
    back = exchange(mixed)
    result = []
    for chunk in range(chunks):
        parts = call(
            bind(inverse_kernel, n1, n2, chunk), [block] * planes, [series, middle], flops, back, *tables
        )
        parts = [swap(part, "tm", step) if step else part for step, part in enumerate(parts)]
        result = call(
            bind(place_kernel, chunk), [array(planes, chunks, dets, span)], [dma(planes)], 0, *parts, *result,
            spaces=[pl.ANY] * (planes + len(result)), out_space=pl.ANY, aliases={planes: 0} if result else None,
        )
    return result[0].reshape(rows, span)


def solution(mesh):
    in_specs = (P("det", "tm"), P("det", "tm", None))
    return jax.shard_map(local, mesh=mesh, in_specs=in_specs, out_specs=P("det", "tm"), check_vma=False)
```

```python
import math

import jax
import jax.numpy as jnp
import ml_dtypes
import numpy as np
from jax import lax
from jax.experimental import pallas as pl
from jax.experimental.pallas import tpu as pltpu
from jax.sharding import PartitionSpec as P


LANES = 128
VMEM_LIMIT = 48 * 1024 * 1024
CHUNKS = 1


def fourier_matrix(n2, planes):
    share = n2 // (2 * planes)
    order = []
    for plane in range(planes):
        low = np.arange(plane * share, (plane + 1) * share)
        order.append(np.concatenate([low, n2 - 1 - low[::-1]]))
    order = np.stack(order)
    angle = 2.0 * np.pi / n2 * (np.arange(n2)[:, None, None] * order[None] % n2)
    cosine, sine = np.cos(angle), np.sin(angle)
    matrix = np.stack([np.stack([cosine, -sine], 2), np.stack([sine, cosine], 2)])
    matrix = matrix.reshape(2 * n2, 2 * n2).astype(np.float32)
    high = matrix.astype(ml_dtypes.bfloat16)
    low = (matrix - high.astype(np.float32)).astype(ml_dtypes.bfloat16)
    return high, low


def twiddles(n1, n2):
    angle = 2.0 * np.pi / (n1 * n2) * (np.arange(n1)[:, None] + 0.25) * np.arange(n2)[None, :]
    return np.stack([np.cos(angle), np.sin(angle)]).astype(np.float32)


def forward_butterflies(parts, shift):
    count = len(parts)
    if count == 1:
        return parts
    half = count // 2
    turn_re, turn_im = math.cos(math.pi * shift), -math.sin(math.pi * shift)
    even, odd = [], []
    for (a_re, a_im), (b_re, b_im) in zip(parts[:half], parts[half:]):
        c_re = b_re * turn_re - b_im * turn_im
        c_im = b_re * turn_im + b_im * turn_re
        even.append((a_re + c_re, a_im + c_im))
        odd.append((a_re - c_re, a_im - c_im))
    even = forward_butterflies(even, shift / 2)
    odd = forward_butterflies(odd, (1 + shift) / 2)
    return [part for pair in zip(even, odd) for part in pair]


def inverse_butterflies(parts, shift):
    if len(parts) == 1:
        return parts
    turn_re, turn_im = math.cos(math.pi * shift), math.sin(math.pi * shift)
    even = inverse_butterflies(parts[0::2], shift / 2)
    odd = inverse_butterflies(parts[1::2], (1 + shift) / 2)
    first, second = [], []
    for (a_re, a_im), (b_re, b_im) in zip(even, odd):
        d_re, d_im = a_re - b_re, a_im - b_im
        first.append((a_re + b_re, a_im + b_im))
        second.append((d_re * turn_re - d_im * turn_im, d_re * turn_im + d_im * turn_re))
    return first + second


def split(value):
    high = value.astype(jnp.bfloat16)
    return high, (value - high.astype(jnp.float32)).astype(jnp.bfloat16)


def product(left, right, contract=((1,), (0,))):
    def dot(a, b):
        return lax.dot_general(a, b, (contract, ((), ())), preferred_element_type=jnp.float32)

    return dot(left[0], right[0]) + (dot(left[0], right[1]) + dot(left[1], right[0]))


def tiles(rows, lanes):
    step = min(8, rows)
    for row in range(0, rows, step):
        for lane in range(0, lanes, LANES):
            yield slice(row, row + step), lane


def slice_kernel(chunk, noise_ref, *refs):
    here = lax.axis_index("tm")
    outs, sem = refs[:-1], refs[-1]
    copies = [
        pltpu.make_async_copy(noise_ref.at[here ^ step, chunk], out, sem.at[step]) for step, out in enumerate(outs)
    ]
    for copy in copies:
        copy.start()
    for copy in copies:
        copy.wait()


def hold_kernel(*refs):
    count = len(refs) // 2
    sem = refs[-1]
    copies = [pltpu.make_async_copy(refs[at], refs[count + at], sem.at[at]) for at in range(count)]
    for copy in copies:
        copy.start()
    for copy in copies:
        copy.wait()


def forward_kernel(n1, n2, chunk, planes, *refs):
    here = lax.axis_index("tm")
    blocks, (turn_ref, high_ref, low_ref) = refs[:planes], refs[planes : planes + 3]
    out_ref, x_ref, mid_ref, stage_ref, sem = refs[-5:]
    _, dets, span = x_ref.shape
    _, groups, pieces, _, width = stage_ref.shape
    per = span // n2
    for step, block in enumerate(blocks):
        x_ref[here ^ step] = block[...]
    for rows, lane in tiles(dets, n2):

        def load(index):
            start = (index % per) * n2 + lane
            return x_ref[index // per, rows, start : start + LANES]

        parts = [(load(t1), -load(t1 + n1)) for t1 in range(n1)]
        for k1, (re, im) in enumerate(forward_butterflies(parts, 0.25)):
            cosine = turn_ref[0, k1 : k1 + 1, lane : lane + LANES]
            sine = turn_ref[1, k1 : k1 + 1, lane : lane + LANES]
            place = slice(k1 * dets + rows.start, k1 * dets + rows.stop)
            mid_ref[place, lane : lane + LANES] = re * cosine + im * sine
            mid_ref[place, n2 + lane : n2 + lane + LANES] = im * cosine - re * sine
    copies = []
    share = groups // 2
    for part in range(2):
        count = share * pieces * dets
        spectrum = product(split(mid_ref[part * count : (part + 1) * count]), (high_ref[...], low_ref[...]))
        these = pl.ds(part * share, share)
        for plane in range(planes):
            value = spectrum[:, plane * width : (plane + 1) * width]
            stage_ref[plane, these] = value.reshape(share, pieces, dets, width)
        copies.append(pltpu.make_async_copy(stage_ref.at[:, these], out_ref.at[:, these, chunk], sem.at[part]))
        copies[-1].start()
    for copy in copies:
        copy.wait()


def inverse_kernel(n1, n2, chunk, y_ref, turn_ref, high_ref, low_ref, *refs):
    here = lax.axis_index("tm")
    outs, (x_ref, mid_ref) = refs[:-2], refs[-2:]
    _, dets, span = x_ref.shape
    planes, _, _, _, _, width = y_ref.shape
    per = span // n2
    scale = 1.0 / (n1 * n2)
    bins = jnp.concatenate([y_ref[plane, :, chunk].reshape(n1 * dets, width) for plane in range(planes)], axis=1)
    mid_ref[...] = product(split(bins), (high_ref[...], low_ref[...]), ((1,), (1,)))
    for rows, lane in tiles(dets, n2):
        parts = []
        for k1 in range(n1):
            cosine = turn_ref[0, k1 : k1 + 1, lane : lane + LANES] * scale
            sine = turn_ref[1, k1 : k1 + 1, lane : lane + LANES] * scale
            place = slice(k1 * dets + rows.start, k1 * dets + rows.stop)
            re = mid_ref[place, lane : lane + LANES]
            im = mid_ref[place, n2 + lane : n2 + lane + LANES]
            parts.append((re * cosine - im * sine, im * cosine + re * sine))
        for t1, (re, im) in enumerate(inverse_butterflies(parts, 0.25)):
            for index, value in ((t1, re), (t1 + n1, -im)):
                start = (index % per) * n2 + lane
                x_ref[index // per, rows, start : start + LANES] = value
    for step, out in enumerate(outs):
        out[...] = x_ref[here ^ step]


def place_kernel(chunk, *refs):
    here = lax.axis_index("tm")
    out_ref, sem = refs[-2:]
    copies = [
        pltpu.make_async_copy(refs[step], out_ref.at[here ^ step, chunk], sem.at[step])
        for step in range(out_ref.shape[0])
    ]
    for copy in copies:
        copy.start()
    for copy in copies:
        copy.wait()


def factor_kernel(masks, factor_ref, high_ref, low_ref):
    here = lax.axis_index("det")
    shares, rows, _ = factor_ref.shape
    for share in range(shares):
        source = here
        for bit, mask in enumerate(masks):
            source = source ^ (mask if share >> bit & 1 else 0)
        place = pl.ds(pl.multiple_of(source * rows, rows), rows)
        high_ref[place], low_ref[place] = split(factor_ref[share])


def mix_kernel(x_ref, f_high, f_low, out_ref, x_mid, stage_ref, sem):
    planes, groups, chunks, pieces, dets, width = x_ref.shape

    def rows_of(group, plane, chunk):
        start = ((group * planes + plane) * chunks + chunk) * dets
        return slice(start, start + dets)

    places = [
        (plane, group, chunk, piece)
        for group in range(groups) for plane in range(planes) for chunk in range(chunks) for piece in range(pieces)
    ]
    for plane, group, chunk, piece in places:
        x_mid[rows_of(group, plane, chunk), piece * width : (piece + 1) * width] = x_ref[plane, group, chunk, piece]
    x_high, x_low = split(x_mid[...])
    steps = 4
    count, share = f_high.shape[0] // steps, groups // steps
    copies = []
    for step in range(steps):
        rows, reach = slice(step * count, (step + 1) * count), (step + 1) * count
        value = product((f_high[rows, :reach], f_low[rows, :reach]), (x_high[:reach], x_low[:reach]))
        for plane, group, chunk, piece in places:
            if group // share == step:
                own = rows_of(group - step * share, plane, chunk)
                stage_ref[plane, group, chunk, piece] = value[own, piece * width : (piece + 1) * width]
        these = pl.ds(step * share, share)
        copies.append(pltpu.make_async_copy(stage_ref.at[:, these], out_ref.at[:, these], sem.at[step]))
        copies[-1].start()
    for copy in copies:
        copy.wait()


def call(kernel, outs, scratch, flops, *args, spaces=None, out_space=pltpu.VMEM, aliases=None):
    spaces = spaces or [pltpu.VMEM] * len(args)
    count = sum(math.prod(arg.shape) * arg.dtype.itemsize for arg in (*args, *outs))
    return pl.pallas_call(
        kernel,
        out_shape=outs,
        in_specs=[pl.BlockSpec(memory_space=space) for space in spaces],
        out_specs=[pl.BlockSpec(memory_space=out_space)] * len(outs),
        scratch_shapes=[pltpu.VMEM(item, jnp.float32) if isinstance(item, tuple) else item for item in scratch],
        compiler_params=pltpu.CompilerParams(vmem_limit_bytes=VMEM_LIMIT),
        cost_estimate=pl.CostEstimate(flops=flops, bytes_accessed=count, transcendentals=0),
        input_output_aliases=aliases or {},
    )(*args)


def array(*shape, dtype=jnp.float32):
    return jax.ShapeDtypeStruct(shape, dtype)


def dma(count):
    return pltpu.SemaphoreType.DMA((count,))


def swap(value, axis, mask):
    return lax.ppermute(value, axis, [(place, place ^ mask) for place in range(lax.axis_size(axis))])


def plane_factor(factor, planes, groups):
    half = factor.shape[1] // 2
    upper = lax.axis_index("det") >= groups // 2
    mine = lax.dynamic_slice_in_dim(factor[0], jnp.where(upper, half, 0), half, 0)
    pairs = []
    for plane in range(planes):
        for group in range(groups):
            target = min(group, groups - 1 - group)
            pairs.append((plane * groups + group, target * groups + 2 * plane + (group >= groups // 2)))
    return lax.ppermute(mine, ("tm", "det"), pairs)


def band_factor(share, groups):
    rows, columns = share.shape
    share = share[None]
    masks = [2**bit for bit in range(1, groups.bit_length() - 1)] + [1]
    for mask in masks:
        share = jnp.concatenate([share, swap(share, "det", mask)])
    whole = array(groups * rows, columns, dtype=jnp.bfloat16)
    return call(lambda *refs: factor_kernel(masks, *refs), [whole, whole], [], 0, share)


def bind(kernel, *static):
    return lambda *refs: kernel(*static, *refs)


def local(noise, factor):
    planes = lax.axis_size("tm")
    groups = lax.axis_size("det")
    rows, span = noise.shape
    n2 = LANES // 2 * planes
    n1 = span * planes // 2 // n2
    pieces = n1 // groups
    chunks = CHUNKS if rows // planes % (8 * CHUNKS) == 0 else 1
    dets = rows // planes // chunks
    flops = 3 * 2 * n1 * dets * (2 * n2) ** 2
    block, series, middle = array(dets, span), (planes, dets, span), (n1 * dets, 2 * n2)
    layout = (planes, groups, chunks, pieces, dets, LANES)
    tables = (twiddles(n1, n2), *fourier_matrix(n2, planes))

    noise = noise.reshape(planes, chunks, dets, span)
    arrived = []
    for chunk in range(chunks):
        parts = call(bind(slice_kernel, chunk), [block] * planes, [dma(planes)], 0, noise, spaces=[pl.ANY])
        arrived.append([swap(part, "tm", step) if step else part for step, part in enumerate(parts)])
    share = plane_factor(factor, planes, groups)
    tables = call(
        hold_kernel, [array(*table.shape, dtype=table.dtype) for table in tables], [dma(len(tables))], 0, *tables,
        spaces=[pl.ANY] * len(tables),
    )
    arrived, share = lax.optimization_barrier((arrived, share))
    f_high, f_low = band_factor(share, groups)
    buffer = []
    for chunk in range(chunks):
        buffer = call(
            bind(forward_kernel, n1, n2, chunk, planes), [array(*layout)],
            [series, middle, (planes, groups, pieces, dets, LANES), dma(2)], flops,
            *arrived[chunk], *tables, *buffer,
            spaces=[pltpu.VMEM] * (planes + len(tables)) + [pl.ANY] * len(buffer),
            out_space=pl.ANY, aliases={planes + len(tables): 0} if buffer else None,
        )

    def exchange(value):
        value = value.reshape(planes * groups, chunks * pieces * dets, LANES)
        return lax.all_to_all(value, ("tm", "det"), split_axis=0, concat_axis=0, tiled=True).reshape(layout)

    count = f_high.shape[0]
    (mixed,) = call(
        mix_kernel, [array(*layout)], [(count, pieces * LANES), layout, dma(4)],
        2 * 3 * count * count * pieces * LANES,
        exchange(buffer[0]), f_high, f_low, out_space=pl.ANY,
    )
    back = exchange(mixed)
    result = []
    for chunk in range(chunks):
        parts = call(
            bind(inverse_kernel, n1, n2, chunk), [block] * planes, [series, middle], flops, back, *tables
        )
        parts = [swap(part, "tm", step) if step else part for step, part in enumerate(parts)]
        result = call(
            bind(place_kernel, chunk), [array(planes, chunks, dets, span)], [dma(planes)], 0, *parts, *result,
            spaces=[pl.ANY] * (planes + len(result)), out_space=pl.ANY, aliases={planes: 0} if result else None,
        )
    return result[0].reshape(rows, span)


def solution(mesh):
    in_specs = (P("det", "tm"), P("det", "tm", None))
    return jax.shard_map(local, mesh=mesh, in_specs=in_specs, out_specs=P("det", "tm"), check_vma=False)
```

```python
import math

import jax
import jax.numpy as jnp
import ml_dtypes
import numpy as np
from jax import lax
from jax.experimental import pallas as pl
from jax.experimental.pallas import tpu as pltpu
from jax.sharding import PartitionSpec as P


LANES = 128
VMEM_LIMIT = 48 * 1024 * 1024
CHUNKS = 1


def band_of(plane, planes):
    return 2 * plane if 2 * plane < planes else 2 * (planes - 1 - plane) + 1


def fourier_matrix(n2, planes):
    share = n2 // (2 * planes)
    order = []
    for plane in range(planes):
        low = band_of(plane, planes) * share + np.arange(share)
        order.append(np.concatenate([low, n2 - 1 - low[::-1]]))
    order = np.stack(order)
    angle = 2.0 * np.pi / n2 * (np.arange(n2)[:, None, None] * order[None] % n2)
    cosine, sine = np.cos(angle), np.sin(angle)
    matrix = np.stack([np.stack([cosine, -sine], 2), np.stack([sine, cosine], 2)])
    matrix = matrix.reshape(2 * n2, 2 * n2).astype(np.float32)
    high = matrix.astype(ml_dtypes.bfloat16)
    low = (matrix - high.astype(np.float32)).astype(ml_dtypes.bfloat16)
    return high, low


def twiddles(n1, n2):
    angle = 2.0 * np.pi / (n1 * n2) * (np.arange(n1)[:, None] + 0.25) * np.arange(n2)[None, :]
    return np.stack([np.cos(angle), np.sin(angle)]).astype(np.float32)


def forward_butterflies(parts, shift):
    count = len(parts)
    if count == 1:
        return parts
    half = count // 2
    turn_re, turn_im = math.cos(math.pi * shift), -math.sin(math.pi * shift)
    even, odd = [], []
    for (a_re, a_im), (b_re, b_im) in zip(parts[:half], parts[half:]):
        c_re = b_re * turn_re - b_im * turn_im
        c_im = b_re * turn_im + b_im * turn_re
        even.append((a_re + c_re, a_im + c_im))
        odd.append((a_re - c_re, a_im - c_im))
    even = forward_butterflies(even, shift / 2)
    odd = forward_butterflies(odd, (1 + shift) / 2)
    return [part for pair in zip(even, odd) for part in pair]


def inverse_butterflies(parts, shift):
    if len(parts) == 1:
        return parts
    turn_re, turn_im = math.cos(math.pi * shift), math.sin(math.pi * shift)
    even = inverse_butterflies(parts[0::2], shift / 2)
    odd = inverse_butterflies(parts[1::2], (1 + shift) / 2)
    first, second = [], []
    for (a_re, a_im), (b_re, b_im) in zip(even, odd):
        d_re, d_im = a_re - b_re, a_im - b_im
        first.append((a_re + b_re, a_im + b_im))
        second.append((d_re * turn_re - d_im * turn_im, d_re * turn_im + d_im * turn_re))
    return first + second


def split(value):
    high = value.astype(jnp.bfloat16)
    return high, (value - high.astype(jnp.float32)).astype(jnp.bfloat16)


def product(left, right, contract=((1,), (0,))):
    def dot(a, b):
        return lax.dot_general(a, b, (contract, ((), ())), preferred_element_type=jnp.float32)

    return dot(left[0], right[0]) + (dot(left[0], right[1]) + dot(left[1], right[0]))


def tiles(rows, lanes):
    step = min(8, rows)
    for row in range(0, rows, step):
        for lane in range(0, lanes, LANES):
            yield slice(row, row + step), lane


def slice_kernel(chunk, noise_ref, *refs):
    here = lax.axis_index("tm")
    outs, sem = refs[:-1], refs[-1]
    copies = [
        pltpu.make_async_copy(noise_ref.at[here ^ step, chunk], out, sem.at[step]) for step, out in enumerate(outs)
    ]
    for copy in copies:
        copy.start()
    for copy in copies:
        copy.wait()


def hold_kernel(*refs):
    count = len(refs) // 2
    sem = refs[-1]
    copies = [pltpu.make_async_copy(refs[at], refs[count + at], sem.at[at]) for at in range(count)]
    for copy in copies:
        copy.start()
    for copy in copies:
        copy.wait()


def forward_kernel(n1, n2, chunk, planes, *refs):
    here = lax.axis_index("tm")
    blocks, (turn_ref, high_ref, low_ref) = refs[:planes], refs[planes : planes + 3]
    out_ref, x_ref, mid_ref, stage_ref, sem = refs[-5:]
    _, dets, span = x_ref.shape
    _, groups, pieces, _, width = stage_ref.shape
    per = span // n2
    for step, block in enumerate(blocks):
        x_ref[here ^ step] = block[...]
    for rows, lane in tiles(dets, n2):

        def load(index):
            start = (index % per) * n2 + lane
            return x_ref[index // per, rows, start : start + LANES]

        parts = [(load(t1), -load(t1 + n1)) for t1 in range(n1)]
        for k1, (re, im) in enumerate(forward_butterflies(parts, 0.25)):
            cosine = turn_ref[0, k1 : k1 + 1, lane : lane + LANES]
            sine = turn_ref[1, k1 : k1 + 1, lane : lane + LANES]
            place = slice(k1 * dets + rows.start, k1 * dets + rows.stop)
            mid_ref[place, lane : lane + LANES] = re * cosine + im * sine
            mid_ref[place, n2 + lane : n2 + lane + LANES] = im * cosine - re * sine
    copies = []
    share = groups // 2
    for part in range(2):
        count = share * pieces * dets
        spectrum = product(split(mid_ref[part * count : (part + 1) * count]), (high_ref[...], low_ref[...]))
        these = pl.ds(part * share, share)
        for plane in range(planes):
            value = spectrum[:, plane * width : (plane + 1) * width]
            stage_ref[plane, these] = value.reshape(share, pieces, dets, width)
        copies.append(pltpu.make_async_copy(stage_ref.at[:, these], out_ref.at[:, these, chunk], sem.at[part]))
        copies[-1].start()
    for copy in copies:
        copy.wait()


def inverse_kernel(n1, n2, chunk, y_ref, turn_ref, high_ref, low_ref, *refs):
    here = lax.axis_index("tm")
    outs, (x_ref, mid_ref) = refs[:-2], refs[-2:]
    _, dets, span = x_ref.shape
    planes, _, _, _, _, width = y_ref.shape
    per = span // n2
    scale = 1.0 / (n1 * n2)
    bins = jnp.concatenate([y_ref[plane, :, chunk].reshape(n1 * dets, width) for plane in range(planes)], axis=1)
    mid_ref[...] = product(split(bins), (high_ref[...], low_ref[...]), ((1,), (1,)))
    for rows, lane in tiles(dets, n2):
        parts = []
        for k1 in range(n1):
            cosine = turn_ref[0, k1 : k1 + 1, lane : lane + LANES] * scale
            sine = turn_ref[1, k1 : k1 + 1, lane : lane + LANES] * scale
            place = slice(k1 * dets + rows.start, k1 * dets + rows.stop)
            re = mid_ref[place, lane : lane + LANES]
            im = mid_ref[place, n2 + lane : n2 + lane + LANES]
            parts.append((re * cosine - im * sine, im * cosine + re * sine))
        for t1, (re, im) in enumerate(inverse_butterflies(parts, 0.25)):
            for index, value in ((t1, re), (t1 + n1, -im)):
                start = (index % per) * n2 + lane
                x_ref[index // per, rows, start : start + LANES] = value
    for step, out in enumerate(outs):
        out[...] = x_ref[here ^ step]


def place_kernel(chunk, *refs):
    here = lax.axis_index("tm")
    out_ref, sem = refs[-2:]
    copies = [
        pltpu.make_async_copy(refs[step], out_ref.at[here ^ step, chunk], sem.at[step])
        for step in range(out_ref.shape[0])
    ]
    for copy in copies:
        copy.start()
    for copy in copies:
        copy.wait()


def factor_kernel(factor_ref, high_ref, low_ref):
    here = lax.axis_index("det")
    shares, rows, _ = factor_ref.shape
    for share in range(shares):
        source = here ^ (2 * share if 2 * share < shares else 2 * share - shares + 1)
        place = pl.ds(pl.multiple_of(source * rows, rows), rows)
        high_ref[place], low_ref[place] = split(factor_ref[share])


def mix_kernel(x_ref, f_high, f_low, out_ref, x_mid, stage_ref, sem):
    planes, groups, chunks, pieces, dets, width = x_ref.shape

    def rows_of(group, plane, chunk):
        start = ((group * planes + plane) * chunks + chunk) * dets
        return slice(start, start + dets)

    places = [
        (plane, group, chunk, piece)
        for group in range(groups) for plane in range(planes) for chunk in range(chunks) for piece in range(pieces)
    ]
    for plane, group, chunk, piece in places:
        x_mid[rows_of(group, plane, chunk), piece * width : (piece + 1) * width] = x_ref[plane, group, chunk, piece]
    x_high, x_low = split(x_mid[...])
    steps = 4
    count, share = f_high.shape[0] // steps, groups // steps
    copies = []
    for step in range(steps):
        rows, reach = slice(step * count, (step + 1) * count), (step + 1) * count
        value = product((f_high[rows, :reach], f_low[rows, :reach]), (x_high[:reach], x_low[:reach]))
        for plane, group, chunk, piece in places:
            if group // share == step:
                own = rows_of(group - step * share, plane, chunk)
                stage_ref[plane, group, chunk, piece] = value[own, piece * width : (piece + 1) * width]
        these = pl.ds(step * share, share)
        copies.append(pltpu.make_async_copy(stage_ref.at[:, these], out_ref.at[:, these], sem.at[step]))
        copies[-1].start()
    for copy in copies:
        copy.wait()


def call(kernel, outs, scratch, flops, *args, spaces=None, out_space=pltpu.VMEM, aliases=None):
    spaces = spaces or [pltpu.VMEM] * len(args)
    count = sum(math.prod(arg.shape) * arg.dtype.itemsize for arg in (*args, *outs))
    return pl.pallas_call(
        kernel,
        out_shape=outs,
        in_specs=[pl.BlockSpec(memory_space=space) for space in spaces],
        out_specs=[pl.BlockSpec(memory_space=out_space)] * len(outs),
        scratch_shapes=[pltpu.VMEM(item, jnp.float32) if isinstance(item, tuple) else item for item in scratch],
        compiler_params=pltpu.CompilerParams(vmem_limit_bytes=VMEM_LIMIT),
        cost_estimate=pl.CostEstimate(flops=flops, bytes_accessed=count, transcendentals=0),
        input_output_aliases=aliases or {},
    )(*args)


def array(*shape, dtype=jnp.float32):
    return jax.ShapeDtypeStruct(shape, dtype)


def dma(count):
    return pltpu.SemaphoreType.DMA((count,))


def swap(value, axis, mask):
    return lax.ppermute(value, axis, [(place, place ^ mask) for place in range(lax.axis_size(axis))])


def spread_out(parts):
    return [swap(part, "tm", step) if step else part for step, part in reversed(list(enumerate(parts)))][::-1]


def plane_factor(factor, planes, groups):
    half = factor.shape[1] // 2
    upper = lax.axis_index("det") >= groups // 2
    mine = lax.dynamic_slice_in_dim(factor[0], jnp.where(upper, half, 0), half, 0)
    plane_of = {band_of(plane, planes): plane for plane in range(planes)}
    pairs = []
    for plane in range(planes):
        for group in range(groups):
            target = plane_of[min(group, groups - 1 - group)]
            pairs.append((plane * groups + group, target * groups + 2 * plane + (group >= groups // 2)))
    return lax.ppermute(mine, ("tm", "det"), pairs)


def band_factor(share, groups):
    rows, columns = share.shape
    share = jnp.stack([share] + [swap(share, "det", mask) for mask in range(2, groups, 2)])
    share = jnp.concatenate([share, swap(share, "det", 1)])
    whole = array(groups * rows, columns, dtype=jnp.bfloat16)
    return call(factor_kernel, [whole, whole], [], 0, share)


def bind(kernel, *static):
    return lambda *refs: kernel(*static, *refs)


def local(noise, factor):
    planes = lax.axis_size("tm")
    groups = lax.axis_size("det")
    rows, span = noise.shape
    n2 = LANES // 2 * planes
    n1 = span * planes // 2 // n2
    pieces = n1 // groups
    chunks = CHUNKS if rows // planes % (8 * CHUNKS) == 0 else 1
    dets = rows // planes // chunks
    flops = 3 * 2 * n1 * dets * (2 * n2) ** 2
    block, series, middle = array(dets, span), (planes, dets, span), (n1 * dets, 2 * n2)
    layout = (planes, groups, chunks, pieces, dets, LANES)
    tables = (twiddles(n1, n2), *fourier_matrix(n2, planes))

    noise = noise.reshape(planes, chunks, dets, span)
    arrived = []
    for chunk in range(chunks):
        parts = call(bind(slice_kernel, chunk), [block] * planes, [dma(planes)], 0, noise, spaces=[pl.ANY])
        arrived.append(spread_out(parts))
    tables = call(
        hold_kernel, [array(*table.shape, dtype=table.dtype) for table in tables], [dma(len(tables))], 0, *tables,
        spaces=[pl.ANY] * len(tables),
    )
    arrived, factor = lax.optimization_barrier((arrived, factor))
    f_high, f_low = band_factor(plane_factor(factor, planes, groups), groups)
    buffer = []
    for chunk in range(chunks):
        buffer = call(
            bind(forward_kernel, n1, n2, chunk, planes), [array(*layout)],
            [series, middle, (planes, groups, pieces, dets, LANES), dma(2)], flops,
            *arrived[chunk], *tables, *buffer,
            spaces=[pltpu.VMEM] * (planes + len(tables)) + [pl.ANY] * len(buffer),
            out_space=pl.ANY, aliases={planes + len(tables): 0} if buffer else None,
        )

    def exchange(value):
        value = value.reshape(planes * groups, chunks * pieces * dets, LANES)
        return lax.all_to_all(value, ("tm", "det"), split_axis=0, concat_axis=0, tiled=True).reshape(layout)

    count = f_high.shape[0]
    (mixed,) = call(
        mix_kernel, [array(*layout)], [(count, pieces * LANES), layout, dma(4)],
        2 * 3 * count * count * pieces * LANES,
        exchange(buffer[0]), f_high, f_low, out_space=pl.ANY,
    )
    back = exchange(mixed)
    result = []
    for chunk in range(chunks):
        parts = call(
            bind(inverse_kernel, n1, n2, chunk), [block] * planes, [series, middle], flops, back, *tables
        )
        parts = spread_out(parts)
        result = call(
            bind(place_kernel, chunk), [array(planes, chunks, dets, span)], [dma(planes)], 0, *parts, *result,
            spaces=[pl.ANY] * (planes + len(result)), out_space=pl.ANY, aliases={planes: 0} if result else None,
        )
    return result[0].reshape(rows, span)


def solution(mesh):
    in_specs = (P("det", "tm"), P("det", "tm", None))
    return jax.shard_map(local, mesh=mesh, in_specs=in_specs, out_specs=P("det", "tm"), check_vma=False)
```

```python
import math

import jax
import jax.numpy as jnp
import ml_dtypes
import numpy as np
from jax import lax
from jax.experimental import pallas as pl
from jax.experimental.pallas import tpu as pltpu
from jax.sharding import PartitionSpec as P


LANES = 128
VMEM_LIMIT = 48 * 1024 * 1024
CHUNKS = 1


def band_of(plane, planes):
    return 2 * plane if 2 * plane < planes else 2 * (planes - 1 - plane) + 1


def fourier_matrix(n2, planes):
    share = n2 // (2 * planes)
    order = []
    for plane in range(planes):
        low = band_of(plane, planes) * share + np.arange(share)
        order.append(np.concatenate([low, n2 - 1 - low[::-1]]))
    order = np.stack(order)
    angle = 2.0 * np.pi / n2 * (np.arange(n2)[:, None, None] * order[None] % n2)
    cosine, sine = np.cos(angle), np.sin(angle)
    matrix = np.stack([np.stack([cosine, -sine], 2), np.stack([sine, cosine], 2)])
    matrix = matrix.reshape(2 * n2, 2 * n2).astype(np.float32)
    high = matrix.astype(ml_dtypes.bfloat16)
    low = (matrix - high.astype(np.float32)).astype(ml_dtypes.bfloat16)
    return high, low


def twiddles(n1, n2):
    angle = 2.0 * np.pi / (n1 * n2) * (np.arange(n1)[:, None] + 0.25) * np.arange(n2)[None, :]
    return np.stack([np.cos(angle), np.sin(angle)]).astype(np.float32)


def forward_butterflies(parts, shift):
    count = len(parts)
    if count == 1:
        return parts
    half = count // 2
    turn_re, turn_im = math.cos(math.pi * shift), -math.sin(math.pi * shift)
    even, odd = [], []
    for (a_re, a_im), (b_re, b_im) in zip(parts[:half], parts[half:]):
        c_re = b_re * turn_re - b_im * turn_im
        c_im = b_re * turn_im + b_im * turn_re
        even.append((a_re + c_re, a_im + c_im))
        odd.append((a_re - c_re, a_im - c_im))
    even = forward_butterflies(even, shift / 2)
    odd = forward_butterflies(odd, (1 + shift) / 2)
    return [part for pair in zip(even, odd) for part in pair]


def inverse_butterflies(parts, shift):
    if len(parts) == 1:
        return parts
    turn_re, turn_im = math.cos(math.pi * shift), math.sin(math.pi * shift)
    even = inverse_butterflies(parts[0::2], shift / 2)
    odd = inverse_butterflies(parts[1::2], (1 + shift) / 2)
    first, second = [], []
    for (a_re, a_im), (b_re, b_im) in zip(even, odd):
        d_re, d_im = a_re - b_re, a_im - b_im
        first.append((a_re + b_re, a_im + b_im))
        second.append((d_re * turn_re - d_im * turn_im, d_re * turn_im + d_im * turn_re))
    return first + second


def split(value):
    high = value.astype(jnp.bfloat16)
    return high, (value - high.astype(jnp.float32)).astype(jnp.bfloat16)


def product(left, right, contract=((1,), (0,))):
    def dot(a, b):
        return lax.dot_general(a, b, (contract, ((), ())), preferred_element_type=jnp.float32)

    return dot(left[0], right[0]) + (dot(left[0], right[1]) + dot(left[1], right[0]))


def tiles(rows, lanes):
    step = min(8, rows)
    for row in range(0, rows, step):
        for lane in range(0, lanes, LANES):
            yield slice(row, row + step), lane


def slice_kernel(chunk, noise_ref, *refs):
    here = lax.axis_index("tm")
    outs, sem = refs[:-1], refs[-1]
    copies = [
        pltpu.make_async_copy(noise_ref.at[lax.rem(here + step, noise_ref.shape[0]), chunk], out, sem.at[step])
        for step, out in enumerate(outs)
    ]
    for copy in copies:
        copy.start()
    for copy in copies:
        copy.wait()


def hold_kernel(*refs):
    count = len(refs) // 2
    sem = refs[-1]
    copies = [pltpu.make_async_copy(refs[at], refs[count + at], sem.at[at]) for at in range(count)]
    for copy in copies:
        copy.start()
    for copy in copies:
        copy.wait()


def forward_kernel(n1, n2, chunk, planes, *refs):
    here = lax.axis_index("tm")
    blocks, (turn_ref, high_ref, low_ref) = refs[:planes], refs[planes : planes + 3]
    out_ref, x_ref, mid_ref, stage_ref, sem = refs[-5:]
    _, dets, span = x_ref.shape
    _, groups, pieces, _, width = stage_ref.shape
    per = span // n2
    for step, block in enumerate(blocks):
        x_ref[lax.rem(here + planes - step, planes)] = block[...]
    for rows, lane in tiles(dets, n2):

        def load(index):
            start = (index % per) * n2 + lane
            return x_ref[index // per, rows, start : start + LANES]

        parts = [(load(t1), -load(t1 + n1)) for t1 in range(n1)]
        for k1, (re, im) in enumerate(forward_butterflies(parts, 0.25)):
            cosine = turn_ref[0, k1 : k1 + 1, lane : lane + LANES]
            sine = turn_ref[1, k1 : k1 + 1, lane : lane + LANES]
            place = slice(k1 * dets + rows.start, k1 * dets + rows.stop)
            mid_ref[place, lane : lane + LANES] = re * cosine + im * sine
            mid_ref[place, n2 + lane : n2 + lane + LANES] = im * cosine - re * sine
    copies = []
    share = groups // 2
    for part in range(2):
        count = share * pieces * dets
        spectrum = product(split(mid_ref[part * count : (part + 1) * count]), (high_ref[...], low_ref[...]))
        these = pl.ds(part * share, share)
        for plane in range(planes):
            value = spectrum[:, plane * width : (plane + 1) * width]
            stage_ref[plane, these] = value.reshape(share, pieces, dets, width)
        copies.append(pltpu.make_async_copy(stage_ref.at[:, these], out_ref.at[:, these, chunk], sem.at[part]))
        copies[-1].start()
    for copy in copies:
        copy.wait()


def inverse_kernel(n1, n2, chunk, y_ref, turn_ref, high_ref, low_ref, *refs):
    here = lax.axis_index("tm")
    outs, (x_ref, mid_ref) = refs[:-2], refs[-2:]
    _, dets, span = x_ref.shape
    planes, _, _, _, _, width = y_ref.shape
    per = span // n2
    scale = 1.0 / (n1 * n2)
    bins = jnp.concatenate([y_ref[plane, :, chunk].reshape(n1 * dets, width) for plane in range(planes)], axis=1)
    mid_ref[...] = product(split(bins), (high_ref[...], low_ref[...]), ((1,), (1,)))
    for rows, lane in tiles(dets, n2):
        parts = []
        for k1 in range(n1):
            cosine = turn_ref[0, k1 : k1 + 1, lane : lane + LANES] * scale
            sine = turn_ref[1, k1 : k1 + 1, lane : lane + LANES] * scale
            place = slice(k1 * dets + rows.start, k1 * dets + rows.stop)
            re = mid_ref[place, lane : lane + LANES]
            im = mid_ref[place, n2 + lane : n2 + lane + LANES]
            parts.append((re * cosine - im * sine, im * cosine + re * sine))
        for t1, (re, im) in enumerate(inverse_butterflies(parts, 0.25)):
            for index, value in ((t1, re), (t1 + n1, -im)):
                start = (index % per) * n2 + lane
                x_ref[index // per, rows, start : start + LANES] = value
    for step, out in enumerate(outs):
        out[...] = x_ref[lax.rem(here + step, planes)]


def place_kernel(chunk, *refs):
    here = lax.axis_index("tm")
    out_ref, sem = refs[-2:]
    planes = out_ref.shape[0]
    copies = [
        pltpu.make_async_copy(refs[step], out_ref.at[lax.rem(here + planes - step, planes), chunk], sem.at[step])
        for step in range(planes)
    ]
    for copy in copies:
        copy.start()
    for copy in copies:
        copy.wait()


def factor_kernel(factor_ref, high_ref, low_ref):
    here = lax.axis_index("det")
    shares, rows, _ = factor_ref.shape
    for share in range(shares):
        source = here ^ (2 * share if 2 * share < shares else 2 * share - shares + 1)
        place = pl.ds(pl.multiple_of(source * rows, rows), rows)
        high_ref[place], low_ref[place] = split(factor_ref[share])


def mix_kernel(x_ref, f_high, f_low, out_ref, x_mid, y_mid):
    planes, groups, chunks, pieces, dets, width = x_ref.shape
    places = []
    for plane, group, chunk, piece in np.ndindex(planes, groups, chunks, pieces):
        start = ((group * planes + plane) * chunks + chunk) * dets
        rows, lanes = slice(start, start + dets), slice(piece * width, (piece + 1) * width)
        places.append(((plane, group, chunk, piece), (rows, lanes)))
    for source, target in places:
        x_mid[target] = x_ref[source]
    x_high, x_low = split(x_mid[...])
    half = f_high.shape[0] // 2
    y_mid[:half] = product((f_high[:half, :half], f_low[:half, :half]), (x_high[:half], x_low[:half]))
    y_mid[half:] = product((f_high[half:, :], f_low[half:, :]), (x_high, x_low))
    for target, source in places:
        out_ref[target] = y_mid[source]


def call(kernel, outs, scratch, flops, *args, spaces=None, out_space=pltpu.VMEM, aliases=None):
    spaces = spaces or [pltpu.VMEM] * len(args)
    count = sum(math.prod(arg.shape) * arg.dtype.itemsize for arg in (*args, *outs))
    return pl.pallas_call(
        kernel,
        out_shape=outs,
        in_specs=[pl.BlockSpec(memory_space=space) for space in spaces],
        out_specs=[pl.BlockSpec(memory_space=out_space)] * len(outs),
        scratch_shapes=[pltpu.VMEM(item, jnp.float32) if isinstance(item, tuple) else item for item in scratch],
        compiler_params=pltpu.CompilerParams(vmem_limit_bytes=VMEM_LIMIT),
        cost_estimate=pl.CostEstimate(flops=flops, bytes_accessed=count, transcendentals=0),
        input_output_aliases=aliases or {},
    )(*args)


def array(*shape, dtype=jnp.float32):
    return jax.ShapeDtypeStruct(shape, dtype)


def dma(count):
    return pltpu.SemaphoreType.DMA((count,))


def swap(value, axis, mask):
    return lax.ppermute(value, axis, [(place, place ^ mask) for place in range(lax.axis_size(axis))])


def rotate(parts):
    planes = len(parts)
    return [parts[0]] + [
        lax.ppermute(parts[step], "tm", [(place, (place + step) % planes) for place in range(planes)])
        for step in range(1, planes)
    ]


def plane_factor(factor, planes, groups):
    half = factor.shape[1] // 2
    upper = lax.axis_index("det") >= groups // 2
    mine = lax.dynamic_slice_in_dim(factor[0], jnp.where(upper, half, 0), half, 0)
    plane_of = {band_of(plane, planes): plane for plane in range(planes)}
    pairs = []
    for plane in range(planes):
        for group in range(groups):
            target = plane_of[min(group, groups - 1 - group)]
            pairs.append((plane * groups + group, target * groups + 2 * plane + (group >= groups // 2)))
    return lax.ppermute(mine, ("tm", "det"), pairs)


def band_factor(share, groups):
    rows, columns = share.shape
    share = jnp.stack([share] + [swap(share, "det", mask) for mask in range(2, groups, 2)])
    share = jnp.concatenate([share, swap(share, "det", 1)])
    whole = array(groups * rows, columns, dtype=jnp.bfloat16)
    return call(factor_kernel, [whole, whole], [], 0, share)


def bind(kernel, *static):
    return lambda *refs: kernel(*static, *refs)


def local(noise, factor):
    planes = lax.axis_size("tm")
    groups = lax.axis_size("det")
    rows, span = noise.shape
    n2 = LANES // 2 * planes
    n1 = span * planes // 2 // n2
    pieces = n1 // groups
    chunks = CHUNKS if rows // planes % (8 * CHUNKS) == 0 else 1
    dets = rows // planes // chunks
    flops = 3 * 2 * n1 * dets * (2 * n2) ** 2
    block, series, middle = array(dets, span), (planes, dets, span), (n1 * dets, 2 * n2)
    layout = (planes, groups, chunks, pieces, dets, LANES)
    tables = (twiddles(n1, n2), *fourier_matrix(n2, planes))

    noise = noise.reshape(planes, chunks, dets, span)
    arrived = []
    for chunk in range(chunks):
        parts = call(bind(slice_kernel, chunk), [block] * planes, [dma(planes)], 0, noise, spaces=[pltpu.HBM])
        arrived.append(rotate(parts))
    share = plane_factor(factor, planes, groups)
    tables = call(
        hold_kernel, [array(*table.shape, dtype=table.dtype) for table in tables], [dma(len(tables))], 0, *tables,
        spaces=[pl.ANY] * len(tables),
    )
    arrived, share = lax.optimization_barrier((arrived, share))
    f_high, f_low = band_factor(share, groups)
    buffer = []
    for chunk in range(chunks):
        buffer = call(
            bind(forward_kernel, n1, n2, chunk, planes), [array(*layout)],
            [series, middle, (planes, groups, pieces, dets, LANES), dma(2)], flops,
            *arrived[chunk], *tables, *buffer,
            spaces=[pltpu.VMEM] * (planes + len(tables)) + [pl.ANY] * len(buffer),
            out_space=pl.ANY, aliases={planes + len(tables): 0} if buffer else None,
        )

    def exchange(value):
        value = value.reshape(planes * groups, chunks * pieces * dets, LANES)
        return lax.all_to_all(value, ("tm", "det"), split_axis=0, concat_axis=0, tiled=True).reshape(layout)

    count = f_high.shape[0]
    (mixed,) = call(
        mix_kernel, [array(*layout)], [(count, pieces * LANES)] * 2,
        2 * 3 * count * count * pieces * LANES,
        exchange(buffer[0]), f_high, f_low,
    )
    back = exchange(mixed)
    result = []
    for chunk in range(chunks):
        parts = call(
            bind(inverse_kernel, n1, n2, chunk), [block] * planes, [series, middle], flops, back, *tables
        )
        parts = rotate(parts)
        result = call(
            bind(place_kernel, chunk), [array(planes, chunks, dets, span)], [dma(planes)], 0, *parts, *result,
            spaces=[pl.ANY] * (planes + len(result)), out_space=pl.ANY, aliases={planes: 0} if result else None,
        )
    return result[0].reshape(rows, span)


def solution(mesh):
    in_specs = (P("det", "tm"), P("det", "tm", None))
    return jax.shard_map(local, mesh=mesh, in_specs=in_specs, out_specs=P("det", "tm"), check_vma=False)
```

```python
import math

import jax
import jax.numpy as jnp
import ml_dtypes
import numpy as np
from jax import lax
from jax.experimental import pallas as pl
from jax.experimental.pallas import tpu as pltpu
from jax.sharding import PartitionSpec as P


LANES = 128
VMEM_LIMIT = 48 * 1024 * 1024
CHUNKS = 1


def band_of(plane, planes):
    return 2 * plane if 2 * plane < planes else 2 * (planes - 1 - plane) + 1


def fourier_matrix(n2, planes):
    share = n2 // (2 * planes)
    order = []
    for plane in range(planes):
        low = band_of(plane, planes) * share + np.arange(share)
        order.append(np.concatenate([low, n2 - 1 - low[::-1]]))
    order = np.stack(order)
    angle = 2.0 * np.pi / n2 * (np.arange(n2)[:, None, None] * order[None] % n2)
    cosine, sine = np.cos(angle), np.sin(angle)
    matrix = np.stack([np.stack([cosine, -sine], 2), np.stack([sine, cosine], 2)])
    matrix = matrix.reshape(2 * n2, 2 * n2).astype(np.float32)
    high = matrix.astype(ml_dtypes.bfloat16)
    low = (matrix - high.astype(np.float32)).astype(ml_dtypes.bfloat16)
    return high, low


def twiddles(n1, n2):
    angle = 2.0 * np.pi / (n1 * n2) * (np.arange(n1)[:, None] + 0.25) * np.arange(n2)[None, :]
    return np.stack([np.cos(angle), np.sin(angle)]).astype(np.float32)


def forward_butterflies(parts, shift):
    count = len(parts)
    if count == 1:
        return parts
    half = count // 2
    turn_re, turn_im = math.cos(math.pi * shift), -math.sin(math.pi * shift)
    even, odd = [], []
    for (a_re, a_im), (b_re, b_im) in zip(parts[:half], parts[half:]):
        c_re = b_re * turn_re - b_im * turn_im
        c_im = b_re * turn_im + b_im * turn_re
        even.append((a_re + c_re, a_im + c_im))
        odd.append((a_re - c_re, a_im - c_im))
    even = forward_butterflies(even, shift / 2)
    odd = forward_butterflies(odd, (1 + shift) / 2)
    return [part for pair in zip(even, odd) for part in pair]


def inverse_butterflies(parts, shift):
    if len(parts) == 1:
        return parts
    turn_re, turn_im = math.cos(math.pi * shift), math.sin(math.pi * shift)
    even = inverse_butterflies(parts[0::2], shift / 2)
    odd = inverse_butterflies(parts[1::2], (1 + shift) / 2)
    first, second = [], []
    for (a_re, a_im), (b_re, b_im) in zip(even, odd):
        d_re, d_im = a_re - b_re, a_im - b_im
        first.append((a_re + b_re, a_im + b_im))
        second.append((d_re * turn_re - d_im * turn_im, d_re * turn_im + d_im * turn_re))
    return first + second


def split(value):
    high = value.astype(jnp.bfloat16)
    return high, (value - high.astype(jnp.float32)).astype(jnp.bfloat16)


def product(left, right, contract=((1,), (0,))):
    def dot(a, b):
        return lax.dot_general(a, b, (contract, ((), ())), preferred_element_type=jnp.float32)

    return dot(left[0], right[0]) + (dot(left[0], right[1]) + dot(left[1], right[0]))


def tiles(rows, lanes):
    step = min(8, rows)
    for row in range(0, rows, step):
        for lane in range(0, lanes, LANES):
            yield slice(row, row + step), lane


def hold_kernel(*refs):
    count = len(refs) // 2
    sem = refs[-1]
    copies = [pltpu.make_async_copy(refs[at], refs[count + at], sem.at[at]) for at in range(count)]
    for copy in copies:
        copy.start()
    for copy in copies:
        copy.wait()


def forward_kernel(n1, n2, chunk, planes, *refs):
    here = lax.axis_index("tm")
    blocks, (turn_ref, high_ref, low_ref) = refs[:planes], refs[planes : planes + 3]
    out_ref, x_ref, mid_ref, stage_ref, sem = refs[-5:]
    _, dets, span = x_ref.shape
    _, groups, pieces, _, width = stage_ref.shape
    per = span // n2
    for step, block in enumerate(reversed(blocks)):
        x_ref[lax.rem(here + planes - step, planes)] = block[...]
    for rows, lane in tiles(dets, n2):

        def load(index):
            start = (index % per) * n2 + lane
            return x_ref[index // per, rows, start : start + LANES]

        parts = [(load(t1), -load(t1 + n1)) for t1 in range(n1)]
        for k1, (re, im) in enumerate(forward_butterflies(parts, 0.25)):
            cosine = turn_ref[0, k1 : k1 + 1, lane : lane + LANES]
            sine = turn_ref[1, k1 : k1 + 1, lane : lane + LANES]
            place = slice(k1 * dets + rows.start, k1 * dets + rows.stop)
            mid_ref[place, lane : lane + LANES] = re * cosine + im * sine
            mid_ref[place, n2 + lane : n2 + lane + LANES] = im * cosine - re * sine
    copies = []
    share = groups // 2
    for part in range(2):
        count = share * pieces * dets
        spectrum = product(split(mid_ref[part * count : (part + 1) * count]), (high_ref[...], low_ref[...]))
        these = pl.ds(part * share, share)
        for plane in range(planes):
            value = spectrum[:, plane * width : (plane + 1) * width]
            stage_ref[plane, these] = value.reshape(share, pieces, dets, width)
        copies.append(pltpu.make_async_copy(stage_ref.at[:, these], out_ref.at[:, these, chunk], sem.at[part]))
        copies[-1].start()
    for copy in copies:
        copy.wait()


def inverse_kernel(n1, n2, chunk, y_ref, turn_ref, high_ref, low_ref, *refs):
    here = lax.axis_index("tm")
    outs, (x_ref, mid_ref) = refs[:-2], refs[-2:]
    _, dets, span = x_ref.shape
    planes, _, _, _, _, width = y_ref.shape
    per = span // n2
    scale = 1.0 / (n1 * n2)
    bins = jnp.concatenate([y_ref[plane, :, chunk].reshape(n1 * dets, width) for plane in range(planes)], axis=1)
    mid_ref[...] = product(split(bins), (high_ref[...], low_ref[...]), ((1,), (1,)))
    for rows, lane in tiles(dets, n2):
        parts = []
        for k1 in range(n1):
            cosine = turn_ref[0, k1 : k1 + 1, lane : lane + LANES] * scale
            sine = turn_ref[1, k1 : k1 + 1, lane : lane + LANES] * scale
            place = slice(k1 * dets + rows.start, k1 * dets + rows.stop)
            re = mid_ref[place, lane : lane + LANES]
            im = mid_ref[place, n2 + lane : n2 + lane + LANES]
            parts.append((re * cosine - im * sine, im * cosine + re * sine))
        for t1, (re, im) in enumerate(inverse_butterflies(parts, 0.25)):
            for index, value in ((t1, re), (t1 + n1, -im)):
                start = (index % per) * n2 + lane
                x_ref[index // per, rows, start : start + LANES] = value
    for step, out in enumerate(outs):
        out[...] = x_ref[lax.rem(here + step, planes)]


def place_kernel(chunk, *refs):
    here = lax.axis_index("tm")
    out_ref, sem = refs[-2:]
    planes = out_ref.shape[0]
    copies = [
        pltpu.make_async_copy(refs[planes - 1 - step], out_ref.at[lax.rem(here + planes - step, planes), chunk], sem.at[step])
        for step in range(planes)
    ]
    for copy in copies:
        copy.start()
    for copy in copies:
        copy.wait()


def factor_kernel(factor_ref, high_ref, low_ref):
    here = lax.axis_index("det")
    shares, rows, _ = factor_ref.shape
    for share in range(shares):
        source = here ^ (2 * share if 2 * share < shares else 2 * share - shares + 1)
        place = pl.ds(pl.multiple_of(source * rows, rows), rows)
        high_ref[place], low_ref[place] = split(factor_ref[share])


def mix_kernel(x_ref, f_high, f_low, out_ref, x_mid, y_mid):
    planes, groups, chunks, pieces, dets, width = x_ref.shape
    places = []
    for plane, group, chunk, piece in np.ndindex(planes, groups, chunks, pieces):
        start = ((group * planes + plane) * chunks + chunk) * dets
        rows, lanes = slice(start, start + dets), slice(piece * width, (piece + 1) * width)
        places.append(((plane, group, chunk, piece), (rows, lanes)))
    for source, target in places:
        x_mid[target] = x_ref[source]
    x_high, x_low = split(x_mid[...])
    half = f_high.shape[0] // 2
    y_mid[:half] = product((f_high[:half, :half], f_low[:half, :half]), (x_high[:half], x_low[:half]))
    y_mid[half:] = product((f_high[half:, :], f_low[half:, :]), (x_high, x_low))
    for target, source in places:
        out_ref[target] = y_mid[source]


def call(kernel, outs, scratch, flops, *args, spaces=None, out_space=pltpu.VMEM, aliases=None):
    spaces = spaces or [pltpu.VMEM] * len(args)
    count = sum(math.prod(arg.shape) * arg.dtype.itemsize for arg in (*args, *outs))
    return pl.pallas_call(
        kernel,
        out_shape=outs,
        in_specs=[pl.BlockSpec(memory_space=space) for space in spaces],
        out_specs=[pl.BlockSpec(memory_space=out_space)] * len(outs),
        scratch_shapes=[pltpu.VMEM(item, jnp.float32) if isinstance(item, tuple) else item for item in scratch],
        compiler_params=pltpu.CompilerParams(vmem_limit_bytes=VMEM_LIMIT),
        cost_estimate=pl.CostEstimate(flops=flops, bytes_accessed=count, transcendentals=0),
        input_output_aliases=aliases or {},
    )(*args)


def array(*shape, dtype=jnp.float32):
    return jax.ShapeDtypeStruct(shape, dtype)


def dma(count):
    return pltpu.SemaphoreType.DMA((count,))


def swap(value, axis, mask):
    return lax.ppermute(value, axis, [(place, place ^ mask) for place in range(lax.axis_size(axis))])


def rotate(parts):
    planes = len(parts)
    return [parts[0]] + [
        lax.ppermute(parts[step], "tm", [(place, (place + step) % planes) for place in range(planes)])
        for step in range(1, planes)
    ]


def blocks_of(noise, chunk):
    here, planes = lax.axis_index("tm"), lax.axis_size("tm")
    parts = []
    for step in [*range(1, planes), 0]:
        place = (lax.rem(here + step, planes), chunk, 0, 0)
        part = lax.dynamic_slice(noise, place, (1, 1, *noise.shape[2:]))[0, 0]
        noise, part = lax.optimization_barrier((noise, part))
        parts.append(part)
    return parts[-1:] + parts[:-1]


def plane_factor(factor, planes, groups):
    half = factor.shape[1] // 2
    upper = lax.axis_index("det") >= groups // 2
    mine = lax.dynamic_slice_in_dim(factor[0], jnp.where(upper, half, 0), half, 0)
    plane_of = {band_of(plane, planes): plane for plane in range(planes)}
    pairs = []
    for plane in range(planes):
        for group in range(groups):
            target = plane_of[min(group, groups - 1 - group)]
            pairs.append((plane * groups + group, target * groups + 2 * plane + (group >= groups // 2)))
    return lax.ppermute(mine, ("tm", "det"), pairs)


def band_factor(share, groups):
    rows, columns = share.shape
    share = jnp.stack([share] + [swap(share, "det", mask) for mask in range(2, groups, 2)])
    share = jnp.concatenate([share, swap(share, "det", 1)])
    whole = array(groups * rows, columns, dtype=jnp.bfloat16)
    return call(factor_kernel, [whole, whole], [], 0, share)


def bind(kernel, *static):
    return lambda *refs: kernel(*static, *refs)


def local(noise, factor):
    planes = lax.axis_size("tm")
    groups = lax.axis_size("det")
    rows, span = noise.shape
    n2 = LANES // 2 * planes
    n1 = span * planes // 2 // n2
    pieces = n1 // groups
    chunks = CHUNKS if rows // planes % (8 * CHUNKS) == 0 else 1
    dets = rows // planes // chunks
    flops = 3 * 2 * n1 * dets * (2 * n2) ** 2
    block, series, middle = array(dets, span), (planes, dets, span), (n1 * dets, 2 * n2)
    layout = (planes, groups, chunks, pieces, dets, LANES)
    tables = (twiddles(n1, n2), *fourier_matrix(n2, planes))

    share = plane_factor(factor, planes, groups)
    noise = noise.reshape(planes, chunks, dets, span)
    arrived = []
    for chunk in range(chunks):
        arrived.append(rotate(blocks_of(noise, chunk)))
    tables = call(
        hold_kernel, [array(*table.shape, dtype=table.dtype) for table in tables], [dma(len(tables))], 0, *tables,
        spaces=[pl.ANY] * len(tables),
    )
    share, arrived = lax.optimization_barrier((share, [blocks[::-1] for blocks in arrived]))
    f_high, f_low = band_factor(share, groups)
    buffer = []
    for chunk in range(chunks):
        buffer = call(
            bind(forward_kernel, n1, n2, chunk, planes), [array(*layout)],
            [series, middle, (planes, groups, pieces, dets, LANES), dma(2)], flops,
            *arrived[chunk], *tables, *buffer,
            spaces=[pltpu.VMEM] * (planes + len(tables)) + [pl.ANY] * len(buffer),
            out_space=pl.ANY, aliases={planes + len(tables): 0} if buffer else None,
        )

    def exchange(value):
        value = value.reshape(planes * groups, chunks * pieces * dets, LANES)
        return lax.all_to_all(value, ("tm", "det"), split_axis=0, concat_axis=0, tiled=True).reshape(layout)

    count = f_high.shape[0]
    (mixed,) = call(
        mix_kernel, [array(*layout)], [(count, pieces * LANES)] * 2,
        2 * 3 * count * count * pieces * LANES,
        exchange(buffer[0]), f_high, f_low,
    )
    back = exchange(mixed)
    result = []
    for chunk in range(chunks):
        parts = call(
            bind(inverse_kernel, n1, n2, chunk), [block] * planes, [series, middle], flops, back, *tables
        )
        parts = rotate(parts)
        result = call(
            bind(place_kernel, chunk), [array(planes, chunks, dets, span)], [dma(planes)], 0, *parts[::-1], *result,
            spaces=[pl.ANY] * (planes + len(result)), out_space=pl.ANY, aliases={planes: 0} if result else None,
        )
    return result[0].reshape(rows, span)


def solution(mesh):
    in_specs = (P("det", "tm"), P("det", "tm", None))
    return jax.shard_map(local, mesh=mesh, in_specs=in_specs, out_specs=P("det", "tm"), check_vma=False)
```

```python
import math

import jax
import jax.numpy as jnp
import ml_dtypes
import numpy as np
from jax import lax
from jax.experimental import pallas as pl
from jax.experimental.pallas import tpu as pltpu
from jax.sharding import PartitionSpec as P


LANES = 128
VMEM_LIMIT = 48 * 1024 * 1024
CHUNKS = 1


def band_of(plane, planes):
    return 2 * plane if 2 * plane < planes else 2 * (planes - 1 - plane) + 1


def fourier_matrix(n2, planes):
    share = n2 // (2 * planes)
    order = []
    for plane in range(planes):
        low = band_of(plane, planes) * share + np.arange(share)
        order.append(np.concatenate([low, n2 - 1 - low[::-1]]))
    order = np.stack(order)
    angle = 2.0 * np.pi / n2 * (np.arange(n2)[:, None, None] * order[None] % n2)
    cosine, sine = np.cos(angle), np.sin(angle)
    matrix = np.stack([np.stack([cosine, -sine], 2), np.stack([sine, cosine], 2)])
    matrix = matrix.reshape(2 * n2, 2 * n2).astype(np.float32)
    high = matrix.astype(ml_dtypes.bfloat16)
    low = (matrix - high.astype(np.float32)).astype(ml_dtypes.bfloat16)
    return high, low


def twiddles(n1, n2):
    angle = 2.0 * np.pi / (n1 * n2) * (np.arange(n1)[:, None] + 0.25) * np.arange(n2)[None, :]
    return np.stack([np.cos(angle), np.sin(angle)]).astype(np.float32)


def forward_butterflies(parts, shift):
    count = len(parts)
    if count == 1:
        return parts
    half = count // 2
    turn_re, turn_im = math.cos(math.pi * shift), -math.sin(math.pi * shift)
    even, odd = [], []
    for (a_re, a_im), (b_re, b_im) in zip(parts[:half], parts[half:]):
        c_re = b_re * turn_re - b_im * turn_im
        c_im = b_re * turn_im + b_im * turn_re
        even.append((a_re + c_re, a_im + c_im))
        odd.append((a_re - c_re, a_im - c_im))
    even = forward_butterflies(even, shift / 2)
    odd = forward_butterflies(odd, (1 + shift) / 2)
    return [part for pair in zip(even, odd) for part in pair]


def inverse_butterflies(parts, shift):
    if len(parts) == 1:
        return parts
    turn_re, turn_im = math.cos(math.pi * shift), math.sin(math.pi * shift)
    even = inverse_butterflies(parts[0::2], shift / 2)
    odd = inverse_butterflies(parts[1::2], (1 + shift) / 2)
    first, second = [], []
    for (a_re, a_im), (b_re, b_im) in zip(even, odd):
        d_re, d_im = a_re - b_re, a_im - b_im
        first.append((a_re + b_re, a_im + b_im))
        second.append((d_re * turn_re - d_im * turn_im, d_re * turn_im + d_im * turn_re))
    return first + second


def split(value):
    high = value.astype(jnp.bfloat16)
    return high, (value - high.astype(jnp.float32)).astype(jnp.bfloat16)


def product(left, right, contract=((1,), (0,))):
    def dot(a, b):
        return lax.dot_general(a, b, (contract, ((), ())), preferred_element_type=jnp.float32)

    return dot(left[0], right[0]) + (dot(left[0], right[1]) + dot(left[1], right[0]))


def tiles(rows, lanes):
    step = min(8, rows)
    for row in range(0, rows, step):
        for lane in range(0, lanes, LANES):
            yield slice(row, row + step), lane


def slice_kernel(chunk, noise_ref, *refs):
    here = lax.axis_index("tm")
    outs, sem = refs[:-1], refs[-1]
    copies = [
        pltpu.make_async_copy(noise_ref.at[lax.rem(here + step, len(outs)), chunk], out, sem.at[step])
        for step, out in enumerate(outs)
    ]
    for copy in copies:
        copy.start()
    for copy in copies:
        copy.wait()


def hold_kernel(*refs):
    count = len(refs) // 2
    sem = refs[-1]
    copies = [pltpu.make_async_copy(refs[at], refs[count + at], sem.at[at]) for at in range(count)]
    for copy in copies:
        copy.start()
    for copy in copies:
        copy.wait()


def forward_kernel(n1, n2, chunk, planes, *refs):
    here = lax.axis_index("tm")
    blocks, (turn_ref, high_ref, low_ref) = refs[:planes], refs[planes : planes + 3]
    out_ref, x_ref, mid_ref, stage_ref, sem = refs[-5:]
    _, dets, span = x_ref.shape
    _, groups, pieces, _, width = stage_ref.shape
    per = span // n2
    for step, block in enumerate(blocks):
        x_ref[lax.rem(here + planes - step, planes)] = block[...]
    for rows, lane in tiles(dets, n2):

        def load(index):
            start = (index % per) * n2 + lane
            return x_ref[index // per, rows, start : start + LANES]

        parts = [(load(t1), -load(t1 + n1)) for t1 in range(n1)]
        for k1, (re, im) in enumerate(forward_butterflies(parts, 0.25)):
            cosine = turn_ref[0, k1 : k1 + 1, lane : lane + LANES]
            sine = turn_ref[1, k1 : k1 + 1, lane : lane + LANES]
            place = slice(k1 * dets + rows.start, k1 * dets + rows.stop)
            mid_ref[place, lane : lane + LANES] = re * cosine + im * sine
            mid_ref[place, n2 + lane : n2 + lane + LANES] = im * cosine - re * sine
    copies = []
    share = groups // 2
    for part in range(2):
        count = share * pieces * dets
        spectrum = product(split(mid_ref[part * count : (part + 1) * count]), (high_ref[...], low_ref[...]))
        these = pl.ds(part * share, share)
        for plane in range(planes):
            value = spectrum[:, plane * width : (plane + 1) * width]
            stage_ref[plane, these] = value.reshape(share, pieces, dets, width)
        copies.append(pltpu.make_async_copy(stage_ref.at[:, these], out_ref.at[:, these, chunk], sem.at[part]))
        copies[-1].start()
    for copy in copies:
        copy.wait()


def inverse_kernel(n1, n2, chunk, y_ref, turn_ref, high_ref, low_ref, *refs):
    here = lax.axis_index("tm")
    outs, (x_ref, mid_ref) = refs[:-2], refs[-2:]
    _, dets, span = x_ref.shape
    planes, _, _, _, _, width = y_ref.shape
    per = span // n2
    scale = 1.0 / (n1 * n2)
    bins = jnp.concatenate([y_ref[plane, :, chunk].reshape(n1 * dets, width) for plane in range(planes)], axis=1)
    mid_ref[...] = product(split(bins), (high_ref[...], low_ref[...]), ((1,), (1,)))
    for rows, lane in tiles(dets, n2):
        parts = []
        for k1 in range(n1):
            cosine = turn_ref[0, k1 : k1 + 1, lane : lane + LANES] * scale
            sine = turn_ref[1, k1 : k1 + 1, lane : lane + LANES] * scale
            place = slice(k1 * dets + rows.start, k1 * dets + rows.stop)
            re = mid_ref[place, lane : lane + LANES]
            im = mid_ref[place, n2 + lane : n2 + lane + LANES]
            parts.append((re * cosine - im * sine, im * cosine + re * sine))
        for t1, (re, im) in enumerate(inverse_butterflies(parts, 0.25)):
            for index, value in ((t1, re), (t1 + n1, -im)):
                start = (index % per) * n2 + lane
                x_ref[index // per, rows, start : start + LANES] = value
    for step, out in enumerate(outs):
        out[...] = x_ref[lax.rem(here + step, planes)]


def place_kernel(chunk, *refs):
    here = lax.axis_index("tm")
    out_ref, sem = refs[-2:]
    planes = out_ref.shape[0]
    copies = [
        pltpu.make_async_copy(refs[step], out_ref.at[lax.rem(here + planes - step, planes), chunk], sem.at[step])
        for step in range(planes)
    ]
    for copy in copies:
        copy.start()
    for copy in copies:
        copy.wait()


def factor_kernel(factor_ref, high_ref, low_ref):
    here = lax.axis_index("det")
    shares, rows, _ = factor_ref.shape
    for share in range(shares):
        source = here ^ (2 * share if 2 * share < shares else 2 * share - shares + 1)
        place = pl.ds(pl.multiple_of(source * rows, rows), rows)
        high_ref[place], low_ref[place] = split(factor_ref[share])


def mix_kernel(x_ref, f_high, f_low, out_ref, x_mid, y_mid):
    planes, groups, chunks, pieces, dets, width = x_ref.shape
    places = []
    for plane, group, chunk, piece in np.ndindex(planes, groups, chunks, pieces):
        start = ((group * planes + plane) * chunks + chunk) * dets
        rows, lanes = slice(start, start + dets), slice(piece * width, (piece + 1) * width)
        places.append(((plane, group, chunk, piece), (rows, lanes)))
    for source, target in places:
        x_mid[target] = x_ref[source]
    x_high, x_low = split(x_mid[...])
    half = f_high.shape[0] // 2
    y_mid[:half] = product((f_high[:half, :half], f_low[:half, :half]), (x_high[:half], x_low[:half]))
    y_mid[half:] = product((f_high[half:, :], f_low[half:, :]), (x_high, x_low))
    for target, source in places:
        out_ref[target] = y_mid[source]


def call(kernel, outs, scratch, flops, *args, spaces=None, out_space=pltpu.VMEM, aliases=None):
    spaces = spaces or [pltpu.VMEM] * len(args)
    count = sum(math.prod(arg.shape) * arg.dtype.itemsize for arg in (*args, *outs))
    return pl.pallas_call(
        kernel,
        out_shape=outs,
        in_specs=[pl.BlockSpec(memory_space=space) for space in spaces],
        out_specs=[pl.BlockSpec(memory_space=out_space)] * len(outs),
        scratch_shapes=[pltpu.VMEM(item, jnp.float32) if isinstance(item, tuple) else item for item in scratch],
        compiler_params=pltpu.CompilerParams(vmem_limit_bytes=VMEM_LIMIT),
        cost_estimate=pl.CostEstimate(flops=flops, bytes_accessed=count, transcendentals=0),
        input_output_aliases=aliases or {},
    )(*args)


def array(*shape, dtype=jnp.float32):
    return jax.ShapeDtypeStruct(shape, dtype)


def dma(count):
    return pltpu.SemaphoreType.DMA((count,))


def swap(value, axis, mask):
    return lax.ppermute(value, axis, [(place, place ^ mask) for place in range(lax.axis_size(axis))])


def far_first(planes):
    return sorted(range(1, planes), key=lambda step: abs(2 * step - planes))


def rotate(part, step):
    planes = lax.axis_size("tm")
    return lax.ppermute(part, "tm", [(place, (place + step) % planes) for place in range(planes)])


def plane_factor(factor, planes, groups):
    half = factor.shape[1] // 2
    upper = lax.axis_index("det") >= groups // 2
    mine = lax.dynamic_slice_in_dim(factor[0], jnp.where(upper, half, 0), half, 0)
    plane_of = {band_of(plane, planes): plane for plane in range(planes)}
    pairs = []
    for plane in range(planes):
        for group in range(groups):
            target = plane_of[min(group, groups - 1 - group)]
            pairs.append((plane * groups + group, target * groups + 2 * plane + (group >= groups // 2)))
    return lax.ppermute(mine, ("tm", "det"), pairs)


def band_factor(share, groups):
    rows, columns = share.shape
    share = jnp.stack([share] + [swap(share, "det", mask) for mask in range(2, groups, 2)])
    share = jnp.concatenate([share, swap(share, "det", 1)])
    whole = array(groups * rows, columns, dtype=jnp.bfloat16)
    return call(factor_kernel, [whole, whole], [], 0, share)


def bind(kernel, *static):
    return lambda *refs: kernel(*static, *refs)


def local(noise, factor):
    planes = lax.axis_size("tm")
    groups = lax.axis_size("det")
    rows, span = noise.shape
    n2 = LANES // 2 * planes
    n1 = span * planes // 2 // n2
    pieces = n1 // groups
    chunks = CHUNKS if rows // planes % (8 * CHUNKS) == 0 else 1
    dets = rows // planes // chunks
    flops = 3 * 2 * n1 * dets * (2 * n2) ** 2
    block, series, middle = array(dets, span), (planes, dets, span), (n1 * dets, 2 * n2)
    layout = (planes, groups, chunks, pieces, dets, LANES)
    tables = (twiddles(n1, n2), *fourier_matrix(n2, planes))

    noise = noise.reshape(planes, chunks, dets, span)
    arrived = []
    for chunk in range(chunks):
        parts = call(bind(slice_kernel, chunk), [block] * planes, [dma(planes)], 0, noise, spaces=[pl.ANY])
        parts = list(parts)
        for at, step in enumerate(far_first(planes)):
            parts[step] = rotate(parts[step], step)
            if chunk == 0 and at == 0:
                share = plane_factor(factor, planes, groups)
        arrived.append(parts)
    tables = call(
        hold_kernel, [array(*table.shape, dtype=table.dtype) for table in tables], [dma(len(tables))], 0, *tables,
        spaces=[pl.ANY] * len(tables),
    )
    share, arrived = lax.optimization_barrier((share, arrived))
    f_high, f_low = band_factor(share, groups)
    buffer = []
    for chunk in range(chunks):
        buffer = call(
            bind(forward_kernel, n1, n2, chunk, planes), [array(*layout)],
            [series, middle, (planes, groups, pieces, dets, LANES), dma(2)], flops,
            *arrived[chunk], *tables, *buffer,
            spaces=[pltpu.VMEM] * (planes + len(tables)) + [pl.ANY] * len(buffer),
            out_space=pl.ANY, aliases={planes + len(tables): 0} if buffer else None,
        )

    def exchange(value):
        value = value.reshape(planes * groups, chunks * pieces * dets, LANES)
        return lax.all_to_all(value, ("tm", "det"), split_axis=0, concat_axis=0, tiled=True).reshape(layout)

    count = f_high.shape[0]
    (mixed,) = call(
        mix_kernel, [array(*layout)], [(count, pieces * LANES)] * 2,
        2 * 3 * count * count * pieces * LANES,
        exchange(buffer[0]), f_high, f_low,
    )
    back = exchange(mixed)
    result = []
    for chunk in range(chunks):
        parts = call(
            bind(inverse_kernel, n1, n2, chunk), [block] * planes, [series, middle], flops, back, *tables
        )
        parts = list(parts)
        for step in far_first(planes):
            parts[step] = rotate(parts[step], step)
        result = call(
            bind(place_kernel, chunk), [array(planes, chunks, dets, span)], [dma(planes)], 0, *parts, *result,
            spaces=[pl.ANY] * (planes + len(result)), out_space=pl.ANY, aliases={planes: 0} if result else None,
        )
    return result[0].reshape(rows, span)


def solution(mesh):
    in_specs = (P("det", "tm"), P("det", "tm", None))
    return jax.shard_map(local, mesh=mesh, in_specs=in_specs, out_specs=P("det", "tm"), check_vma=False)
```

```python
import math

import jax
import jax.numpy as jnp
import ml_dtypes
import numpy as np
from jax import lax
from jax.experimental import pallas as pl
from jax.experimental.pallas import tpu as pltpu
from jax.sharding import PartitionSpec as P


LANES = 128
VMEM_LIMIT = 48 * 1024 * 1024
CHUNKS = 2


def band_of(plane, planes):
    return 2 * plane if 2 * plane < planes else 2 * (planes - 1 - plane) + 1


def fourier_matrix(n2, planes):
    share = n2 // (2 * planes)
    order = []
    for plane in range(planes):
        low = band_of(plane, planes) * share + np.arange(share)
        order.append(np.concatenate([low, n2 - 1 - low[::-1]]))
    order = np.stack(order)
    angle = 2.0 * np.pi / n2 * (np.arange(n2)[:, None, None] * order[None] % n2)
    cosine, sine = np.cos(angle), np.sin(angle)
    matrix = np.stack([np.stack([cosine, -sine], 2), np.stack([sine, cosine], 2)])
    matrix = matrix.reshape(2 * n2, 2 * n2).astype(np.float32)
    high = matrix.astype(ml_dtypes.bfloat16)
    low = (matrix - high.astype(np.float32)).astype(ml_dtypes.bfloat16)
    return high, low


def twiddles(n1, n2):
    angle = 2.0 * np.pi / (n1 * n2) * (np.arange(n1)[:, None] + 0.25) * np.arange(n2)[None, :]
    return np.stack([np.cos(angle), np.sin(angle)]).astype(np.float32)


def forward_butterflies(parts, shift):
    count = len(parts)
    if count == 1:
        return parts
    half = count // 2
    turn_re, turn_im = math.cos(math.pi * shift), -math.sin(math.pi * shift)
    even, odd = [], []
    for (a_re, a_im), (b_re, b_im) in zip(parts[:half], parts[half:]):
        c_re = b_re * turn_re - b_im * turn_im
        c_im = b_re * turn_im + b_im * turn_re
        even.append((a_re + c_re, a_im + c_im))
        odd.append((a_re - c_re, a_im - c_im))
    even = forward_butterflies(even, shift / 2)
    odd = forward_butterflies(odd, (1 + shift) / 2)
    return [part for pair in zip(even, odd) for part in pair]


def inverse_butterflies(parts, shift):
    if len(parts) == 1:
        return parts
    turn_re, turn_im = math.cos(math.pi * shift), math.sin(math.pi * shift)
    even = inverse_butterflies(parts[0::2], shift / 2)
    odd = inverse_butterflies(parts[1::2], (1 + shift) / 2)
    first, second = [], []
    for (a_re, a_im), (b_re, b_im) in zip(even, odd):
        d_re, d_im = a_re - b_re, a_im - b_im
        first.append((a_re + b_re, a_im + b_im))
        second.append((d_re * turn_re - d_im * turn_im, d_re * turn_im + d_im * turn_re))
    return first + second


def split(value):
    high = value.astype(jnp.bfloat16)
    return high, (value - high.astype(jnp.float32)).astype(jnp.bfloat16)


def product(left, right, contract=((1,), (0,))):
    def dot(a, b):
        return lax.dot_general(a, b, (contract, ((), ())), preferred_element_type=jnp.float32)

    return dot(left[0], right[0]) + (dot(left[0], right[1]) + dot(left[1], right[0]))


def tiles(rows, lanes):
    step = min(8, rows)
    for row in range(0, rows, step):
        for lane in range(0, lanes, LANES):
            yield slice(row, row + step), lane


def slice_kernel(chunk, noise_ref, *refs):
    here = lax.axis_index("tm")
    outs, sem = refs[:-1], refs[-1]
    copies = [
        pltpu.make_async_copy(noise_ref.at[lax.rem(here + step, len(outs)), chunk], out, sem.at[step])
        for step, out in enumerate(outs)
    ]
    for copy in copies:
        copy.start()
    for copy in copies:
        copy.wait()


def hold_kernel(*refs):
    count = len(refs) // 2
    sem = refs[-1]
    copies = [pltpu.make_async_copy(refs[at], refs[count + at], sem.at[at]) for at in range(count)]
    for copy in copies:
        copy.start()
    for copy in copies:
        copy.wait()


def forward_kernel(n1, n2, chunk, planes, *refs):
    here = lax.axis_index("tm")
    blocks, (turn_ref, high_ref, low_ref) = refs[:planes], refs[planes : planes + 3]
    out_ref, x_ref, mid_ref, stage_ref, sem = refs[-5:]
    _, dets, span = x_ref.shape
    _, groups, pieces, _, width = stage_ref.shape
    per = span // n2
    for step, block in zip([*far_first(planes), 0], blocks):
        x_ref[lax.rem(here + planes - step, planes)] = block[...]
    for rows, lane in tiles(dets, n2):

        def load(index):
            start = (index % per) * n2 + lane
            return x_ref[index // per, rows, start : start + LANES]

        parts = [(load(t1), -load(t1 + n1)) for t1 in range(n1)]
        for k1, (re, im) in enumerate(forward_butterflies(parts, 0.25)):
            cosine = turn_ref[0, k1 : k1 + 1, lane : lane + LANES]
            sine = turn_ref[1, k1 : k1 + 1, lane : lane + LANES]
            place = slice(k1 * dets + rows.start, k1 * dets + rows.stop)
            mid_ref[place, lane : lane + LANES] = re * cosine + im * sine
            mid_ref[place, n2 + lane : n2 + lane + LANES] = im * cosine - re * sine
    copies = []
    share = groups // 2
    for part in range(2):
        count = share * pieces * dets
        spectrum = product(split(mid_ref[part * count : (part + 1) * count]), (high_ref[...], low_ref[...]))
        these = pl.ds(part * share, share)
        for plane in range(planes):
            value = spectrum[:, plane * width : (plane + 1) * width]
            stage_ref[plane, these] = value.reshape(share, pieces, dets, width)
        copies.append(pltpu.make_async_copy(stage_ref.at[:, these], out_ref.at[:, these, chunk], sem.at[part]))
        copies[-1].start()
    for copy in copies:
        copy.wait()


def inverse_kernel(n1, n2, chunk, y_ref, turn_ref, high_ref, low_ref, *refs):
    here = lax.axis_index("tm")
    outs, (x_ref, mid_ref) = refs[:-2], refs[-2:]
    _, dets, span = x_ref.shape
    planes, _, _, _, _, width = y_ref.shape
    per = span // n2
    scale = 1.0 / (n1 * n2)
    bins = jnp.concatenate([y_ref[plane, :, chunk].reshape(n1 * dets, width) for plane in range(planes)], axis=1)
    mid_ref[...] = product(split(bins), (high_ref[...], low_ref[...]), ((1,), (1,)))
    for rows, lane in tiles(dets, n2):
        parts = []
        for k1 in range(n1):
            cosine = turn_ref[0, k1 : k1 + 1, lane : lane + LANES] * scale
            sine = turn_ref[1, k1 : k1 + 1, lane : lane + LANES] * scale
            place = slice(k1 * dets + rows.start, k1 * dets + rows.stop)
            re = mid_ref[place, lane : lane + LANES]
            im = mid_ref[place, n2 + lane : n2 + lane + LANES]
            parts.append((re * cosine - im * sine, im * cosine + re * sine))
        for t1, (re, im) in enumerate(inverse_butterflies(parts, 0.25)):
            for index, value in ((t1, re), (t1 + n1, -im)):
                start = (index % per) * n2 + lane
                x_ref[index // per, rows, start : start + LANES] = value
    for step, out in enumerate(outs):
        out[...] = x_ref[lax.rem(here + step, planes)]


def place_kernel(chunk, *refs):
    here = lax.axis_index("tm")
    out_ref, sem = refs[-2:]
    planes = out_ref.shape[0]
    copies = [
        pltpu.make_async_copy(block, out_ref.at[lax.rem(here + planes - step, planes), chunk], sem.at[step])
        for step, block in zip([*far_first(planes), 0], refs)
    ]
    for copy in copies:
        copy.start()
    for copy in copies:
        copy.wait()


def factor_kernel(factor_ref, high_ref, low_ref):
    here = lax.axis_index("det")
    shares, rows, _ = factor_ref.shape
    for share in range(shares):
        source = here ^ (2 * share if 2 * share < shares else 2 * share - shares + 1)
        place = pl.ds(pl.multiple_of(source * rows, rows), rows)
        high_ref[place], low_ref[place] = split(factor_ref[share])


def mix_kernel(x_ref, f_high, f_low, out_ref, x_mid, y_mid):
    planes, groups, chunks, pieces, dets, width = x_ref.shape
    places = []
    for plane, group, chunk, piece in np.ndindex(planes, groups, chunks, pieces):
        start = ((group * planes + plane) * chunks + chunk) * dets
        rows, lanes = slice(start, start + dets), slice(piece * width, (piece + 1) * width)
        places.append(((plane, group, chunk, piece), (rows, lanes)))
    for source, target in places:
        x_mid[target] = x_ref[source]
    x_high, x_low = split(x_mid[...])
    half = f_high.shape[0] // 2
    y_mid[:half] = product((f_high[:half, :half], f_low[:half, :half]), (x_high[:half], x_low[:half]))
    y_mid[half:] = product((f_high[half:, :], f_low[half:, :]), (x_high, x_low))
    for target, source in places:
        out_ref[target] = y_mid[source]


def call(kernel, outs, scratch, flops, *args, spaces=None, out_space=pltpu.VMEM, aliases=None):
    spaces = spaces or [pltpu.VMEM] * len(args)
    count = sum(math.prod(arg.shape) * arg.dtype.itemsize for arg in (*args, *outs))
    return pl.pallas_call(
        kernel,
        out_shape=outs,
        in_specs=[pl.BlockSpec(memory_space=space) for space in spaces],
        out_specs=[pl.BlockSpec(memory_space=out_space)] * len(outs),
        scratch_shapes=[pltpu.VMEM(item, jnp.float32) if isinstance(item, tuple) else item for item in scratch],
        compiler_params=pltpu.CompilerParams(vmem_limit_bytes=VMEM_LIMIT),
        cost_estimate=pl.CostEstimate(flops=flops, bytes_accessed=count, transcendentals=0),
        input_output_aliases=aliases or {},
    )(*args)


def array(*shape, dtype=jnp.float32):
    return jax.ShapeDtypeStruct(shape, dtype)


def dma(count):
    return pltpu.SemaphoreType.DMA((count,))


def swap(value, axis, mask):
    return lax.ppermute(value, axis, [(place, place ^ mask) for place in range(lax.axis_size(axis))])


def far_first(planes):
    return sorted(range(1, planes), key=lambda step: abs(2 * step - planes))


def rotate(parts):
    planes = len(parts)
    return [
        lax.ppermute(parts[step], "tm", [(place, (place + step) % planes) for place in range(planes)])
        for step in far_first(planes)
    ] + [parts[0]]


def plane_factor(factor, planes, groups):
    half = factor.shape[1] // 2
    upper = lax.axis_index("det") >= groups // 2
    mine = lax.dynamic_slice_in_dim(factor[0], jnp.where(upper, half, 0), half, 0)
    plane_of = {band_of(plane, planes): plane for plane in range(planes)}
    pairs = []
    for plane in range(planes):
        for group in range(groups):
            target = plane_of[min(group, groups - 1 - group)]
            pairs.append((plane * groups + group, target * groups + 2 * plane + (group >= groups // 2)))
    return lax.ppermute(mine, ("tm", "det"), pairs)


def band_factor(share, groups):
    rows, columns = share.shape
    share = jnp.stack([share] + [swap(share, "det", mask) for mask in range(2, groups, 2)])
    share = jnp.concatenate([share, swap(share, "det", 1)])
    whole = array(groups * rows, columns, dtype=jnp.bfloat16)
    return call(factor_kernel, [whole, whole], [], 0, share)


def bind(kernel, *static):
    return lambda *refs: kernel(*static, *refs)


def local(noise, factor):
    planes = lax.axis_size("tm")
    groups = lax.axis_size("det")
    rows, span = noise.shape
    n2 = LANES // 2 * planes
    n1 = span * planes // 2 // n2
    pieces = n1 // groups
    chunks = CHUNKS if rows // planes % (8 * CHUNKS) == 0 else 1
    dets = rows // planes // chunks
    flops = 3 * 2 * n1 * dets * (2 * n2) ** 2
    block, series, middle = array(dets, span), (planes, dets, span), (n1 * dets, 2 * n2)
    layout = (planes, groups, chunks, pieces, dets, LANES)
    tables = (twiddles(n1, n2), *fourier_matrix(n2, planes))

    noise = noise.reshape(planes, chunks, dets, span)
    arrived = []
    for chunk in range(chunks):
        parts = call(bind(slice_kernel, chunk), [block] * planes, [dma(planes)], 0, noise, spaces=[pl.ANY])
        arrived.append(rotate(parts))
    tables = call(
        hold_kernel, [array(*table.shape, dtype=table.dtype) for table in tables], [dma(len(tables))], 0, *tables,
        spaces=[pl.ANY] * len(tables),
    )
    arrived[-1], share = lax.optimization_barrier((arrived[-1], plane_factor(factor, planes, groups)))
    f_high, f_low = band_factor(share, groups)
    buffer = []
    for chunk in range(chunks):
        buffer = call(
            bind(forward_kernel, n1, n2, chunk, planes), [array(*layout)],
            [series, middle, (planes, groups, pieces, dets, LANES), dma(2)], flops,
            *arrived[chunk], *tables, *buffer,
            spaces=[pltpu.VMEM] * (planes + len(tables)) + [pl.ANY] * len(buffer),
            out_space=pl.ANY, aliases={planes + len(tables): 0} if buffer else None,
        )

    def exchange(value):
        value = value.reshape(planes * groups, chunks * pieces * dets, LANES)
        return lax.all_to_all(value, ("tm", "det"), split_axis=0, concat_axis=0, tiled=True).reshape(layout)

    count = f_high.shape[0]
    (mixed,) = call(
        mix_kernel, [array(*layout)], [(count, pieces * LANES)] * 2,
        2 * 3 * count * count * pieces * LANES,
        exchange(buffer[0]), f_high, f_low,
    )
    back = exchange(mixed)
    result = []
    for chunk in range(chunks):
        parts = call(
            bind(inverse_kernel, n1, n2, chunk), [block] * planes, [series, middle], flops, back, *tables
        )
        parts = rotate(parts)
        result = call(
            bind(place_kernel, chunk), [array(planes, chunks, dets, span)], [dma(planes)], 0, *parts, *result,
            spaces=[pl.ANY] * (planes + len(result)), out_space=pl.ANY, aliases={planes: 0} if result else None,
        )
    return result[0].reshape(rows, span)


def solution(mesh):
    in_specs = (P("det", "tm"), P("det", "tm", None))
    return jax.shard_map(local, mesh=mesh, in_specs=in_specs, out_specs=P("det", "tm"), check_vma=False)
```

```python
import math

import jax
import jax.numpy as jnp
import ml_dtypes
import numpy as np
from jax import lax
from jax.experimental import pallas as pl
from jax.experimental.pallas import tpu as pltpu
from jax.sharding import PartitionSpec as P


LANES = 128
VMEM_LIMIT = 48 * 1024 * 1024
VMEM_ALL = 63 * 1024 * 1024
CHUNKS = 2


def band_of(plane, planes):
    return 2 * plane if 2 * plane < planes else 2 * (planes - 1 - plane) + 1


def fourier_matrix(n2, planes):
    share = n2 // (2 * planes)
    order = []
    for plane in range(planes):
        low = band_of(plane, planes) * share + np.arange(share)
        order.append(np.concatenate([low, n2 - 1 - low[::-1]]))
    order = np.stack(order)
    angle = 2.0 * np.pi / n2 * (np.arange(n2)[:, None, None] * order[None] % n2)
    cosine, sine = np.cos(angle), np.sin(angle)
    matrix = np.stack([np.stack([cosine, -sine], 2), np.stack([sine, cosine], 2)])
    matrix = matrix.reshape(2 * n2, 2 * n2).astype(np.float32)
    high = matrix.astype(ml_dtypes.bfloat16)
    low = (matrix - high.astype(np.float32)).astype(ml_dtypes.bfloat16)
    return high, low


def twiddles(n1, n2):
    angle = 2.0 * np.pi / (n1 * n2) * (np.arange(n1)[:, None] + 0.25) * np.arange(n2)[None, :]
    return np.stack([np.cos(angle), np.sin(angle)]).astype(np.float32)


def forward_butterflies(parts, shift):
    count = len(parts)
    if count == 1:
        return parts
    half = count // 2
    turn_re, turn_im = math.cos(math.pi * shift), -math.sin(math.pi * shift)
    even, odd = [], []
    for (a_re, a_im), (b_re, b_im) in zip(parts[:half], parts[half:]):
        c_re = b_re * turn_re - b_im * turn_im
        c_im = b_re * turn_im + b_im * turn_re
        even.append((a_re + c_re, a_im + c_im))
        odd.append((a_re - c_re, a_im - c_im))
    even = forward_butterflies(even, shift / 2)
    odd = forward_butterflies(odd, (1 + shift) / 2)
    return [part for pair in zip(even, odd) for part in pair]


def inverse_butterflies(parts, shift):
    if len(parts) == 1:
        return parts
    turn_re, turn_im = math.cos(math.pi * shift), math.sin(math.pi * shift)
    even = inverse_butterflies(parts[0::2], shift / 2)
    odd = inverse_butterflies(parts[1::2], (1 + shift) / 2)
    first, second = [], []
    for (a_re, a_im), (b_re, b_im) in zip(even, odd):
        d_re, d_im = a_re - b_re, a_im - b_im
        first.append((a_re + b_re, a_im + b_im))
        second.append((d_re * turn_re - d_im * turn_im, d_re * turn_im + d_im * turn_re))
    return first + second


def split(value):
    high = value.astype(jnp.bfloat16)
    return high, (value - high.astype(jnp.float32)).astype(jnp.bfloat16)


def product(left, right, contract=((1,), (0,))):
    def dot(a, b):
        return lax.dot_general(a, b, (contract, ((), ())), preferred_element_type=jnp.float32)

    rows = left[0].shape[0]
    both = dot(jnp.concatenate(left), right[0])
    return both[:rows] + (both[rows:] + dot(left[0], right[1]))


def tiles(rows, lanes):
    step = min(8, rows)
    for row in range(0, rows, step):
        for lane in range(0, lanes, LANES):
            yield slice(row, row + step), lane


def slice_kernel(chunk, noise_ref, *refs):
    here = lax.axis_index("tm")
    outs, sem = refs[:-1], refs[-1]
    copies = [
        pltpu.make_async_copy(noise_ref.at[lax.rem(here + step, len(outs)), chunk], out, sem.at[step])
        for step, out in enumerate(outs)
    ]
    for copy in copies:
        copy.start()
    for copy in copies:
        copy.wait()


def hold_kernel(*refs):
    count = len(refs) // 2
    sem = refs[-1]
    copies = [pltpu.make_async_copy(refs[at], refs[count + at], sem.at[at]) for at in range(count)]
    for copy in copies:
        copy.start()
    for copy in copies:
        copy.wait()


def forward_kernel(n1, n2, chunk, planes, *refs):
    here = lax.axis_index("tm")
    blocks, (turn_ref, high_ref, low_ref) = refs[:planes], refs[planes : planes + 3]
    out_ref, x_ref, mid_ref, stage_ref, sem = refs[-5:]
    _, dets, span = x_ref.shape
    _, groups, pieces, _, width = stage_ref.shape
    per = span // n2
    for step, block in zip([*far_first(planes), 0], blocks):
        x_ref[lax.rem(here + planes - step, planes)] = block[...]
    for rows, lane in tiles(dets, n2):

        def load(index):
            start = (index % per) * n2 + lane
            return x_ref[index // per, rows, start : start + LANES]

        parts = [(load(t1), -load(t1 + n1)) for t1 in range(n1)]
        for k1, (re, im) in enumerate(forward_butterflies(parts, 0.25)):
            cosine = turn_ref[0, k1 : k1 + 1, lane : lane + LANES]
            sine = turn_ref[1, k1 : k1 + 1, lane : lane + LANES]
            place = slice(k1 * dets + rows.start, k1 * dets + rows.stop)
            mid_ref[place, lane : lane + LANES] = re * cosine + im * sine
            mid_ref[place, n2 + lane : n2 + lane + LANES] = im * cosine - re * sine
    halves = split(mid_ref[...])
    copies = []
    share = planes // 2
    for part in range(2):
        columns = slice(part * share * width, (part + 1) * share * width)
        spectrum = product(halves, (high_ref[:, columns], low_ref[:, columns]))
        these = pl.ds(part * share, share)
        for plane in range(share):
            value = spectrum[:, plane * width : (plane + 1) * width]
            stage_ref[part * share + plane] = value.reshape(groups, pieces, dets, width)
        copies.append(pltpu.make_async_copy(stage_ref.at[these], out_ref.at[these, :, chunk], sem.at[part]))
        copies[-1].start()
    for copy in copies:
        copy.wait()


def inverse_kernel(n1, n2, chunk, y_ref, turn_ref, high_ref, low_ref, *refs):
    here = lax.axis_index("tm")
    outs, (x_ref, mid_ref) = refs[:-2], refs[-2:]
    _, dets, span = x_ref.shape
    planes, _, _, _, _, width = y_ref.shape
    per = span // n2
    scale = 1.0 / (n1 * n2)
    bins = jnp.concatenate([y_ref[plane, :, chunk].reshape(n1 * dets, width) for plane in range(planes)], axis=1)
    mid_ref[...] = product(split(bins), (high_ref[...], low_ref[...]), ((1,), (1,)))
    for rows, lane in tiles(dets, n2):
        parts = []
        for k1 in range(n1):
            cosine = turn_ref[0, k1 : k1 + 1, lane : lane + LANES] * scale
            sine = turn_ref[1, k1 : k1 + 1, lane : lane + LANES] * scale
            place = slice(k1 * dets + rows.start, k1 * dets + rows.stop)
            re = mid_ref[place, lane : lane + LANES]
            im = mid_ref[place, n2 + lane : n2 + lane + LANES]
            parts.append((re * cosine - im * sine, im * cosine + re * sine))
        for t1, (re, im) in enumerate(inverse_butterflies(parts, 0.25)):
            for index, value in ((t1, re), (t1 + n1, -im)):
                start = (index % per) * n2 + lane
                x_ref[index // per, rows, start : start + LANES] = value
    for step, out in enumerate(outs):
        out[...] = x_ref[lax.rem(here + step, planes)]


def place_kernel(chunk, steps, *refs):
    here = lax.axis_index("tm")
    out_ref, sem = refs[-2:]
    planes = out_ref.shape[0]
    copies = [
        pltpu.make_async_copy(block, out_ref.at[lax.rem(here + planes - step, planes), chunk], sem.at[at])
        for at, (step, block) in enumerate(zip(steps, refs))
    ]
    for copy in copies:
        copy.start()
    for copy in copies:
        copy.wait()


def factor_kernel(factor_ref, high_ref, low_ref):
    here = lax.axis_index("det")
    shares, rows, _ = factor_ref.shape
    for share in range(shares):
        source = here ^ (2 * share if 2 * share < shares else 2 * share - shares + 1)
        place = pl.ds(pl.multiple_of(source * rows, rows), rows)
        high_ref[place], low_ref[place] = split(factor_ref[share])


def mix_kernel(x_ref, f_high, f_low, out_ref, x_mid, y_mid, stage_ref, sem):
    planes, groups, chunks, pieces, dets, width = x_ref.shape
    places = []
    for plane, group, chunk, piece in np.ndindex(planes, groups, chunks, pieces):
        start = ((group * planes + plane) * chunks + chunk) * dets
        rows, lanes = slice(start, start + dets), slice(piece * width, (piece + 1) * width)
        places.append(((plane, group, chunk, piece), (rows, lanes)))
    for source, target in places:
        x_mid[target] = x_ref[source]
    x_high, x_low = split(x_mid[...])
    half, share = f_high.shape[0] // 2, groups // 2
    copies = []
    for part in range(2):
        rows, reach = slice(part * half, (part + 1) * half), (part + 1) * half
        y_mid[rows] = product((f_high[rows, :reach], f_low[rows, :reach]), (x_high[:reach], x_low[:reach]))
        for target, source in places:
            if target[1] // share == part:
                stage_ref[target] = y_mid[source]
        these = pl.ds(part * share, share)
        copies.append(pltpu.make_async_copy(stage_ref.at[:, these], out_ref.at[:, these], sem.at[part]))
        copies[-1].start()
    for copy in copies:
        copy.wait()


def call(kernel, outs, scratch, flops, *args, spaces=None, out_space=pltpu.VMEM, aliases=None, limit=VMEM_LIMIT):
    spaces = spaces or [pltpu.VMEM] * len(args)
    count = sum(math.prod(arg.shape) * arg.dtype.itemsize for arg in (*args, *outs))
    return pl.pallas_call(
        kernel,
        out_shape=outs,
        in_specs=[pl.BlockSpec(memory_space=space) for space in spaces],
        out_specs=[pl.BlockSpec(memory_space=out_space)] * len(outs),
        scratch_shapes=[pltpu.VMEM(item, jnp.float32) if isinstance(item, tuple) else item for item in scratch],
        compiler_params=pltpu.CompilerParams(vmem_limit_bytes=limit),
        cost_estimate=pl.CostEstimate(flops=flops, bytes_accessed=count, transcendentals=0),
        input_output_aliases=aliases or {},
    )(*args)


def array(*shape, dtype=jnp.float32):
    return jax.ShapeDtypeStruct(shape, dtype)


def dma(count):
    return pltpu.SemaphoreType.DMA((count,))


def swap(value, axis, mask):
    return lax.ppermute(value, axis, [(place, place ^ mask) for place in range(lax.axis_size(axis))])


def far_first(planes):
    return sorted(range(1, planes), key=lambda step: abs(2 * step - planes))


def rotate(parts):
    planes = len(parts)
    return [
        lax.ppermute(parts[step], "tm", [(place, (place + step) % planes) for place in range(planes)])
        for step in far_first(planes)
    ] + [parts[0]]


def plane_factor(factor, planes, groups):
    half = factor.shape[1] // 2
    upper = lax.axis_index("det") >= groups // 2
    mine = lax.dynamic_slice_in_dim(factor[0], jnp.where(upper, half, 0), half, 0)
    plane_of = {band_of(plane, planes): plane for plane in range(planes)}
    pairs = []
    for plane in range(planes):
        for group in range(groups):
            target = plane_of[min(group, groups - 1 - group)]
            pairs.append((plane * groups + group, target * groups + 2 * plane + (group >= groups // 2)))
    return lax.ppermute(mine, ("tm", "det"), pairs)


def band_factor(share, groups):
    rows, columns = share.shape
    share = jnp.stack([share] + [swap(share, "det", mask) for mask in range(2, groups, 2)])
    share = jnp.concatenate([share, swap(share, "det", 1)])
    whole = array(groups * rows, columns, dtype=jnp.bfloat16)
    return call(factor_kernel, [whole, whole], [], 0, share)


def hold(tables):
    outs = [array(*table.shape, dtype=table.dtype) for table in tables]
    return call(hold_kernel, outs, [dma(len(tables))], 0, *tables, spaces=[pl.ANY] * len(tables))


def bind(kernel, *static):
    return lambda *refs: kernel(*static, *refs)


def local(noise, factor):
    planes = lax.axis_size("tm")
    groups = lax.axis_size("det")
    rows, span = noise.shape
    n2 = LANES // 2 * planes
    n1 = span * planes // 2 // n2
    pieces = n1 // groups
    chunks = CHUNKS if rows // planes % (8 * CHUNKS) == 0 else 1
    dets = rows // planes // chunks
    flops = 3 * 2 * n1 * dets * (2 * n2) ** 2
    block, series, middle = array(dets, span), (planes, dets, span), (n1 * dets, 2 * n2)
    layout = (planes, groups, chunks, pieces, dets, LANES)
    tables = (twiddles(n1, n2), *fourier_matrix(n2, planes))

    noise = noise.reshape(planes, chunks, dets, span)
    arrived = []
    for chunk in range(chunks):
        parts = call(
            bind(slice_kernel, chunk), [block] * planes, [dma(planes)], 0, noise, spaces=[pl.ANY], out_space=pl.ANY,
            limit=VMEM_ALL,
        )
        arrived.append(rotate(parts))
    tables = hold(tables)
    arrived[0][0], factor = lax.optimization_barrier((arrived[0][0], factor))
    arrived[-1], share = lax.optimization_barrier((arrived[-1], plane_factor(factor, planes, groups)))
    f_high, f_low = band_factor(share, groups)
    buffer = []
    for chunk in range(chunks):
        buffer = call(
            bind(forward_kernel, n1, n2, chunk, planes), [array(*layout)],
            [series, middle, (planes, groups, pieces, dets, LANES), dma(2)], flops,
            *arrived[chunk], *tables, *buffer,
            spaces=[pltpu.VMEM] * (planes + len(tables)) + [pl.ANY] * len(buffer),
            out_space=pl.ANY, aliases={planes + len(tables): 0} if buffer else None,
        )

    def exchange(value):
        value = value.reshape(planes * groups, chunks * pieces * dets, LANES)
        return lax.all_to_all(value, ("tm", "det"), split_axis=0, concat_axis=0, tiled=True).reshape(layout)

    count = f_high.shape[0]
    (mixed,) = call(
        mix_kernel, [array(*layout)], [(count, pieces * LANES)] * 2 + [layout, dma(2)],
        2 * 3 * count * count * pieces * LANES,
        exchange(buffer[0]), f_high, f_low, out_space=pl.ANY,
    )
    mixed, tables = lax.optimization_barrier((mixed, tables))
    tables = hold(tables)
    back = exchange(mixed)
    result = []
    for chunk in range(chunks):
        parts = call(
            bind(inverse_kernel, n1, n2, chunk), [block] * planes, [series, middle], flops, back, *tables
        )
        parts = rotate(parts)
        pairs = list(zip([*far_first(planes), 0], parts))
        pairs = [pairs[-1], *pairs[:-1]]
        for group in [pairs] if chunk < chunks - 1 else [pairs[:-1], pairs[-1:]]:
            steps, blocks = zip(*group)
            result = call(
                bind(place_kernel, chunk, steps), [array(planes, chunks, dets, span)], [dma(len(steps))], 0,
                *blocks, *result, spaces=[pl.ANY] * (len(steps) + len(result)), out_space=pl.ANY,
                aliases={len(steps): 0} if result else None,
            )
    return result[0].reshape(rows, span)


def solution(mesh):
    in_specs = (P("det", "tm"), P("det", "tm", None))
    return jax.shard_map(local, mesh=mesh, in_specs=in_specs, out_specs=P("det", "tm"), check_vma=False)
```

```python
import math

import jax
import jax.numpy as jnp
import ml_dtypes
import numpy as np
from jax import lax
from jax.experimental import pallas as pl
from jax.experimental.pallas import tpu as pltpu
from jax.sharding import PartitionSpec as P


LANES = 128
VMEM_LIMIT = 48 * 1024 * 1024
CHUNKS = 2


def band_of(plane, planes):
    return 2 * plane if 2 * plane < planes else 2 * (planes - 1 - plane) + 1


def fourier_matrix(n2, planes):
    share = n2 // (2 * planes)
    order = []
    for plane in range(planes):
        low = band_of(plane, planes) * share + np.arange(share)
        order.append(np.concatenate([low, n2 - 1 - low[::-1]]))
    order = np.stack(order)
    angle = 2.0 * np.pi / n2 * (np.arange(n2)[:, None, None] * order[None] % n2)
    cosine, sine = np.cos(angle), np.sin(angle)
    matrix = np.stack([np.stack([cosine, -sine], 2), np.stack([sine, cosine], 2)])
    matrix = matrix.reshape(2 * n2, 2 * n2).astype(np.float32)
    high = matrix.astype(ml_dtypes.bfloat16)
    low = (matrix - high.astype(np.float32)).astype(ml_dtypes.bfloat16)
    return high, low


def twiddles(n1, n2):
    angle = 2.0 * np.pi / (n1 * n2) * (np.arange(n1)[:, None] + 0.25) * np.arange(n2)[None, :]
    return np.stack([np.cos(angle), np.sin(angle)]).astype(np.float32)


def forward_butterflies(parts, shift):
    count = len(parts)
    if count == 1:
        return parts
    half = count // 2
    turn_re, turn_im = math.cos(math.pi * shift), -math.sin(math.pi * shift)
    even, odd = [], []
    for (a_re, a_im), (b_re, b_im) in zip(parts[:half], parts[half:]):
        c_re = b_re * turn_re - b_im * turn_im
        c_im = b_re * turn_im + b_im * turn_re
        even.append((a_re + c_re, a_im + c_im))
        odd.append((a_re - c_re, a_im - c_im))
    even = forward_butterflies(even, shift / 2)
    odd = forward_butterflies(odd, (1 + shift) / 2)
    return [part for pair in zip(even, odd) for part in pair]


def inverse_butterflies(parts, shift):
    if len(parts) == 1:
        return parts
    turn_re, turn_im = math.cos(math.pi * shift), math.sin(math.pi * shift)
    even = inverse_butterflies(parts[0::2], shift / 2)
    odd = inverse_butterflies(parts[1::2], (1 + shift) / 2)
    first, second = [], []
    for (a_re, a_im), (b_re, b_im) in zip(even, odd):
        d_re, d_im = a_re - b_re, a_im - b_im
        first.append((a_re + b_re, a_im + b_im))
        second.append((d_re * turn_re - d_im * turn_im, d_re * turn_im + d_im * turn_re))
    return first + second


def split(value):
    high = value.astype(jnp.bfloat16)
    return high, (value - high.astype(jnp.float32)).astype(jnp.bfloat16)


def product(left, right, contract=((1,), (0,))):
    def dot(a, b):
        return lax.dot_general(a, b, (contract, ((), ())), preferred_element_type=jnp.float32)

    rows = left[0].shape[0]
    both = dot(jnp.concatenate(left), right[0])
    return both[:rows] + (both[rows:] + dot(left[0], right[1]))


def tiles(rows, lanes):
    step = min(8, rows)
    for row in range(0, rows, step):
        for lane in range(0, lanes, LANES):
            yield slice(row, row + step), lane


def slice_kernel(noise_ref, *refs):
    here = lax.axis_index("tm")
    outs, sem = refs[:-1], refs[-1]
    copies = [
        pltpu.make_async_copy(noise_ref.at[here ^ step], out, sem.at[step]) for step, out in enumerate(outs)
    ]
    for copy in copies:
        copy.start()
    for copy in copies:
        copy.wait()


def hold_kernel(*refs):
    count = len(refs) // 2
    sem = refs[-1]
    copies = [pltpu.make_async_copy(refs[at], refs[count + at], sem.at[at]) for at in range(count)]
    for copy in copies:
        copy.start()
    for copy in copies:
        copy.wait()


def forward_kernel(n1, n2, planes, *refs):
    here = lax.axis_index("tm")
    blocks, (turn_ref, high_ref, low_ref) = refs[:planes], refs[planes : planes + 3]
    out_ref, x_ref, mid_ref, stage_ref, sem = refs[-5:]
    _, dets, span = x_ref.shape
    _, groups, pieces, _, width = stage_ref.shape
    per = span // n2
    for step, block in enumerate(reversed(blocks)):
        x_ref[here ^ step] = block[...]
    for rows, lane in tiles(dets, n2):

        def load(index):
            start = (index % per) * n2 + lane
            return x_ref[index // per, rows, start : start + LANES]

        parts = [(load(t1), -load(t1 + n1)) for t1 in range(n1)]
        for k1, (re, im) in enumerate(forward_butterflies(parts, 0.25)):
            cosine = turn_ref[0, k1 : k1 + 1, lane : lane + LANES]
            sine = turn_ref[1, k1 : k1 + 1, lane : lane + LANES]
            place = slice(k1 * dets + rows.start, k1 * dets + rows.stop)
            mid_ref[place, lane : lane + LANES] = re * cosine + im * sine
            mid_ref[place, n2 + lane : n2 + lane + LANES] = im * cosine - re * sine
    halves = split(mid_ref[...])
    copies = []
    share = planes // 2
    for part in range(2):
        columns = slice(part * share * width, (part + 1) * share * width)
        spectrum = product(halves, (high_ref[:, columns], low_ref[:, columns]))
        these = pl.ds(part * share, share)
        for plane in range(share):
            value = spectrum[:, plane * width : (plane + 1) * width]
            stage_ref[part * share + plane] = value.reshape(groups, pieces, dets, width)
        copies.append(pltpu.make_async_copy(stage_ref.at[these], out_ref.at[these], sem.at[part]))
        copies[-1].start()
    for copy in copies:
        copy.wait()


def inverse_kernel(n1, n2, chunk, y_ref, turn_ref, high_ref, low_ref, *refs):
    here = lax.axis_index("tm")
    outs, (x_ref, mid_ref) = refs[:-2], refs[-2:]
    _, dets, span = x_ref.shape
    planes, _, _, _, _, width = y_ref.shape
    per = span // n2
    scale = 1.0 / (n1 * n2)
    bins = jnp.concatenate([y_ref[plane, :, chunk].reshape(n1 * dets, width) for plane in range(planes)], axis=1)
    mid_ref[...] = product(split(bins), (high_ref[...], low_ref[...]), ((1,), (1,)))
    for rows, lane in tiles(dets, n2):
        parts = []
        for k1 in range(n1):
            cosine = turn_ref[0, k1 : k1 + 1, lane : lane + LANES] * scale
            sine = turn_ref[1, k1 : k1 + 1, lane : lane + LANES] * scale
            place = slice(k1 * dets + rows.start, k1 * dets + rows.stop)
            re = mid_ref[place, lane : lane + LANES]
            im = mid_ref[place, n2 + lane : n2 + lane + LANES]
            parts.append((re * cosine - im * sine, im * cosine + re * sine))
        for t1, (re, im) in enumerate(inverse_butterflies(parts, 0.25)):
            for index, value in ((t1, re), (t1 + n1, -im)):
                start = (index % per) * n2 + lane
                x_ref[index // per, rows, start : start + LANES] = value
    for step, out in enumerate(outs):
        out[...] = x_ref[here ^ step]


def place_kernel(chunk, *refs):
    here = lax.axis_index("tm")
    out_ref, sem = refs[-2:]
    planes = out_ref.shape[0]
    copies = [
        pltpu.make_async_copy(refs[planes - 1 - step], out_ref.at[here ^ step, chunk], sem.at[step])
        for step in range(planes)
    ]
    for copy in copies:
        copy.start()
    for copy in copies:
        copy.wait()


def factor_kernel(factor_ref, high_ref, low_ref):
    here = lax.axis_index("det")
    shares, rows, _ = factor_ref.shape
    for share in range(shares):
        source = here ^ (2 * share if 2 * share < shares else 2 * share - shares + 1)
        place = pl.ds(pl.multiple_of(source * rows, rows), rows)
        high_ref[place], low_ref[place] = split(factor_ref[share])


def mix_kernel(x_ref, f_high, f_low, out_ref, x_mid, y_mid):
    planes, groups, chunks, pieces, dets, width = out_ref.shape
    own = chunks * dets
    for plane, group, piece in np.ndindex(planes, groups, pieces):
        start = (group * planes + plane) * own
        x_mid[start : start + own, piece * width : (piece + 1) * width] = x_ref[plane, group, piece]
    x_high, x_low = split(x_mid[...])
    half = f_high.shape[0] // 2
    for part in range(2):
        rows, reach = slice(part * half, (part + 1) * half), (part + 1) * half
        y_mid[rows] = product((f_high[rows, :reach], f_low[rows, :reach]), (x_high[:reach], x_low[:reach]))
    for plane, group, chunk, piece in np.ndindex(planes, groups, chunks, pieces):
        start = (group * planes + plane) * own + chunk * dets
        out_ref[plane, group, chunk, piece] = y_mid[start : start + dets, piece * width : (piece + 1) * width]


def call(kernel, outs, scratch, flops, *args, spaces=None, out_space=pltpu.VMEM, aliases=None):
    spaces = spaces or [pltpu.VMEM] * len(args)
    count = sum(math.prod(arg.shape) * arg.dtype.itemsize for arg in (*args, *outs))
    return pl.pallas_call(
        kernel,
        out_shape=outs,
        in_specs=[pl.BlockSpec(memory_space=space) for space in spaces],
        out_specs=[pl.BlockSpec(memory_space=out_space)] * len(outs),
        scratch_shapes=[pltpu.VMEM(item, jnp.float32) if isinstance(item, tuple) else item for item in scratch],
        compiler_params=pltpu.CompilerParams(vmem_limit_bytes=VMEM_LIMIT),
        cost_estimate=pl.CostEstimate(flops=flops, bytes_accessed=count, transcendentals=0),
        input_output_aliases=aliases or {},
    )(*args)


def array(*shape, dtype=jnp.float32):
    return jax.ShapeDtypeStruct(shape, dtype)


def dma(count):
    return pltpu.SemaphoreType.DMA((count,))


def swap(value, axis, mask):
    return lax.ppermute(value, axis, [(place, place ^ mask) for place in range(lax.axis_size(axis))])


def trade(parts):
    return [swap(parts[step], "tm", step) for step in reversed(range(1, len(parts)))] + [parts[0]]


def plane_factor(factor, planes, groups):
    half = factor.shape[1] // 2
    upper = lax.axis_index("det") >= groups // 2
    mine = lax.dynamic_slice_in_dim(factor[0], jnp.where(upper, half, 0), half, 0)
    plane_of = {band_of(plane, planes): plane for plane in range(planes)}
    pairs = []
    for plane in range(planes):
        for group in range(groups):
            target = plane_of[min(group, groups - 1 - group)]
            pairs.append((plane * groups + group, target * groups + 2 * plane + (group >= groups // 2)))
    return lax.ppermute(mine, ("tm", "det"), pairs)


def band_factor(share, groups):
    rows, columns = share.shape
    share = jnp.stack([share] + [swap(share, "det", mask) for mask in range(2, groups, 2)])
    share = jnp.concatenate([share, swap(share, "det", 1)])
    whole = array(groups * rows, columns, dtype=jnp.bfloat16)
    return call(factor_kernel, [whole, whole], [], 0, share)


def hold(tables):
    outs = [array(*table.shape, dtype=table.dtype) for table in tables]
    return call(hold_kernel, outs, [dma(len(tables))], 0, *tables, spaces=[pl.ANY] * len(tables))


def bind(kernel, *static):
    return lambda *refs: kernel(*static, *refs)


def local(noise, factor):
    planes = lax.axis_size("tm")
    groups = lax.axis_size("det")
    rows, span = noise.shape
    own = rows // planes
    n2 = LANES // 2 * planes
    n1 = span * planes // 2 // n2
    pieces = n1 // groups
    chunks = CHUNKS if own % (8 * CHUNKS) == 0 else 1
    dets = own // chunks
    flops = 3 * 2 * n1 * own * (2 * n2) ** 2
    tables = hold((twiddles(n1, n2), *fourier_matrix(n2, planes)))

    def exchange(value, shape):
        value = value.reshape(planes * groups, pieces * own, LANES)
        return lax.all_to_all(value, ("tm", "det"), split_axis=0, concat_axis=0, tiled=True).reshape(shape)

    parts = call(
        slice_kernel, [array(own, span)] * planes, [dma(planes)], 0, noise.reshape(planes, own, span), spaces=[pl.ANY]
    )
    layout = (planes, groups, pieces, own, LANES)
    (spectrum,) = call(
        bind(forward_kernel, n1, n2, planes), [array(*layout)],
        [(planes, own, span), (n1 * own, 2 * n2), layout, dma(2)], flops, *trade(parts), *tables, out_space=pl.ANY,
    )
    spectrum, share = lax.optimization_barrier((spectrum, plane_factor(factor, planes, groups)))
    f_high, f_low = band_factor(share, groups)

    count = f_high.shape[0]
    (mixed,) = call(
        mix_kernel, [array(planes, groups, chunks, pieces, dets, LANES)], [(count, pieces * LANES)] * 2,
        2 * 3 * count * count * pieces * LANES, exchange(spectrum, layout), f_high, f_low,
    )
    back = exchange(mixed, mixed.shape)
    result = []
    for chunk in range(chunks):
        parts = call(
            bind(inverse_kernel, n1, n2, chunk), [array(dets, span)] * planes,
            [(planes, dets, span), (n1 * dets, 2 * n2)], flops // chunks, back, *tables,
        )
        result = call(
            bind(place_kernel, chunk), [array(planes, chunks, dets, span)], [dma(planes)], 0, *trade(parts), *result,
            spaces=[pl.ANY] * (planes + len(result)), out_space=pl.ANY, aliases={planes: 0} if result else None,
        )
    return result[0].reshape(rows, span)


def solution(mesh):
    in_specs = (P("det", "tm"), P("det", "tm", None))
    return jax.shard_map(local, mesh=mesh, in_specs=in_specs, out_specs=P("det", "tm"), check_vma=False)
```

```python
import math

import jax
import jax.numpy as jnp
import ml_dtypes
import numpy as np
from jax import lax
from jax.experimental import pallas as pl
from jax.experimental.pallas import tpu as pltpu
from jax.sharding import PartitionSpec as P


LANES = 128
VMEM_LIMIT = 48 * 1024 * 1024
CHUNKS = 2


def band_of(plane, planes):
    return 2 * plane if 2 * plane < planes else 2 * (planes - 1 - plane) + 1


def fourier_matrix(n2, planes):
    share = n2 // (2 * planes)
    order = []
    for plane in range(planes):
        low = band_of(plane, planes) * share + np.arange(share)
        order.append(np.concatenate([low, n2 - 1 - low[::-1]]))
    order = np.stack(order)
    angle = 2.0 * np.pi / n2 * (np.arange(n2)[:, None, None] * order[None] % n2)
    cosine, sine = np.cos(angle), np.sin(angle)
    matrix = np.stack([np.stack([cosine, -sine], 2), np.stack([sine, cosine], 2)])
    matrix = matrix.reshape(2 * n2, 2 * n2).astype(np.float32)
    high = matrix.astype(ml_dtypes.bfloat16)
    low = (matrix - high.astype(np.float32)).astype(ml_dtypes.bfloat16)
    return high, low


def twiddles(n1, n2):
    angle = 2.0 * np.pi / (n1 * n2) * (np.arange(n1)[:, None] + 0.25) * np.arange(n2)[None, :]
    return np.stack([np.cos(angle), np.sin(angle)]).astype(np.float32)


def forward_butterflies(parts, shift):
    count = len(parts)
    if count == 1:
        return parts
    half = count // 2
    turn_re, turn_im = math.cos(math.pi * shift), -math.sin(math.pi * shift)
    even, odd = [], []
    for (a_re, a_im), (b_re, b_im) in zip(parts[:half], parts[half:]):
        c_re = b_re * turn_re - b_im * turn_im
        c_im = b_re * turn_im + b_im * turn_re
        even.append((a_re + c_re, a_im + c_im))
        odd.append((a_re - c_re, a_im - c_im))
    even = forward_butterflies(even, shift / 2)
    odd = forward_butterflies(odd, (1 + shift) / 2)
    return [part for pair in zip(even, odd) for part in pair]


def inverse_butterflies(parts, shift):
    if len(parts) == 1:
        return parts
    turn_re, turn_im = math.cos(math.pi * shift), math.sin(math.pi * shift)
    even = inverse_butterflies(parts[0::2], shift / 2)
    odd = inverse_butterflies(parts[1::2], (1 + shift) / 2)
    first, second = [], []
    for (a_re, a_im), (b_re, b_im) in zip(even, odd):
        d_re, d_im = a_re - b_re, a_im - b_im
        first.append((a_re + b_re, a_im + b_im))
        second.append((d_re * turn_re - d_im * turn_im, d_re * turn_im + d_im * turn_re))
    return first + second


def split(value):
    high = value.astype(jnp.bfloat16)
    return high, (value - high.astype(jnp.float32)).astype(jnp.bfloat16)


def product(left, right, contract=((1,), (0,))):
    def dot(a, b):
        return lax.dot_general(a, b, (contract, ((), ())), preferred_element_type=jnp.float32)

    rows = left[0].shape[0]
    both = dot(jnp.concatenate(left), right[0])
    return both[:rows] + (both[rows:] + dot(left[0], right[1]))


def tiles(rows, lanes):
    step = min(8, rows)
    for row in range(0, rows, step):
        for lane in range(0, lanes, LANES):
            yield slice(row, row + step), lane


def slice_kernel(noise_ref, *refs):
    here = lax.axis_index("tm")
    outs, sem = refs[:-1], refs[-1]
    copies = [
        pltpu.make_async_copy(noise_ref.at[here ^ step], out, sem.at[step]) for step, out in enumerate(outs)
    ]
    for copy in copies:
        copy.start()
    for copy in copies:
        copy.wait()


def forward_kernel(n1, n2, planes, *refs):
    here = lax.axis_index("tm")
    blocks, (turn_ref, high_ref, low_ref) = refs[:planes], refs[planes : planes + 3]
    out_ref, x_ref, mid_ref, stage_ref, sem = refs[-5:]
    _, dets, span = x_ref.shape
    _, groups, pieces, _, width = stage_ref.shape
    per = span // n2
    for step, block in enumerate(reversed(blocks)):
        x_ref[here ^ step] = block[...]
    for rows, lane in tiles(dets, n2):

        def load(index):
            start = (index % per) * n2 + lane
            return x_ref[index // per, rows, start : start + LANES]

        parts = [(load(t1), -load(t1 + n1)) for t1 in range(n1)]
        for k1, (re, im) in enumerate(forward_butterflies(parts, 0.25)):
            cosine = turn_ref[0, k1 : k1 + 1, lane : lane + LANES]
            sine = turn_ref[1, k1 : k1 + 1, lane : lane + LANES]
            place = slice(k1 * dets + rows.start, k1 * dets + rows.stop)
            mid_ref[place, lane : lane + LANES] = re * cosine + im * sine
            mid_ref[place, n2 + lane : n2 + lane + LANES] = im * cosine - re * sine
    halves = split(mid_ref[...])
    copies = []
    share = planes // 2
    for part in range(2):
        columns = slice(part * share * width, (part + 1) * share * width)
        spectrum = product(halves, (high_ref[:, columns], low_ref[:, columns]))
        these = pl.ds(part * share, share)
        for plane in range(share):
            value = spectrum[:, plane * width : (plane + 1) * width]
            stage_ref[part * share + plane] = value.reshape(groups, pieces, dets, width)
        copies.append(pltpu.make_async_copy(stage_ref.at[these], out_ref.at[these], sem.at[part]))
        copies[-1].start()
    for copy in copies:
        copy.wait()


def inverse_kernel(n1, n2, chunk, y_ref, turn_ref, high_ref, low_ref, *refs):
    here = lax.axis_index("tm")
    outs, (x_ref, mid_ref) = refs[:-2], refs[-2:]
    _, dets, span = x_ref.shape
    planes, _, _, _, _, width = y_ref.shape
    per = span // n2
    scale = 1.0 / (n1 * n2)
    bins = jnp.concatenate([y_ref[plane, :, chunk].reshape(n1 * dets, width) for plane in range(planes)], axis=1)
    mid_ref[...] = product(split(bins), (high_ref[...], low_ref[...]), ((1,), (1,)))
    for rows, lane in tiles(dets, n2):
        parts = []
        for k1 in range(n1):
            cosine = turn_ref[0, k1 : k1 + 1, lane : lane + LANES] * scale
            sine = turn_ref[1, k1 : k1 + 1, lane : lane + LANES] * scale
            place = slice(k1 * dets + rows.start, k1 * dets + rows.stop)
            re = mid_ref[place, lane : lane + LANES]
            im = mid_ref[place, n2 + lane : n2 + lane + LANES]
            parts.append((re * cosine - im * sine, im * cosine + re * sine))
        for t1, (re, im) in enumerate(inverse_butterflies(parts, 0.25)):
            for index, value in ((t1, re), (t1 + n1, -im)):
                start = (index % per) * n2 + lane
                x_ref[index // per, rows, start : start + LANES] = value
    for step, out in enumerate(outs):
        out[...] = x_ref[here ^ step]


def place_kernel(chunk, *refs):
    here = lax.axis_index("tm")
    out_ref, sem = refs[-2:]
    planes = out_ref.shape[0]
    copies = [
        pltpu.make_async_copy(refs[planes - 1 - step], out_ref.at[here ^ step, chunk], sem.at[step])
        for step in range(planes)
    ]
    for copy in copies:
        copy.start()
    for copy in copies:
        copy.wait()


def factor_kernel(factor_ref, high_ref, low_ref):
    here = lax.axis_index("det")
    shares, rows, _ = factor_ref.shape
    for share in range(shares):
        source = here ^ (2 * share if 2 * share < shares else 2 * share - shares + 1)
        place = pl.ds(pl.multiple_of(source * rows, rows), rows)
        high_ref[place], low_ref[place] = split(factor_ref[share])


def mix_kernel(x_ref, f_high, f_low, out_ref, x_mid, y_mid):
    planes, groups, chunks, pieces, dets, width = out_ref.shape
    own = chunks * dets
    for plane, group, piece in np.ndindex(planes, groups, pieces):
        start = (group * planes + plane) * own
        x_mid[start : start + own, piece * width : (piece + 1) * width] = x_ref[plane, group, piece]
    x_high, x_low = split(x_mid[...])
    half = f_high.shape[0] // 2
    for part in range(2):
        rows, reach = slice(part * half, (part + 1) * half), (part + 1) * half
        y_mid[rows] = product((f_high[rows, :reach], f_low[rows, :reach]), (x_high[:reach], x_low[:reach]))
    for plane, group, chunk, piece in np.ndindex(planes, groups, chunks, pieces):
        start = (group * planes + plane) * own + chunk * dets
        out_ref[plane, group, chunk, piece] = y_mid[start : start + dets, piece * width : (piece + 1) * width]


def call(kernel, outs, scratch, flops, *args, spaces=None, out_space=pltpu.VMEM, aliases=None):
    spaces = spaces or [pltpu.VMEM] * len(args)
    count = sum(math.prod(arg.shape) * arg.dtype.itemsize for arg in (*args, *outs))
    return pl.pallas_call(
        kernel,
        out_shape=outs,
        in_specs=[pl.BlockSpec(memory_space=space) for space in spaces],
        out_specs=[pl.BlockSpec(memory_space=out_space)] * len(outs),
        scratch_shapes=[pltpu.VMEM(item, jnp.float32) if isinstance(item, tuple) else item for item in scratch],
        compiler_params=pltpu.CompilerParams(vmem_limit_bytes=VMEM_LIMIT),
        cost_estimate=pl.CostEstimate(flops=flops, bytes_accessed=count, transcendentals=0),
        input_output_aliases=aliases or {},
    )(*args)


def array(*shape, dtype=jnp.float32):
    return jax.ShapeDtypeStruct(shape, dtype)


def dma(count):
    return pltpu.SemaphoreType.DMA((count,))


def swap(value, axis, mask):
    return lax.ppermute(value, axis, [(place, place ^ mask) for place in range(lax.axis_size(axis))])


def trade(parts):
    return [swap(parts[step], "tm", step) for step in reversed(range(1, len(parts)))] + [parts[0]]


def plane_factor(factor, planes, groups):
    half = factor.shape[1] // 2
    upper = lax.axis_index("det") >= groups // 2
    mine = lax.dynamic_slice_in_dim(factor[0], jnp.where(upper, half, 0), half, 0)
    plane_of = {band_of(plane, planes): plane for plane in range(planes)}
    pairs = []
    for plane in range(planes):
        for group in range(groups):
            target = plane_of[min(group, groups - 1 - group)]
            pairs.append((plane * groups + group, target * groups + 2 * plane + (group >= groups // 2)))
    return lax.ppermute(mine, ("tm", "det"), pairs)


def band_factor(share, groups):
    rows, columns = share.shape
    share = jnp.stack([share] + [swap(share, "det", mask) for mask in range(2, groups, 2)])
    share = jnp.concatenate([share, swap(share, "det", 1)])
    whole = array(groups * rows, columns, dtype=jnp.bfloat16)
    return call(factor_kernel, [whole, whole], [], 0, share)


def bind(kernel, *static):
    return lambda *refs: kernel(*static, *refs)


def local(noise, factor):
    planes = lax.axis_size("tm")
    groups = lax.axis_size("det")
    rows, span = noise.shape
    own = rows // planes
    n2 = LANES // 2 * planes
    n1 = span * planes // 2 // n2
    pieces = n1 // groups
    chunks = CHUNKS if own % (8 * CHUNKS) == 0 else 1
    dets = own // chunks
    flops = 3 * 2 * n1 * own * (2 * n2) ** 2
    tables = (twiddles(n1, n2), *fourier_matrix(n2, planes))

    def exchange(value, shape):
        value = value.reshape(planes * groups, pieces * own, LANES)
        return lax.all_to_all(value, ("tm", "det"), split_axis=0, concat_axis=0, tiled=True).reshape(shape)

    parts = call(
        slice_kernel, [array(own, span)] * planes, [dma(planes)], 0, noise.reshape(planes, own, span), spaces=[pl.ANY],
        out_space=pl.ANY,
    )
    layout = (planes, groups, pieces, own, LANES)
    (spectrum,) = call(
        bind(forward_kernel, n1, n2, planes), [array(*layout)],
        [(planes, own, span), (n1 * own, 2 * n2), layout, dma(2)], flops, *trade(parts), *tables, out_space=pl.ANY,
    )
    spectrum, share = lax.optimization_barrier((spectrum, plane_factor(factor, planes, groups)))
    f_high, f_low = band_factor(share, groups)

    count = f_high.shape[0]
    (mixed,) = call(
        mix_kernel, [array(planes, groups, chunks, pieces, dets, LANES)], [(count, pieces * LANES)] * 2,
        2 * 3 * count * count * pieces * LANES, exchange(spectrum, layout), f_high, f_low,
    )
    back = exchange(mixed, mixed.shape)
    result = []
    for chunk in range(chunks):
        parts = call(
            bind(inverse_kernel, n1, n2, chunk), [array(dets, span)] * planes,
            [(planes, dets, span), (n1 * dets, 2 * n2)], flops // chunks, back, *tables,
        )
        result = call(
            bind(place_kernel, chunk), [array(planes, chunks, dets, span)], [dma(planes)], 0, *trade(parts), *result,
            spaces=[pl.ANY] * (planes + len(result)), out_space=pl.ANY, aliases={planes: 0} if result else None,
        )
    return result[0].reshape(rows, span)


def solution(mesh):
    in_specs = (P("det", "tm"), P("det", "tm", None))
    return jax.shard_map(local, mesh=mesh, in_specs=in_specs, out_specs=P("det", "tm"), check_vma=False)
```

```python
import math

import jax
import jax.numpy as jnp
import ml_dtypes
import numpy as np
from jax import lax
from jax.experimental import pallas as pl
from jax.experimental.pallas import tpu as pltpu
from jax.sharding import PartitionSpec as P


LANES = 128
VMEM_LIMIT = 48 * 1024 * 1024
CHUNKS = 2


def band_of(plane, planes):
    return 2 * plane if 2 * plane < planes else 2 * (planes - 1 - plane) + 1


def fourier_matrix(n2, planes):
    share = n2 // (2 * planes)
    order = []
    for plane in range(planes):
        low = band_of(plane, planes) * share + np.arange(share)
        order.append(np.concatenate([low, n2 - 1 - low[::-1]]))
    order = np.stack(order)
    angle = 2.0 * np.pi / n2 * (np.arange(n2)[:, None, None] * order[None] % n2)
    cosine, sine = np.cos(angle), np.sin(angle)
    matrix = np.stack([np.stack([cosine, -sine], 2), np.stack([sine, cosine], 2)])
    matrix = matrix.reshape(2 * n2, 2 * n2).astype(np.float32)
    high = matrix.astype(ml_dtypes.bfloat16)
    low = (matrix - high.astype(np.float32)).astype(ml_dtypes.bfloat16)
    return high, low


def twiddles(n1, n2):
    angle = 2.0 * np.pi / (n1 * n2) * (np.arange(n1)[:, None] + 0.25) * np.arange(n2)[None, :]
    return np.stack([np.cos(angle), np.sin(angle)]).astype(np.float32)


def forward_butterflies(parts, shift):
    count = len(parts)
    if count == 1:
        return parts
    half = count // 2
    turn_re, turn_im = math.cos(math.pi * shift), -math.sin(math.pi * shift)
    even, odd = [], []
    for (a_re, a_im), (b_re, b_im) in zip(parts[:half], parts[half:]):
        c_re = b_re * turn_re - b_im * turn_im
        c_im = b_re * turn_im + b_im * turn_re
        even.append((a_re + c_re, a_im + c_im))
        odd.append((a_re - c_re, a_im - c_im))
    even = forward_butterflies(even, shift / 2)
    odd = forward_butterflies(odd, (1 + shift) / 2)
    return [part for pair in zip(even, odd) for part in pair]


def inverse_butterflies(parts, shift):
    if len(parts) == 1:
        return parts
    turn_re, turn_im = math.cos(math.pi * shift), math.sin(math.pi * shift)
    even = inverse_butterflies(parts[0::2], shift / 2)
    odd = inverse_butterflies(parts[1::2], (1 + shift) / 2)
    first, second = [], []
    for (a_re, a_im), (b_re, b_im) in zip(even, odd):
        d_re, d_im = a_re - b_re, a_im - b_im
        first.append((a_re + b_re, a_im + b_im))
        second.append((d_re * turn_re - d_im * turn_im, d_re * turn_im + d_im * turn_re))
    return first + second


def split(value):
    high = value.astype(jnp.bfloat16)
    return high, (value - high.astype(jnp.float32)).astype(jnp.bfloat16)


def product(left, right, contract=((1,), (0,))):
    def dot(a, b):
        return lax.dot_general(a, b, (contract, ((), ())), preferred_element_type=jnp.float32)

    rows = left[0].shape[0]
    both = dot(jnp.concatenate(left), right[0])
    return both[:rows] + (both[rows:] + dot(left[0], right[1]))


def tiles(rows, lanes):
    step = min(8, rows)
    for row in range(0, rows, step):
        for lane in range(0, lanes, LANES):
            yield slice(row, row + step), lane


def slice_kernel(noise_ref, *refs):
    here = lax.axis_index("tm")
    outs, sem = refs[:-1], refs[-1]
    copies = [
        pltpu.make_async_copy(noise_ref.at[here ^ step], out, sem.at[step]) for step, out in enumerate(outs)
    ]
    for copy in copies:
        copy.start()
    for copy in copies:
        copy.wait()


def forward_kernel(n1, n2, planes, *refs):
    here = lax.axis_index("tm")
    blocks, (turn_ref, high_ref, low_ref) = refs[:planes], refs[planes : planes + 3]
    out_ref, x_ref, mid_ref, stage_ref, sem = refs[-5:]
    span = x_ref.shape[-1]
    _, groups, chunks, pieces, dets, width = stage_ref.shape
    per = span // n2
    for step, block in enumerate(reversed(blocks)):
        x_ref[here ^ step] = block[...]
    copies = []
    for chunk in range(chunks):
        for tile, lane in tiles(dets, n2):
            rows = slice(chunk * dets + tile.start, chunk * dets + tile.stop)

            def load(index):
                start = (index % per) * n2 + lane
                return x_ref[index // per, rows, start : start + LANES]

            parts = [(load(t1), -load(t1 + n1)) for t1 in range(n1)]
            for k1, (re, im) in enumerate(forward_butterflies(parts, 0.25)):
                cosine = turn_ref[0, k1 : k1 + 1, lane : lane + LANES]
                sine = turn_ref[1, k1 : k1 + 1, lane : lane + LANES]
                place = slice(k1 * dets + tile.start, k1 * dets + tile.stop)
                mid_ref[chunk, place, lane : lane + LANES] = re * cosine + im * sine
                mid_ref[chunk, place, n2 + lane : n2 + lane + LANES] = im * cosine - re * sine
        spectrum = product(split(mid_ref[chunk]), (high_ref[...], low_ref[...]))
        for plane in range(planes):
            value = spectrum[:, plane * width : (plane + 1) * width]
            stage_ref[plane, :, chunk] = value.reshape(groups, pieces, dets, width)
        copies.append(pltpu.make_async_copy(stage_ref.at[:, :, chunk], out_ref.at[:, :, chunk], sem.at[chunk]))
        copies[-1].start()
    for copy in copies:
        copy.wait()


def inverse_kernel(n1, n2, chunk, y_ref, turn_ref, high_ref, low_ref, *refs):
    here = lax.axis_index("tm")
    outs, (x_ref, mid_ref) = refs[:-2], refs[-2:]
    _, dets, span = x_ref.shape
    planes, _, _, _, _, width = y_ref.shape
    per = span // n2
    scale = 1.0 / (n1 * n2)
    bins = jnp.concatenate([y_ref[plane, :, chunk].reshape(n1 * dets, width) for plane in range(planes)], axis=1)
    mid_ref[...] = product(split(bins), (high_ref[...], low_ref[...]), ((1,), (1,)))
    for rows, lane in tiles(dets, n2):
        parts = []
        for k1 in range(n1):
            cosine = turn_ref[0, k1 : k1 + 1, lane : lane + LANES] * scale
            sine = turn_ref[1, k1 : k1 + 1, lane : lane + LANES] * scale
            place = slice(k1 * dets + rows.start, k1 * dets + rows.stop)
            re = mid_ref[place, lane : lane + LANES]
            im = mid_ref[place, n2 + lane : n2 + lane + LANES]
            parts.append((re * cosine - im * sine, im * cosine + re * sine))
        for t1, (re, im) in enumerate(inverse_butterflies(parts, 0.25)):
            for index, value in ((t1, re), (t1 + n1, -im)):
                start = (index % per) * n2 + lane
                x_ref[index // per, rows, start : start + LANES] = value
    for step, out in enumerate(outs):
        out[...] = x_ref[here ^ step]


def place_kernel(chunk, *refs):
    here = lax.axis_index("tm")
    out_ref, sem = refs[-2:]
    planes = out_ref.shape[0]
    copies = [
        pltpu.make_async_copy(refs[planes - 1 - step], out_ref.at[here ^ step, chunk], sem.at[step])
        for step in range(planes)
    ]
    for copy in copies:
        copy.start()
    for copy in copies:
        copy.wait()


def factor_kernel(factor_ref, high_ref, low_ref):
    here = lax.axis_index("det")
    shares, rows, _ = factor_ref.shape
    for share in range(shares):
        source = here ^ (2 * share if 2 * share < shares else 2 * share - shares + 1)
        place = pl.ds(pl.multiple_of(source * rows, rows), rows)
        high_ref[place], low_ref[place] = split(factor_ref[share])


def mix_kernel(x_ref, f_high, f_low, out_ref, x_mid, y_mid):
    planes, groups, chunks, pieces, dets, width = out_ref.shape
    places = []
    for plane, group, chunk, piece in np.ndindex(planes, groups, chunks, pieces):
        start = ((group * planes + plane) * chunks + chunk) * dets
        rows, lanes = slice(start, start + dets), slice(piece * width, (piece + 1) * width)
        places.append(((plane, group, chunk, piece), (rows, lanes)))
    for source, target in places:
        x_mid[target] = x_ref[source]
    x_high, x_low = split(x_mid[...])
    half = f_high.shape[0] // 2
    for part in range(2):
        rows, reach = slice(part * half, (part + 1) * half), (part + 1) * half
        y_mid[rows] = product((f_high[rows, :reach], f_low[rows, :reach]), (x_high[:reach], x_low[:reach]))
    for target, source in places:
        out_ref[target] = y_mid[source]


def call(kernel, outs, scratch, flops, *args, spaces=None, out_space=pltpu.VMEM, aliases=None):
    spaces = spaces or [pltpu.VMEM] * len(args)
    count = sum(math.prod(arg.shape) * arg.dtype.itemsize for arg in (*args, *outs))
    return pl.pallas_call(
        kernel,
        out_shape=outs,
        in_specs=[pl.BlockSpec(memory_space=space) for space in spaces],
        out_specs=[pl.BlockSpec(memory_space=out_space)] * len(outs),
        scratch_shapes=[pltpu.VMEM(item, jnp.float32) if isinstance(item, tuple) else item for item in scratch],
        compiler_params=pltpu.CompilerParams(vmem_limit_bytes=VMEM_LIMIT),
        cost_estimate=pl.CostEstimate(flops=flops, bytes_accessed=count, transcendentals=0),
        input_output_aliases=aliases or {},
    )(*args)


def array(*shape, dtype=jnp.float32):
    return jax.ShapeDtypeStruct(shape, dtype)


def dma(count):
    return pltpu.SemaphoreType.DMA((count,))


def swap(value, axis, mask):
    return lax.ppermute(value, axis, [(place, place ^ mask) for place in range(lax.axis_size(axis))])


def trade(parts):
    return [swap(parts[step], "tm", step) for step in reversed(range(1, len(parts)))] + [parts[0]]


def plane_factor(factor, planes, groups):
    half = factor.shape[1] // 2
    upper = lax.axis_index("det") >= groups // 2
    mine = lax.dynamic_slice_in_dim(factor[0], jnp.where(upper, half, 0), half, 0)
    plane_of = {band_of(plane, planes): plane for plane in range(planes)}
    pairs = []
    for plane in range(planes):
        for group in range(groups):
            target = plane_of[min(group, groups - 1 - group)]
            pairs.append((plane * groups + group, target * groups + 2 * plane + (group >= groups // 2)))
    middle = factor.shape[2] // 2
    low = lax.ppermute(mine[:, :middle], ("tm", "det"), pairs)
    high = lax.ppermute(mine[:, middle:], ("tm", "det"), [pair for pair in pairs if 2 * (pair[0] // groups) >= planes])
    return low, high


def band_factor(sides, groups):
    share = jnp.concatenate(sides, axis=1)
    rows, columns = share.shape
    share = jnp.stack([share] + [swap(share, "det", mask) for mask in range(2, groups, 2)])
    share = jnp.concatenate([share, swap(share, "det", 1)])
    whole = array(groups * rows, columns, dtype=jnp.bfloat16)
    return call(factor_kernel, [whole, whole], [], 0, share)


def bind(kernel, *static):
    return lambda *refs: kernel(*static, *refs)


def local(noise, factor):
    planes = lax.axis_size("tm")
    groups = lax.axis_size("det")
    rows, span = noise.shape
    own = rows // planes
    n2 = LANES // 2 * planes
    n1 = span * planes // 2 // n2
    pieces = n1 // groups
    chunks = CHUNKS if own % (8 * CHUNKS) == 0 else 1
    dets = own // chunks
    flops = 3 * 2 * n1 * own * (2 * n2) ** 2
    tables = (twiddles(n1, n2), *fourier_matrix(n2, planes))

    parts = call(
        slice_kernel, [array(own, span)] * planes, [dma(planes)], 0, noise.reshape(planes, own, span), spaces=[pl.ANY],
        out_space=pl.ANY,
    )
    layout = (planes, groups, chunks, pieces, dets, LANES)

    def exchange(value):
        value = value.reshape(planes * groups, pieces * own, LANES)
        return lax.all_to_all(value, ("tm", "det"), split_axis=0, concat_axis=0, tiled=True).reshape(layout)

    (spectrum,) = call(
        bind(forward_kernel, n1, n2, planes), [array(*layout)],
        [(planes, own, span), (chunks, n1 * dets, 2 * n2), layout, dma(chunks)], flops, *trade(parts), *tables, out_space=pl.ANY,
    )
    spectrum, sides = lax.optimization_barrier((spectrum, plane_factor(factor, planes, groups)))
    f_high, f_low = band_factor(sides, groups)

    count = f_high.shape[0]
    (mixed,) = call(
        mix_kernel, [array(*layout)], [(count, pieces * LANES)] * 2,
        2 * 3 * count * count * pieces * LANES, exchange(spectrum), f_high, f_low,
    )
    back = exchange(mixed)
    result = []
    for chunk in range(chunks):
        parts = call(
            bind(inverse_kernel, n1, n2, chunk), [array(dets, span)] * planes,
            [(planes, dets, span), (n1 * dets, 2 * n2)], flops // chunks, back, *tables,
        )
        result = call(
            bind(place_kernel, chunk), [array(planes, chunks, dets, span)], [dma(planes)], 0, *trade(parts), *result,
            spaces=[pl.ANY] * (planes + len(result)), out_space=pl.ANY, aliases={planes: 0} if result else None,
        )
    return result[0].reshape(rows, span)


def solution(mesh):
    in_specs = (P("det", "tm"), P("det", "tm", None))
    return jax.shard_map(local, mesh=mesh, in_specs=in_specs, out_specs=P("det", "tm"), check_vma=False)
```

```python
import math

import jax
import jax.numpy as jnp
import ml_dtypes
import numpy as np
from jax import lax
from jax.experimental import pallas as pl
from jax.experimental.pallas import tpu as pltpu
from jax.sharding import PartitionSpec as P


LANES = 128
VMEM_LIMIT = 48 * 1024 * 1024
CHUNKS = 2
FACTOR_WORK = 7 * 10**9


def band_of(plane, planes):
    return 2 * plane if 2 * plane < planes else 2 * (planes - 1 - plane) + 1


def fourier_matrix(n2, planes):
    share = n2 // (2 * planes)
    order = []
    for plane in range(planes):
        low = band_of(plane, planes) * share + np.arange(share)
        order.append(np.concatenate([low, n2 - 1 - low[::-1]]))
    order = np.stack(order)
    angle = 2.0 * np.pi / n2 * (np.arange(n2)[:, None, None] * order[None] % n2)
    cosine, sine = np.cos(angle), np.sin(angle)
    matrix = np.stack([np.stack([cosine, -sine], 2), np.stack([sine, cosine], 2)])
    matrix = matrix.reshape(2 * n2, 2 * n2).astype(np.float32)
    high = matrix.astype(ml_dtypes.bfloat16)
    low = (matrix - high.astype(np.float32)).astype(ml_dtypes.bfloat16)
    return high, low


def twiddles(n1, n2):
    angle = 2.0 * np.pi / (n1 * n2) * (np.arange(n1)[:, None] + 0.25) * np.arange(n2)[None, :]
    return np.stack([np.cos(angle), np.sin(angle)]).astype(np.float32)


def forward_butterflies(parts, shift):
    count = len(parts)
    if count == 1:
        return parts
    half = count // 2
    turn_re, turn_im = math.cos(math.pi * shift), -math.sin(math.pi * shift)
    even, odd = [], []
    for (a_re, a_im), (b_re, b_im) in zip(parts[:half], parts[half:]):
        c_re = b_re * turn_re - b_im * turn_im
        c_im = b_re * turn_im + b_im * turn_re
        even.append((a_re + c_re, a_im + c_im))
        odd.append((a_re - c_re, a_im - c_im))
    even = forward_butterflies(even, shift / 2)
    odd = forward_butterflies(odd, (1 + shift) / 2)
    return [part for pair in zip(even, odd) for part in pair]


def inverse_butterflies(parts, shift):
    if len(parts) == 1:
        return parts
    turn_re, turn_im = math.cos(math.pi * shift), math.sin(math.pi * shift)
    even = inverse_butterflies(parts[0::2], shift / 2)
    odd = inverse_butterflies(parts[1::2], (1 + shift) / 2)
    first, second = [], []
    for (a_re, a_im), (b_re, b_im) in zip(even, odd):
        d_re, d_im = a_re - b_re, a_im - b_im
        first.append((a_re + b_re, a_im + b_im))
        second.append((d_re * turn_re - d_im * turn_im, d_re * turn_im + d_im * turn_re))
    return first + second


def split(value):
    high = value.astype(jnp.bfloat16)
    return high, (value - high.astype(jnp.float32)).astype(jnp.bfloat16)


def product(left, right, contract=((1,), (0,))):
    def dot(a, b):
        return lax.dot_general(a, b, (contract, ((), ())), preferred_element_type=jnp.float32)

    rows = left[0].shape[0]
    both = dot(jnp.concatenate(left), right[0])
    return both[:rows] + (both[rows:] + dot(left[0], right[1]))


def tiles(rows, lanes):
    step = min(8, rows)
    for row in range(0, rows, step):
        for lane in range(0, lanes, LANES):
            yield slice(row, row + step), lane


def slice_kernel(noise_ref, *refs):
    here = lax.axis_index("tm")
    outs, sem = refs[:-1], refs[-1]
    copies = [
        pltpu.make_async_copy(noise_ref.at[here ^ step], out, sem.at[step]) for step, out in enumerate(outs)
    ]
    for copy in copies:
        copy.start()
    for copy in copies:
        copy.wait()


def forward_kernel(n1, n2, planes, *refs):
    here = lax.axis_index("tm")
    blocks, (turn_ref, high_ref, low_ref) = refs[:planes], refs[planes : planes + 3]
    out_ref, x_ref, mid_ref, stage_ref, sem = refs[-5:]
    span = x_ref.shape[-1]
    _, groups, chunks, pieces, dets, width = stage_ref.shape
    per = span // n2
    for step, block in enumerate(reversed(blocks)):
        x_ref[here ^ step] = block[...]
    copies = []
    for chunk in range(chunks):
        for tile, lane in tiles(dets, n2):
            rows = slice(chunk * dets + tile.start, chunk * dets + tile.stop)

            def load(index):
                start = (index % per) * n2 + lane
                return x_ref[index // per, rows, start : start + LANES]

            parts = [(load(t1), -load(t1 + n1)) for t1 in range(n1)]
            for k1, (re, im) in enumerate(forward_butterflies(parts, 0.25)):
                cosine = turn_ref[0, k1 : k1 + 1, lane : lane + LANES]
                sine = turn_ref[1, k1 : k1 + 1, lane : lane + LANES]
                place = slice(k1 * dets + tile.start, k1 * dets + tile.stop)
                mid_ref[chunk, place, lane : lane + LANES] = re * cosine + im * sine
                mid_ref[chunk, place, n2 + lane : n2 + lane + LANES] = im * cosine - re * sine
        spectrum = product(split(mid_ref[chunk]), (high_ref[...], low_ref[...]))
        for plane in range(planes):
            value = spectrum[:, plane * width : (plane + 1) * width]
            stage_ref[plane, :, chunk] = value.reshape(groups, pieces, dets, width)
        copies.append(pltpu.make_async_copy(stage_ref.at[:, :, chunk], out_ref.at[:, :, chunk], sem.at[chunk]))
        copies[-1].start()
    for copy in copies:
        copy.wait()


def inverse_kernel(n1, n2, chunk, y_ref, turn_ref, high_ref, low_ref, *refs):
    here = lax.axis_index("tm")
    outs, (x_ref, mid_ref) = refs[:-2], refs[-2:]
    _, dets, span = x_ref.shape
    planes, _, _, _, _, width = y_ref.shape
    per = span // n2
    scale = 1.0 / (n1 * n2)
    bins = jnp.concatenate([y_ref[plane, :, chunk].reshape(n1 * dets, width) for plane in range(planes)], axis=1)
    mid_ref[...] = product(split(bins), (high_ref[...], low_ref[...]), ((1,), (1,)))
    for rows, lane in tiles(dets, n2):
        parts = []
        for k1 in range(n1):
            cosine = turn_ref[0, k1 : k1 + 1, lane : lane + LANES] * scale
            sine = turn_ref[1, k1 : k1 + 1, lane : lane + LANES] * scale
            place = slice(k1 * dets + rows.start, k1 * dets + rows.stop)
            re = mid_ref[place, lane : lane + LANES]
            im = mid_ref[place, n2 + lane : n2 + lane + LANES]
            parts.append((re * cosine - im * sine, im * cosine + re * sine))
        for t1, (re, im) in enumerate(inverse_butterflies(parts, 0.25)):
            for index, value in ((t1, re), (t1 + n1, -im)):
                start = (index % per) * n2 + lane
                x_ref[index // per, rows, start : start + LANES] = value
    for step, out in enumerate(outs):
        out[...] = x_ref[here ^ step]


def place_kernel(chunk, *refs):
    here = lax.axis_index("tm")
    out_ref, sem = refs[-2:]
    planes = out_ref.shape[0]
    copies = [
        pltpu.make_async_copy(refs[planes - 1 - step], out_ref.at[here ^ step, chunk], sem.at[step])
        for step in range(planes)
    ]
    for copy in copies:
        copy.start()
    for copy in copies:
        copy.wait()


def factor_kernel(factor_ref, high_ref, low_ref):
    here = lax.axis_index("det")
    shares, rows, _ = factor_ref.shape
    for share in range(shares):
        source = here ^ (2 * share if 2 * share < shares else 2 * share - shares + 1)
        place = pl.ds(pl.multiple_of(source * rows, rows), rows)
        high_ref[place], low_ref[place] = split(factor_ref[share])


def mix_kernel(x_ref, f_high, f_low, out_ref, x_mid, y_mid):
    planes, groups, chunks, pieces, dets, width = out_ref.shape
    places = []
    for plane, group, chunk, piece in np.ndindex(planes, groups, chunks, pieces):
        start = ((group * planes + plane) * chunks + chunk) * dets
        rows, lanes = slice(start, start + dets), slice(piece * width, (piece + 1) * width)
        places.append(((plane, group, chunk, piece), (rows, lanes)))
    for source, target in places:
        x_mid[target] = x_ref[source]
    x_high, x_low = split(x_mid[...])
    half = f_high.shape[0] // 2
    for part in range(2):
        rows, reach = slice(part * half, (part + 1) * half), (part + 1) * half
        y_mid[rows] = product((f_high[rows, :reach], f_low[rows, :reach]), (x_high[:reach], x_low[:reach]))
    for target, source in places:
        out_ref[target] = y_mid[source]


def call(kernel, outs, scratch, flops, *args, spaces=None, out_space=pltpu.VMEM, aliases=None):
    spaces = spaces or [pltpu.VMEM] * len(args)
    count = sum(math.prod(arg.shape) * arg.dtype.itemsize for arg in (*args, *outs))
    return pl.pallas_call(
        kernel,
        out_shape=outs,
        in_specs=[pl.BlockSpec(memory_space=space) for space in spaces],
        out_specs=[pl.BlockSpec(memory_space=out_space)] * len(outs),
        scratch_shapes=[pltpu.VMEM(item, jnp.float32) if isinstance(item, tuple) else item for item in scratch],
        compiler_params=pltpu.CompilerParams(vmem_limit_bytes=VMEM_LIMIT),
        cost_estimate=pl.CostEstimate(flops=flops, bytes_accessed=count, transcendentals=0),
        input_output_aliases=aliases or {},
    )(*args)


def array(*shape, dtype=jnp.float32):
    return jax.ShapeDtypeStruct(shape, dtype)


def dma(count):
    return pltpu.SemaphoreType.DMA((count,))


def swap(value, axis, mask):
    return lax.ppermute(value, axis, [(place, place ^ mask) for place in range(lax.axis_size(axis))])


def trade(parts):
    return [swap(parts[step], "tm", step) for step in reversed(range(1, len(parts)))] + [parts[0]]


def plane_factor(factor, planes, groups):
    half = factor.shape[1] // 2
    upper = lax.axis_index("det") >= groups // 2
    mine = lax.dynamic_slice_in_dim(factor[0], jnp.where(upper, half, 0), half, 0)
    plane_of = {band_of(plane, planes): plane for plane in range(planes)}
    pairs = []
    for plane in range(planes):
        for group in range(groups):
            target = plane_of[min(group, groups - 1 - group)]
            pairs.append((plane * groups + group, target * groups + 2 * plane + (group >= groups // 2)))
    middle = factor.shape[2] // 2
    low = lax.ppermute(mine[:, :middle], ("tm", "det"), pairs)
    high = lax.ppermute(mine[:, middle:], ("tm", "det"), [pair for pair in pairs if 2 * (pair[0] // groups) >= planes])
    return low, high


def band_factor(sides, groups):
    share = jnp.concatenate(sides, axis=1)
    rows, columns = share.shape
    share = jnp.stack([share] + [swap(share, "det", mask) for mask in range(2, groups, 2)])
    share = jnp.concatenate([share, swap(share, "det", 1)])
    whole = array(groups * rows, columns, dtype=jnp.bfloat16)
    return call(factor_kernel, [whole, whole], [], FACTOR_WORK, share)


def bind(kernel, *static):
    return lambda *refs: kernel(*static, *refs)


def local(noise, factor):
    planes = lax.axis_size("tm")
    groups = lax.axis_size("det")
    rows, span = noise.shape
    own = rows // planes
    n2 = LANES // 2 * planes
    n1 = span * planes // 2 // n2
    pieces = n1 // groups
    chunks = CHUNKS if own % (8 * CHUNKS) == 0 else 1
    dets = own // chunks
    flops = 3 * 2 * n1 * own * (2 * n2) ** 2
    tables = (twiddles(n1, n2), *fourier_matrix(n2, planes))

    parts = call(
        slice_kernel, [array(own, span)] * planes, [dma(planes)], 0, noise.reshape(planes, own, span), spaces=[pl.ANY],
        out_space=pl.ANY,
    )
    layout = (planes, groups, chunks, pieces, dets, LANES)

    def exchange(value):
        value = value.reshape(planes * groups, pieces * own, LANES)
        return lax.all_to_all(value, ("tm", "det"), split_axis=0, concat_axis=0, tiled=True).reshape(layout)

    (spectrum,) = call(
        bind(forward_kernel, n1, n2, planes), [array(*layout)],
        [(planes, own, span), (chunks, n1 * dets, 2 * n2), layout, dma(chunks)], flops, *trade(parts), *tables, out_space=pl.ANY,
    )
    sides = plane_factor(factor, planes, groups)
    f_high, f_low = band_factor(sides, groups)

    count = f_high.shape[0]
    (mixed,) = call(
        mix_kernel, [array(*layout)], [(count, pieces * LANES)] * 2,
        2 * 3 * count * count * pieces * LANES, exchange(spectrum), f_high, f_low,
    )
    back = exchange(mixed)
    result = []
    for chunk in range(chunks):
        parts = call(
            bind(inverse_kernel, n1, n2, chunk), [array(dets, span)] * planes,
            [(planes, dets, span), (n1 * dets, 2 * n2)], flops // chunks, back, *tables,
        )
        result = call(
            bind(place_kernel, chunk), [array(planes, chunks, dets, span)], [dma(planes)], 0, *trade(parts), *result,
            spaces=[pl.ANY] * (planes + len(result)), out_space=pl.ANY, aliases={planes: 0} if result else None,
        )
    return result[0].reshape(rows, span)


def solution(mesh):
    in_specs = (P("det", "tm"), P("det", "tm", None))
    return jax.shard_map(local, mesh=mesh, in_specs=in_specs, out_specs=P("det", "tm"), check_vma=False)
```

```python
import math

import jax
import jax.numpy as jnp
import ml_dtypes
import numpy as np
from jax import lax
from jax.experimental import pallas as pl
from jax.experimental.pallas import tpu as pltpu
from jax.sharding import PartitionSpec as P


LANES = 128
VMEM_LIMIT = 48 * 1024 * 1024
CHUNKS = 2
FACTOR_WORK = 7 * 10**9


def band_of(plane, planes):
    return 2 * plane if 2 * plane < planes else 2 * (planes - 1 - plane) + 1


def fourier_matrix(n2, planes):
    share = n2 // (2 * planes)
    order = []
    for plane in range(planes):
        low = band_of(plane, planes) * share + np.arange(share)
        order.append(np.concatenate([low, n2 - 1 - low[::-1]]))
    order = np.stack(order)
    angle = 2.0 * np.pi / n2 * (np.arange(n2)[:, None, None] * order[None] % n2)
    cosine, sine = np.cos(angle), np.sin(angle)
    matrix = np.stack([np.stack([cosine, -sine], 2), np.stack([sine, cosine], 2)])
    matrix = matrix.reshape(2 * n2, 2 * n2).astype(np.float32)
    high = matrix.astype(ml_dtypes.bfloat16)
    low = (matrix - high.astype(np.float32)).astype(ml_dtypes.bfloat16)
    return high, low


def twiddles(n1, n2):
    angle = 2.0 * np.pi / (n1 * n2) * (np.arange(n1)[:, None] + 0.25) * np.arange(n2)[None, :]
    return np.stack([np.cos(angle), np.sin(angle)]).astype(np.float32)


def forward_butterflies(parts, shift):
    count = len(parts)
    if count == 1:
        return parts
    half = count // 2
    turn_re, turn_im = math.cos(math.pi * shift), -math.sin(math.pi * shift)
    even, odd = [], []
    for (a_re, a_im), (b_re, b_im) in zip(parts[:half], parts[half:]):
        c_re = b_re * turn_re - b_im * turn_im
        c_im = b_re * turn_im + b_im * turn_re
        even.append((a_re + c_re, a_im + c_im))
        odd.append((a_re - c_re, a_im - c_im))
    even = forward_butterflies(even, shift / 2)
    odd = forward_butterflies(odd, (1 + shift) / 2)
    return [part for pair in zip(even, odd) for part in pair]


def inverse_butterflies(parts, shift):
    if len(parts) == 1:
        return parts
    turn_re, turn_im = math.cos(math.pi * shift), math.sin(math.pi * shift)
    even = inverse_butterflies(parts[0::2], shift / 2)
    odd = inverse_butterflies(parts[1::2], (1 + shift) / 2)
    first, second = [], []
    for (a_re, a_im), (b_re, b_im) in zip(even, odd):
        d_re, d_im = a_re - b_re, a_im - b_im
        first.append((a_re + b_re, a_im + b_im))
        second.append((d_re * turn_re - d_im * turn_im, d_re * turn_im + d_im * turn_re))
    return first + second


def split(value):
    high = value.astype(jnp.bfloat16)
    return high, (value - high.astype(jnp.float32)).astype(jnp.bfloat16)


def product(left, right, contract=((1,), (0,))):
    def dot(a, b):
        return lax.dot_general(a, b, (contract, ((), ())), preferred_element_type=jnp.float32)

    rows = left[0].shape[0]
    both = dot(jnp.concatenate(left), right[0])
    return both[:rows] + (both[rows:] + dot(left[0], right[1]))


def tiles(rows, lanes):
    step = min(8, rows)
    for row in range(0, rows, step):
        for lane in range(0, lanes, LANES):
            yield slice(row, row + step), lane


def slice_kernel(noise_ref, *refs):
    here = lax.axis_index("tm")
    outs, sem = refs[:-1], refs[-1]
    copies = [
        pltpu.make_async_copy(noise_ref.at[here ^ step], out, sem.at[step]) for step, out in enumerate(outs)
    ]
    for copy in copies:
        copy.start()
    for copy in copies:
        copy.wait()


def forward_kernel(n1, n2, planes, *refs):
    here = lax.axis_index("tm")
    blocks, (turn_ref, high_ref, low_ref) = refs[:planes], refs[planes : planes + 3]
    out_ref, x_ref, mid_ref, stage_ref, sem = refs[-5:]
    span = x_ref.shape[-1]
    _, groups, chunks, pieces, dets, width = stage_ref.shape
    per = span // n2
    for step, block in zip(farthest_first(planes), blocks):
        x_ref[here ^ step] = block[...]
    copies = []
    for chunk in range(chunks):
        for tile, lane in tiles(dets, n2):
            rows = slice(chunk * dets + tile.start, chunk * dets + tile.stop)

            def load(index):
                start = (index % per) * n2 + lane
                return x_ref[index // per, rows, start : start + LANES]

            parts = [(load(t1), -load(t1 + n1)) for t1 in range(n1)]
            for k1, (re, im) in enumerate(forward_butterflies(parts, 0.25)):
                cosine = turn_ref[0, k1 : k1 + 1, lane : lane + LANES]
                sine = turn_ref[1, k1 : k1 + 1, lane : lane + LANES]
                place = slice(k1 * dets + tile.start, k1 * dets + tile.stop)
                mid_ref[chunk, place, lane : lane + LANES] = re * cosine + im * sine
                mid_ref[chunk, place, n2 + lane : n2 + lane + LANES] = im * cosine - re * sine
        spectrum = product(split(mid_ref[chunk]), (high_ref[...], low_ref[...]))
        for plane in range(planes):
            value = spectrum[:, plane * width : (plane + 1) * width]
            stage_ref[plane, :, chunk] = value.reshape(groups, pieces, dets, width)
        copies.append(pltpu.make_async_copy(stage_ref.at[:, :, chunk], out_ref.at[:, :, chunk], sem.at[chunk]))
        copies[-1].start()
    for copy in copies:
        copy.wait()


def inverse_kernel(n1, n2, chunk, y_ref, turn_ref, high_ref, low_ref, *refs):
    here = lax.axis_index("tm")
    outs, (x_ref, mid_ref) = refs[:-2], refs[-2:]
    _, dets, span = x_ref.shape
    planes, _, _, _, _, width = y_ref.shape
    per = span // n2
    scale = 1.0 / (n1 * n2)
    bins = jnp.concatenate([y_ref[plane, :, chunk].reshape(n1 * dets, width) for plane in range(planes)], axis=1)
    mid_ref[...] = product(split(bins), (high_ref[...], low_ref[...]), ((1,), (1,)))
    for rows, lane in tiles(dets, n2):
        parts = []
        for k1 in range(n1):
            cosine = turn_ref[0, k1 : k1 + 1, lane : lane + LANES] * scale
            sine = turn_ref[1, k1 : k1 + 1, lane : lane + LANES] * scale
            place = slice(k1 * dets + rows.start, k1 * dets + rows.stop)
            re = mid_ref[place, lane : lane + LANES]
            im = mid_ref[place, n2 + lane : n2 + lane + LANES]
            parts.append((re * cosine - im * sine, im * cosine + re * sine))
        for t1, (re, im) in enumerate(inverse_butterflies(parts, 0.25)):
            for index, value in ((t1, re), (t1 + n1, -im)):
                start = (index % per) * n2 + lane
                x_ref[index // per, rows, start : start + LANES] = value
    for step, out in enumerate(outs):
        out[...] = x_ref[here ^ step]


def place_kernel(chunk, *refs):
    here = lax.axis_index("tm")
    out_ref, sem = refs[-2:]
    planes = out_ref.shape[0]
    copies = [
        pltpu.make_async_copy(block, out_ref.at[here ^ step, chunk], sem.at[step])
        for step, block in zip(half_first(planes), refs)
    ]
    for copy in copies:
        copy.start()
    for copy in copies:
        copy.wait()


def factor_kernel(factor_ref, high_ref, low_ref):
    here = lax.axis_index("det")
    shares, rows, _ = factor_ref.shape
    for share in range(shares):
        source = here ^ (2 * share if 2 * share < shares else 2 * share - shares + 1)
        place = pl.ds(pl.multiple_of(source * rows, rows), rows)
        high_ref[place], low_ref[place] = split(factor_ref[share])


def mix_kernel(x_ref, f_high, f_low, out_ref, x_mid, y_mid):
    planes, groups, chunks, pieces, dets, width = out_ref.shape
    places = []
    for plane, group, chunk, piece in np.ndindex(planes, groups, chunks, pieces):
        start = ((group * planes + plane) * chunks + chunk) * dets
        rows, lanes = slice(start, start + dets), slice(piece * width, (piece + 1) * width)
        places.append(((plane, group, chunk, piece), (rows, lanes)))
    for source, target in places:
        x_mid[target] = x_ref[source]
    x_high, x_low = split(x_mid[...])
    half = f_high.shape[0] // 2
    for part in range(2):
        rows, reach = slice(part * half, (part + 1) * half), (part + 1) * half
        y_mid[rows] = product((f_high[rows, :reach], f_low[rows, :reach]), (x_high[:reach], x_low[:reach]))
    for target, source in places:
        out_ref[target] = y_mid[source]


def call(kernel, outs, scratch, flops, *args, spaces=None, out_space=pltpu.VMEM, aliases=None):
    spaces = spaces or [pltpu.VMEM] * len(args)
    count = sum(math.prod(arg.shape) * arg.dtype.itemsize for arg in (*args, *outs))
    return pl.pallas_call(
        kernel,
        out_shape=outs,
        in_specs=[pl.BlockSpec(memory_space=space) for space in spaces],
        out_specs=[pl.BlockSpec(memory_space=out_space)] * len(outs),
        scratch_shapes=[pltpu.VMEM(item, jnp.float32) if isinstance(item, tuple) else item for item in scratch],
        compiler_params=pltpu.CompilerParams(vmem_limit_bytes=VMEM_LIMIT),
        cost_estimate=pl.CostEstimate(flops=flops, bytes_accessed=count, transcendentals=0),
        input_output_aliases=aliases or {},
    )(*args)


def array(*shape, dtype=jnp.float32):
    return jax.ShapeDtypeStruct(shape, dtype)


def dma(count):
    return pltpu.SemaphoreType.DMA((count,))


def swap(value, axis, mask):
    return lax.ppermute(value, axis, [(place, place ^ mask) for place in range(lax.axis_size(axis))])


def farthest_first(planes):
    return list(reversed(range(planes)))


def half_first(planes):
    return sorted(range(1, planes), key=lambda step: 2 * step != planes) + [0]


def trade(parts, order):
    return [swap(parts[step], "tm", step) if step else parts[step] for step in order(len(parts))]


def plane_factor(factor, planes, groups):
    half = factor.shape[1] // 2
    upper = lax.axis_index("det") >= groups // 2
    mine = lax.dynamic_slice_in_dim(factor[0], jnp.where(upper, half, 0), half, 0)
    plane_of = {band_of(plane, planes): plane for plane in range(planes)}
    pairs = []
    for plane in range(planes):
        for group in range(groups):
            target = plane_of[min(group, groups - 1 - group)]
            pairs.append((plane * groups + group, target * groups + 2 * plane + (group >= groups // 2)))
    middle = factor.shape[2] // 2
    low = lax.ppermute(mine[:, :middle], ("tm", "det"), pairs)
    high = lax.ppermute(mine[:, middle:], ("tm", "det"), [pair for pair in pairs if 2 * (pair[0] // groups) >= planes])
    return low, high


def band_factor(sides, groups):
    share = jnp.concatenate(sides, axis=1)
    rows, columns = share.shape
    share = jnp.stack([share] + [swap(share, "det", mask) for mask in range(2, groups, 2)])
    share = jnp.concatenate([share, swap(share, "det", 1)])
    whole = array(groups * rows, columns, dtype=jnp.bfloat16)
    return call(factor_kernel, [whole, whole], [], FACTOR_WORK, share)


def bind(kernel, *static):
    return lambda *refs: kernel(*static, *refs)


def local(noise, factor):
    planes = lax.axis_size("tm")
    groups = lax.axis_size("det")
    rows, span = noise.shape
    own = rows // planes
    n2 = LANES // 2 * planes
    n1 = span * planes // 2 // n2
    pieces = n1 // groups
    chunks = CHUNKS if own % (8 * CHUNKS) == 0 else 1
    dets = own // chunks
    flops = 3 * 2 * n1 * own * (2 * n2) ** 2
    tables = (twiddles(n1, n2), *fourier_matrix(n2, planes))

    parts = call(
        slice_kernel, [array(own, span)] * planes, [dma(planes)], 0, noise.reshape(planes, own, span), spaces=[pl.ANY],
        out_space=pl.ANY,
    )
    layout = (planes, groups, chunks, pieces, dets, LANES)

    def exchange(value):
        value = value.reshape(planes * groups, pieces * own, LANES)
        return lax.all_to_all(value, ("tm", "det"), split_axis=0, concat_axis=0, tiled=True).reshape(layout)

    (spectrum,) = call(
        bind(forward_kernel, n1, n2, planes), [array(*layout)],
        [(planes, own, span), (chunks, n1 * dets, 2 * n2), layout, dma(chunks)], flops, *trade(parts, farthest_first), *tables, out_space=pl.ANY,
    )
    sides = plane_factor(factor, planes, groups)
    f_high, f_low = band_factor(sides, groups)

    count = f_high.shape[0]
    (mixed,) = call(
        mix_kernel, [array(*layout)], [(count, pieces * LANES)] * 2,
        2 * 3 * count * count * pieces * LANES, exchange(spectrum), f_high, f_low,
    )
    back = exchange(mixed)
    result = []
    for chunk in range(chunks):
        parts = call(
            bind(inverse_kernel, n1, n2, chunk), [array(dets, span)] * planes,
            [(planes, dets, span), (n1 * dets, 2 * n2)], flops // chunks, back, *tables,
        )
        result = call(
            bind(place_kernel, chunk), [array(planes, chunks, dets, span)], [dma(planes)], 0, *trade(parts, half_first), *result,
            spaces=[pl.ANY] * (planes + len(result)), out_space=pl.ANY, aliases={planes: 0} if result else None,
        )
    return result[0].reshape(rows, span)


def solution(mesh):
    in_specs = (P("det", "tm"), P("det", "tm", None))
    return jax.shard_map(local, mesh=mesh, in_specs=in_specs, out_specs=P("det", "tm"), check_vma=False)
```

```python
import math

import jax
import jax.numpy as jnp
import ml_dtypes
import numpy as np
from jax import lax
from jax.experimental import pallas as pl
from jax.experimental.pallas import tpu as pltpu
from jax.sharding import PartitionSpec as P


LANES = 128
VMEM_LIMIT = 48 * 1024 * 1024
CHUNKS = 2
FACTOR_WORK = 74 * 10**8


def band_of(plane, planes):
    return 2 * plane if 2 * plane < planes else 2 * (planes - 1 - plane) + 1


def fourier_matrix(n2, planes):
    share = n2 // (2 * planes)
    order = []
    for plane in range(planes):
        low = band_of(plane, planes) * share + np.arange(share)
        order.append(np.concatenate([low, n2 - 1 - low[::-1]]))
    order = np.stack(order)
    angle = 2.0 * np.pi / n2 * (np.arange(n2)[:, None, None] * order[None] % n2)
    cosine, sine = np.cos(angle), np.sin(angle)
    matrix = np.stack([np.stack([cosine, -sine], 2), np.stack([sine, cosine], 2)])
    matrix = matrix.reshape(2 * n2, 2 * n2).astype(np.float32)
    high = matrix.astype(ml_dtypes.bfloat16)
    low = (matrix - high.astype(np.float32)).astype(ml_dtypes.bfloat16)
    return high, low


def twiddles(n1, n2):
    angle = 2.0 * np.pi / (n1 * n2) * (np.arange(n1)[:, None] + 0.25) * np.arange(n2)[None, :]
    return np.stack([np.cos(angle), np.sin(angle)]).astype(np.float32)


def forward_butterflies(parts, shift):
    count = len(parts)
    if count == 1:
        return parts
    half = count // 2
    turn_re, turn_im = math.cos(math.pi * shift), -math.sin(math.pi * shift)
    even, odd = [], []
    for (a_re, a_im), (b_re, b_im) in zip(parts[:half], parts[half:]):
        c_re = b_re * turn_re - b_im * turn_im
        c_im = b_re * turn_im + b_im * turn_re
        even.append((a_re + c_re, a_im + c_im))
        odd.append((a_re - c_re, a_im - c_im))
    even = forward_butterflies(even, shift / 2)
    odd = forward_butterflies(odd, (1 + shift) / 2)
    return [part for pair in zip(even, odd) for part in pair]


def inverse_butterflies(parts, shift):
    if len(parts) == 1:
        return parts
    turn_re, turn_im = math.cos(math.pi * shift), math.sin(math.pi * shift)
    even = inverse_butterflies(parts[0::2], shift / 2)
    odd = inverse_butterflies(parts[1::2], (1 + shift) / 2)
    first, second = [], []
    for (a_re, a_im), (b_re, b_im) in zip(even, odd):
        d_re, d_im = a_re - b_re, a_im - b_im
        first.append((a_re + b_re, a_im + b_im))
        second.append((d_re * turn_re - d_im * turn_im, d_re * turn_im + d_im * turn_re))
    return first + second


def split(value):
    high = value.astype(jnp.bfloat16)
    return high, (value - high.astype(jnp.float32)).astype(jnp.bfloat16)


def product(left, right, contract=((1,), (0,))):
    def dot(a, b):
        return lax.dot_general(a, b, (contract, ((), ())), preferred_element_type=jnp.float32)

    rows = left[0].shape[0]
    both = dot(jnp.concatenate(left), right[0])
    return both[:rows] + (both[rows:] + dot(left[0], right[1]))


def tiles(rows, lanes):
    step = min(8, rows)
    for row in range(0, rows, step):
        for lane in range(0, lanes, LANES):
            yield slice(row, row + step), lane


def slice_kernel(noise_ref, *refs):
    here = lax.axis_index("tm")
    outs, sem = refs[:-1], refs[-1]
    copies = [
        pltpu.make_async_copy(noise_ref.at[here ^ step], out, sem.at[step]) for step, out in enumerate(outs)
    ]
    for copy in copies:
        copy.start()
    for copy in copies:
        copy.wait()


def forward_kernel(n1, n2, planes, *refs):
    here = lax.axis_index("tm")
    blocks, (turn_ref, high_ref, low_ref) = refs[:planes], refs[planes : planes + 3]
    out_ref, x_ref, mid_ref, stage_ref, sem = refs[-5:]
    span = x_ref.shape[-1]
    groups, _, chunks, pieces, dets, width = stage_ref.shape
    per = span // n2
    for step, block in zip(farthest_first(planes), blocks):
        x_ref[here ^ step] = block[...]
    copies = []
    for chunk in range(chunks):
        for tile, lane in tiles(dets, n2):
            rows = slice(chunk * dets + tile.start, chunk * dets + tile.stop)

            def load(index):
                start = (index % per) * n2 + lane
                return x_ref[index // per, rows, start : start + LANES]

            parts = [(load(t1), -load(t1 + n1)) for t1 in range(n1)]
            for k1, (re, im) in enumerate(forward_butterflies(parts, 0.25)):
                cosine = turn_ref[0, k1 : k1 + 1, lane : lane + LANES]
                sine = turn_ref[1, k1 : k1 + 1, lane : lane + LANES]
                place = slice(k1 * dets + tile.start, k1 * dets + tile.stop)
                mid_ref[chunk, place, lane : lane + LANES] = re * cosine + im * sine
                mid_ref[chunk, place, n2 + lane : n2 + lane + LANES] = im * cosine - re * sine
        spectrum = product(split(mid_ref[chunk]), (high_ref[...], low_ref[...]))
        for plane in range(planes):
            value = spectrum[:, plane * width : (plane + 1) * width]
            stage_ref[:, plane, chunk] = value.reshape(groups, pieces, dets, width)
        copies.append(pltpu.make_async_copy(stage_ref.at[:, :, chunk], out_ref.at[:, :, chunk], sem.at[chunk]))
        copies[-1].start()
    for copy in copies:
        copy.wait()


def inverse_kernel(n1, n2, chunk, y_ref, turn_ref, high_ref, low_ref, *refs):
    here = lax.axis_index("tm")
    outs, (x_ref, mid_ref) = refs[:-2], refs[-2:]
    _, dets, span = x_ref.shape
    _, planes, _, _, _, width = y_ref.shape
    per = span // n2
    scale = 1.0 / (n1 * n2)
    bins = jnp.concatenate([y_ref[:, plane, chunk].reshape(n1 * dets, width) for plane in range(planes)], axis=1)
    mid_ref[...] = product(split(bins), (high_ref[...], low_ref[...]), ((1,), (1,)))
    for rows, lane in tiles(dets, n2):
        parts = []
        for k1 in range(n1):
            cosine = turn_ref[0, k1 : k1 + 1, lane : lane + LANES] * scale
            sine = turn_ref[1, k1 : k1 + 1, lane : lane + LANES] * scale
            place = slice(k1 * dets + rows.start, k1 * dets + rows.stop)
            re = mid_ref[place, lane : lane + LANES]
            im = mid_ref[place, n2 + lane : n2 + lane + LANES]
            parts.append((re * cosine - im * sine, im * cosine + re * sine))
        for t1, (re, im) in enumerate(inverse_butterflies(parts, 0.25)):
            for index, value in ((t1, re), (t1 + n1, -im)):
                start = (index % per) * n2 + lane
                x_ref[index // per, rows, start : start + LANES] = value
    for step, out in enumerate(outs):
        out[...] = x_ref[here ^ step]


def place_kernel(chunk, *refs):
    here = lax.axis_index("tm")
    out_ref, sem = refs[-2:]
    planes = out_ref.shape[0]
    copies = [
        pltpu.make_async_copy(block, out_ref.at[here ^ step, chunk], sem.at[step])
        for step, block in zip(half_first(planes), refs)
    ]
    for copy in copies:
        copy.start()
    for copy in copies:
        copy.wait()


def factor_kernel(factor_ref, high_ref, low_ref):
    here = lax.axis_index("det")
    shares, rows, _ = factor_ref.shape
    for share in range(shares):
        source = here ^ (2 * share if 2 * share < shares else 2 * share - shares + 1)
        place = pl.ds(pl.multiple_of(source * rows, rows), rows)
        high_ref[place], low_ref[place] = split(factor_ref[share])


def mix_kernel(x_ref, f_high, f_low, out_ref, x_mid, y_mid):
    groups, planes, chunks, pieces, dets, width = out_ref.shape
    places = []
    for group, plane, chunk, piece in np.ndindex(groups, planes, chunks, pieces):
        start = ((group * planes + plane) * chunks + chunk) * dets
        rows, lanes = slice(start, start + dets), slice(piece * width, (piece + 1) * width)
        places.append(((group, plane, chunk, piece), (rows, lanes)))
    for source, target in places:
        x_mid[target] = x_ref[source]
    x_high, x_low = split(x_mid[...])
    half = f_high.shape[0] // 2
    for part in range(2):
        rows, reach = slice(part * half, (part + 1) * half), (part + 1) * half
        y_mid[rows] = product((f_high[rows, :reach], f_low[rows, :reach]), (x_high[:reach], x_low[:reach]))
    for target, source in places:
        out_ref[target] = y_mid[source]


def call(kernel, outs, scratch, flops, *args, spaces=None, out_space=pltpu.VMEM, aliases=None):
    spaces = spaces or [pltpu.VMEM] * len(args)
    count = sum(math.prod(arg.shape) * arg.dtype.itemsize for arg in (*args, *outs))
    return pl.pallas_call(
        kernel,
        out_shape=outs,
        in_specs=[pl.BlockSpec(memory_space=space) for space in spaces],
        out_specs=[pl.BlockSpec(memory_space=out_space)] * len(outs),
        scratch_shapes=[pltpu.VMEM(item, jnp.float32) if isinstance(item, tuple) else item for item in scratch],
        compiler_params=pltpu.CompilerParams(vmem_limit_bytes=VMEM_LIMIT),
        cost_estimate=pl.CostEstimate(flops=flops, bytes_accessed=count, transcendentals=0),
        input_output_aliases=aliases or {},
    )(*args)


def array(*shape, dtype=jnp.float32):
    return jax.ShapeDtypeStruct(shape, dtype)


def dma(count):
    return pltpu.SemaphoreType.DMA((count,))


def swap(value, axis, mask):
    return lax.ppermute(value, axis, [(place, place ^ mask) for place in range(lax.axis_size(axis))])


def farthest_first(planes):
    return list(reversed(range(planes)))


def half_first(planes):
    return sorted(range(1, planes), key=lambda step: 2 * step != planes) + [0]


def trade(parts, order):
    return [swap(parts[step], "tm", step) if step else parts[step] for step in order(len(parts))]


def plane_factor(factor, planes, groups):
    half = factor.shape[1] // 2
    upper = lax.axis_index("det") >= groups // 2
    mine = lax.dynamic_slice_in_dim(factor[0], jnp.where(upper, half, 0), half, 0)
    plane_of = {band_of(plane, planes): plane for plane in range(planes)}
    pairs = []
    for plane in range(planes):
        for group in range(groups):
            target = plane_of[min(group, groups - 1 - group)]
            pairs.append((plane * groups + group, target * groups + 2 * plane + (group >= groups // 2)))
    middle = factor.shape[2] // 2
    low = lax.ppermute(mine[:, :middle], ("tm", "det"), pairs)
    high = lax.ppermute(mine[:, middle:], ("tm", "det"), [pair for pair in pairs if 2 * (pair[0] // groups) >= planes])
    return low, high


def band_factor(sides, groups):
    share = jnp.concatenate(sides, axis=1)
    rows, columns = share.shape
    share = jnp.stack([share] + [swap(share, "det", mask) for mask in range(2, groups, 2)])
    share = jnp.concatenate([share, swap(share, "det", 1)])
    whole = array(groups * rows, columns, dtype=jnp.bfloat16)
    return call(factor_kernel, [whole, whole], [], FACTOR_WORK, share)


def bind(kernel, *static):
    return lambda *refs: kernel(*static, *refs)


def local(noise, factor):
    planes = lax.axis_size("tm")
    groups = lax.axis_size("det")
    rows, span = noise.shape
    own = rows // planes
    n2 = LANES // 2 * planes
    n1 = span * planes // 2 // n2
    pieces = n1 // groups
    chunks = CHUNKS if own % (8 * CHUNKS) == 0 else 1
    dets = own // chunks
    flops = 3 * 2 * n1 * own * (2 * n2) ** 2
    tables = (twiddles(n1, n2), *fourier_matrix(n2, planes))

    parts = call(
        slice_kernel, [array(own, span)] * planes, [dma(planes)], 0, noise.reshape(planes, own, span), spaces=[pl.ANY],
        out_space=pl.ANY,
    )
    layout = (groups, planes, chunks, pieces, dets, LANES)

    def exchange(value):
        value = value.reshape(groups * planes, pieces * own, LANES)
        return lax.all_to_all(value, ("det", "tm"), split_axis=0, concat_axis=0, tiled=True).reshape(layout)

    (spectrum,) = call(
        bind(forward_kernel, n1, n2, planes), [array(*layout)],
        [(planes, own, span), (chunks, n1 * dets, 2 * n2), layout, dma(chunks)], flops, *trade(parts, farthest_first), *tables, out_space=pl.ANY,
    )
    sides = plane_factor(factor, planes, groups)
    f_high, f_low = band_factor(sides, groups)

    count = f_high.shape[0]
    (mixed,) = call(
        mix_kernel, [array(*layout)], [(count, pieces * LANES)] * 2,
        2 * 3 * count * count * pieces * LANES, exchange(spectrum), f_high, f_low,
    )
    back = exchange(mixed)
    result = []
    for chunk in range(chunks):
        parts = call(
            bind(inverse_kernel, n1, n2, chunk), [array(dets, span)] * planes,
            [(planes, dets, span), (n1 * dets, 2 * n2)], flops // chunks, back, *tables,
        )
        result = call(
            bind(place_kernel, chunk), [array(planes, chunks, dets, span)], [dma(planes)], 0, *trade(parts, half_first), *result,
            spaces=[pl.ANY] * (planes + len(result)), out_space=pl.ANY, aliases={planes: 0} if result else None,
        )
    return result[0].reshape(rows, span)


def solution(mesh):
    in_specs = (P("det", "tm"), P("det", "tm", None))
    return jax.shard_map(local, mesh=mesh, in_specs=in_specs, out_specs=P("det", "tm"), check_vma=False)
```

```python
import math

import jax
import jax.numpy as jnp
import ml_dtypes
import numpy as np
from jax import lax
from jax.experimental import pallas as pl
from jax.experimental.pallas import tpu as pltpu
from jax.sharding import PartitionSpec as P


LANES = 128
VMEM_LIMIT = 48 * 1024 * 1024
CHUNKS = 2
FACTOR_WORK = 74 * 10**8


def band_of(plane, planes):
    return 2 * plane if 2 * plane < planes else 2 * (planes - 1 - plane) + 1


def fourier_matrix(n2, planes):
    share = n2 // (2 * planes)
    order = []
    for plane in range(planes):
        low = band_of(plane, planes) * share + np.arange(share)
        order.append(np.concatenate([low, n2 - 1 - low[::-1]]))
    order = np.stack(order)
    angle = 2.0 * np.pi / n2 * (np.arange(n2)[:, None, None] * order[None] % n2)
    cosine, sine = np.cos(angle), np.sin(angle)
    matrix = np.stack([np.stack([cosine, -sine], 2), np.stack([sine, cosine], 2)])
    matrix = matrix.reshape(2 * n2, 2 * n2).astype(np.float32)
    high = matrix.astype(ml_dtypes.bfloat16)
    low = (matrix - high.astype(np.float32)).astype(ml_dtypes.bfloat16)
    return high, low


def twiddles(n1, n2):
    angle = 2.0 * np.pi / (n1 * n2) * (np.arange(n1)[:, None] + 0.25) * np.arange(n2)[None, :]
    return np.stack([np.cos(angle), np.sin(angle)]).astype(np.float32)


def forward_butterflies(parts, shift):
    count = len(parts)
    if count == 1:
        return parts
    half = count // 2
    turn_re, turn_im = math.cos(math.pi * shift), -math.sin(math.pi * shift)
    even, odd = [], []
    for (a_re, a_im), (b_re, b_im) in zip(parts[:half], parts[half:]):
        c_re = b_re * turn_re - b_im * turn_im
        c_im = b_re * turn_im + b_im * turn_re
        even.append((a_re + c_re, a_im + c_im))
        odd.append((a_re - c_re, a_im - c_im))
    even = forward_butterflies(even, shift / 2)
    odd = forward_butterflies(odd, (1 + shift) / 2)
    return [part for pair in zip(even, odd) for part in pair]


def inverse_butterflies(parts, shift):
    if len(parts) == 1:
        return parts
    turn_re, turn_im = math.cos(math.pi * shift), math.sin(math.pi * shift)
    even = inverse_butterflies(parts[0::2], shift / 2)
    odd = inverse_butterflies(parts[1::2], (1 + shift) / 2)
    first, second = [], []
    for (a_re, a_im), (b_re, b_im) in zip(even, odd):
        d_re, d_im = a_re - b_re, a_im - b_im
        first.append((a_re + b_re, a_im + b_im))
        second.append((d_re * turn_re - d_im * turn_im, d_re * turn_im + d_im * turn_re))
    return first + second


def split(value):
    high = value.astype(jnp.bfloat16)
    return high, (value - high.astype(jnp.float32)).astype(jnp.bfloat16)


def product(left, right, contract=((1,), (0,))):
    def dot(a, b):
        return lax.dot_general(a, b, (contract, ((), ())), preferred_element_type=jnp.float32)

    rows = left[0].shape[0]
    both = dot(jnp.concatenate(left), right[0])
    return both[:rows] + (both[rows:] + dot(left[0], right[1]))


def tiles(rows, lanes):
    step = min(8, rows)
    for row in range(0, rows, step):
        for lane in range(0, lanes, LANES):
            yield slice(row, row + step), lane


def slice_kernel(noise_ref, *refs):
    here = lax.axis_index("tm")
    outs, sem = refs[:-1], refs[-1]
    copies = [
        pltpu.make_async_copy(noise_ref.at[here ^ step], out, sem.at[step]) for step, out in enumerate(outs)
    ]
    for copy in copies:
        copy.start()
    for copy in copies:
        copy.wait()


def forward_kernel(n1, n2, planes, *refs):
    here = lax.axis_index("tm")
    blocks, (turn_ref, high_ref, low_ref) = refs[:planes], refs[planes : planes + 3]
    out_ref, x_ref, mid_ref, stage_ref, sem = refs[-5:]
    span = x_ref.shape[-1]
    groups, _, chunks, pieces, dets, width = stage_ref.shape
    per = span // n2
    for step, block in zip(farthest_first(planes), blocks):
        x_ref[here ^ step] = block[...]
    copies = []
    for chunk in range(chunks):
        for tile, lane in tiles(dets, n2):
            rows = slice(chunk * dets + tile.start, chunk * dets + tile.stop)

            def load(index):
                start = (index % per) * n2 + lane
                return x_ref[index // per, rows, start : start + LANES]

            parts = [(load(t1), -load(t1 + n1)) for t1 in range(n1)]
            for k1, (re, im) in enumerate(forward_butterflies(parts, 0.25)):
                cosine = turn_ref[0, k1 : k1 + 1, lane : lane + LANES]
                sine = turn_ref[1, k1 : k1 + 1, lane : lane + LANES]
                place = slice(k1 * dets + tile.start, k1 * dets + tile.stop)
                mid_ref[chunk, place, lane : lane + LANES] = re * cosine + im * sine
                mid_ref[chunk, place, n2 + lane : n2 + lane + LANES] = im * cosine - re * sine
        spectrum = product(split(mid_ref[chunk]), (high_ref[...], low_ref[...]))
        for plane in range(planes):
            value = spectrum[:, plane * width : (plane + 1) * width]
            stage_ref[:, plane, chunk] = value.reshape(groups, pieces, dets, width)
        copies.append(pltpu.make_async_copy(stage_ref.at[:, :, chunk], out_ref.at[:, :, chunk], sem.at[chunk]))
        copies[-1].start()
    for copy in copies:
        copy.wait()


def inverse_kernel(n1, n2, chunk, y_ref, turn_ref, high_ref, low_ref, *refs):
    here = lax.axis_index("tm")
    outs, (x_ref, mid_ref) = refs[:-2], refs[-2:]
    _, dets, span = x_ref.shape
    _, planes, _, _, _, width = y_ref.shape
    per = span // n2
    scale = 1.0 / (n1 * n2)
    bins = jnp.concatenate([y_ref[:, plane, chunk].reshape(n1 * dets, width) for plane in range(planes)], axis=1)
    mid_ref[...] = product(split(bins), (high_ref[...], low_ref[...]), ((1,), (1,)))
    for rows, lane in tiles(dets, n2):
        parts = []
        for k1 in range(n1):
            cosine = turn_ref[0, k1 : k1 + 1, lane : lane + LANES] * scale
            sine = turn_ref[1, k1 : k1 + 1, lane : lane + LANES] * scale
            place = slice(k1 * dets + rows.start, k1 * dets + rows.stop)
            re = mid_ref[place, lane : lane + LANES]
            im = mid_ref[place, n2 + lane : n2 + lane + LANES]
            parts.append((re * cosine - im * sine, im * cosine + re * sine))
        for t1, (re, im) in enumerate(inverse_butterflies(parts, 0.25)):
            for index, value in ((t1, re), (t1 + n1, -im)):
                start = (index % per) * n2 + lane
                x_ref[index // per, rows, start : start + LANES] = value
    for step, out in enumerate(outs):
        out[...] = x_ref[here ^ step]


def place_kernel(spots, *refs):
    here = lax.axis_index("tm")
    out_ref, sem = refs[-2:]
    copies = [
        pltpu.make_async_copy(block, out_ref.at[here ^ step, chunk], sem.at[at])
        for at, ((chunk, step), block) in enumerate(zip(spots, refs))
    ]
    for copy in copies:
        copy.start()
    for copy in copies:
        copy.wait()


def factor_kernel(factor_ref, high_ref, low_ref):
    here = lax.axis_index("det")
    shares, rows, _ = factor_ref.shape
    for share in range(shares):
        source = here ^ (2 * share if 2 * share < shares else 2 * share - shares + 1)
        place = pl.ds(pl.multiple_of(source * rows, rows), rows)
        high_ref[place], low_ref[place] = split(factor_ref[share])


def mix_kernel(x_ref, f_high, f_low, out_ref, x_mid, y_mid):
    groups, planes, chunks, pieces, dets, width = out_ref.shape
    places = []
    for group, plane, chunk, piece in np.ndindex(groups, planes, chunks, pieces):
        start = ((group * planes + plane) * chunks + chunk) * dets
        rows, lanes = slice(start, start + dets), slice(piece * width, (piece + 1) * width)
        places.append(((group, plane, chunk, piece), (rows, lanes)))
    for source, target in places:
        x_mid[target] = x_ref[source]
    x_high, x_low = split(x_mid[...])
    half = f_high.shape[0] // 2
    for part in range(2):
        rows, reach = slice(part * half, (part + 1) * half), (part + 1) * half
        y_mid[rows] = product((f_high[rows, :reach], f_low[rows, :reach]), (x_high[:reach], x_low[:reach]))
    for target, source in places:
        out_ref[target] = y_mid[source]


def call(kernel, outs, scratch, flops, *args, spaces=None, out_space=pltpu.VMEM, aliases=None):
    spaces = spaces or [pltpu.VMEM] * len(args)
    count = sum(math.prod(arg.shape) * arg.dtype.itemsize for arg in (*args, *outs))
    return pl.pallas_call(
        kernel,
        out_shape=outs,
        in_specs=[pl.BlockSpec(memory_space=space) for space in spaces],
        out_specs=[pl.BlockSpec(memory_space=out_space)] * len(outs),
        scratch_shapes=[pltpu.VMEM(item, jnp.float32) if isinstance(item, tuple) else item for item in scratch],
        compiler_params=pltpu.CompilerParams(vmem_limit_bytes=VMEM_LIMIT),
        cost_estimate=pl.CostEstimate(flops=flops, bytes_accessed=count, transcendentals=0),
        input_output_aliases=aliases or {},
    )(*args)


def array(*shape, dtype=jnp.float32):
    return jax.ShapeDtypeStruct(shape, dtype)


def dma(count):
    return pltpu.SemaphoreType.DMA((count,))


def swap(value, axis, mask):
    return lax.ppermute(value, axis, [(place, place ^ mask) for place in range(lax.axis_size(axis))])


def farthest_first(planes):
    return list(reversed(range(planes)))


def half_first(planes):
    return sorted(range(1, planes), key=lambda step: 2 * step != planes) + [0]


def trade(parts, order):
    return [swap(parts[step], "tm", step) if step else parts[step] for step in order(len(parts))]


def plane_factor(factor, planes, groups):
    half = factor.shape[1] // 2
    upper = lax.axis_index("det") >= groups // 2
    mine = lax.dynamic_slice_in_dim(factor[0], jnp.where(upper, half, 0), half, 0)
    plane_of = {band_of(plane, planes): plane for plane in range(planes)}
    pairs = []
    for plane in range(planes):
        for group in range(groups):
            target = plane_of[min(group, groups - 1 - group)]
            pairs.append((plane * groups + group, target * groups + 2 * plane + (group >= groups // 2)))
    middle = factor.shape[2] // 2
    low = lax.ppermute(mine[:, :middle], ("tm", "det"), pairs)
    high = lax.ppermute(mine[:, middle:], ("tm", "det"), [pair for pair in pairs if 2 * (pair[0] // groups) >= planes])
    return low, high


def band_factor(sides, groups):
    share = jnp.concatenate(sides, axis=1)
    rows, columns = share.shape
    share = jnp.stack([share] + [swap(share, "det", mask) for mask in range(2, groups, 2)])
    share = jnp.concatenate([share, swap(share, "det", 1)])
    whole = array(groups * rows, columns, dtype=jnp.bfloat16)
    return call(factor_kernel, [whole, whole], [], FACTOR_WORK, share)


def bind(kernel, *static):
    return lambda *refs: kernel(*static, *refs)


def local(noise, factor):
    planes = lax.axis_size("tm")
    groups = lax.axis_size("det")
    rows, span = noise.shape
    own = rows // planes
    n2 = LANES // 2 * planes
    n1 = span * planes // 2 // n2
    pieces = n1 // groups
    chunks = CHUNKS if own % (8 * CHUNKS) == 0 else 1
    dets = own // chunks
    flops = 3 * 2 * n1 * own * (2 * n2) ** 2
    tables = (twiddles(n1, n2), *fourier_matrix(n2, planes))

    parts = call(
        slice_kernel, [array(own, span)] * planes, [dma(planes)], 0, noise.reshape(planes, own, span), spaces=[pl.ANY],
        out_space=pl.ANY,
    )
    layout = (groups, planes, chunks, pieces, dets, LANES)

    def exchange(value):
        value = value.reshape(groups * planes, pieces * own, LANES)
        return lax.all_to_all(value, ("det", "tm"), split_axis=0, concat_axis=0, tiled=True).reshape(layout)

    (spectrum,) = call(
        bind(forward_kernel, n1, n2, planes), [array(*layout)],
        [(planes, own, span), (chunks, n1 * dets, 2 * n2), layout, dma(chunks)], flops, *trade(parts, farthest_first), *tables, out_space=pl.ANY,
    )
    sides = plane_factor(factor, planes, groups)
    f_high, f_low = band_factor(sides, groups)

    count = f_high.shape[0]
    (mixed,) = call(
        mix_kernel, [array(*layout)], [(count, pieces * LANES)] * 2,
        2 * 3 * count * count * pieces * LANES, exchange(spectrum), f_high, f_low,
    )
    back = exchange(mixed)
    arrived = [
        trade(
            call(
                bind(inverse_kernel, n1, n2, chunk), [array(dets, span)] * planes,
                [(planes, dets, span), (n1 * dets, 2 * n2)], flops // chunks, back, *tables,
            ),
            half_first,
        )
        for chunk in range(chunks)
    ]
    places = [[(chunk, step) for step in half_first(planes)] for chunk in range(chunks)]
    if chunks > 1:
        places[0].append(places[-1].pop())
        arrived[0].append(arrived[-1].pop())
    result = []
    for blocks, spots in zip(arrived, places):
        count = len(blocks)
        result = call(
            bind(place_kernel, spots), [array(planes, chunks, dets, span)], [dma(count)], 0, *blocks, *result,
            spaces=[pl.ANY] * (count + len(result)), out_space=pl.ANY, aliases={count: 0} if result else None,
        )
    return result[0].reshape(rows, span)


def solution(mesh):
    in_specs = (P("det", "tm"), P("det", "tm", None))
    return jax.shard_map(local, mesh=mesh, in_specs=in_specs, out_specs=P("det", "tm"), check_vma=False)
```

```python
import math

import jax
import jax.numpy as jnp
import ml_dtypes
import numpy as np
from jax import lax
from jax.experimental import pallas as pl
from jax.experimental.pallas import tpu as pltpu
from jax.sharding import PartitionSpec as P


LANES = 128
VMEM_LIMIT = 48 * 1024 * 1024
CHUNKS = 2
FACTOR_WORK = 74 * 10**8


def band_of(plane, planes):
    return 2 * plane if 2 * plane < planes else 2 * (planes - 1 - plane) + 1


def fourier_matrix(n2, planes):
    share = n2 // (2 * planes)
    order = []
    for plane in range(planes):
        low = band_of(plane, planes) * share + np.arange(share)
        order.append(np.concatenate([low, n2 - 1 - low[::-1]]))
    order = np.stack(order)
    angle = 2.0 * np.pi / n2 * (np.arange(n2)[:, None, None] * order[None] % n2)
    cosine, sine = np.cos(angle), np.sin(angle)
    matrix = np.stack([np.stack([cosine, -sine], 2), np.stack([sine, cosine], 2)])
    matrix = matrix.reshape(2 * n2, 2 * n2).astype(np.float32)
    high = matrix.astype(ml_dtypes.bfloat16)
    low = (matrix - high.astype(np.float32)).astype(ml_dtypes.bfloat16)
    return high, low


def twiddles(n1, n2):
    angle = 2.0 * np.pi / (n1 * n2) * (np.arange(n1)[:, None] + 0.25) * np.arange(n2)[None, :]
    return np.stack([np.cos(angle), np.sin(angle)]).astype(np.float32)


def forward_butterflies(parts, shift):
    count = len(parts)
    if count == 1:
        return parts
    half = count // 2
    turn_re, turn_im = math.cos(math.pi * shift), -math.sin(math.pi * shift)
    even, odd = [], []
    for (a_re, a_im), (b_re, b_im) in zip(parts[:half], parts[half:]):
        c_re = b_re * turn_re - b_im * turn_im
        c_im = b_re * turn_im + b_im * turn_re
        even.append((a_re + c_re, a_im + c_im))
        odd.append((a_re - c_re, a_im - c_im))
    even = forward_butterflies(even, shift / 2)
    odd = forward_butterflies(odd, (1 + shift) / 2)
    return [part for pair in zip(even, odd) for part in pair]


def inverse_butterflies(parts, shift):
    if len(parts) == 1:
        return parts
    turn_re, turn_im = math.cos(math.pi * shift), math.sin(math.pi * shift)
    even = inverse_butterflies(parts[0::2], shift / 2)
    odd = inverse_butterflies(parts[1::2], (1 + shift) / 2)
    first, second = [], []
    for (a_re, a_im), (b_re, b_im) in zip(even, odd):
        d_re, d_im = a_re - b_re, a_im - b_im
        first.append((a_re + b_re, a_im + b_im))
        second.append((d_re * turn_re - d_im * turn_im, d_re * turn_im + d_im * turn_re))
    return first + second


def split(value):
    high = value.astype(jnp.bfloat16)
    return high, (value - high.astype(jnp.float32)).astype(jnp.bfloat16)


def product(left, right, contract=((1,), (0,))):
    def dot(a, b):
        return lax.dot_general(a, b, (contract, ((), ())), preferred_element_type=jnp.float32)

    rows = left[0].shape[0]
    both = dot(jnp.concatenate(left), right[0])
    return both[:rows] + (both[rows:] + dot(left[0], right[1]))


def tiles(rows, lanes):
    step = min(8, rows)
    for row in range(0, rows, step):
        for lane in range(0, lanes, LANES):
            yield slice(row, row + step), lane


def slice_kernel(noise_ref, *refs):
    here = lax.axis_index("tm")
    outs, sem = refs[:-1], refs[-1]
    copies = [
        pltpu.make_async_copy(noise_ref.at[here ^ step], out, sem.at[step]) for step, out in enumerate(outs)
    ]
    for copy in copies:
        copy.start()
    for copy in copies:
        copy.wait()


def forward_kernel(n1, n2, planes, *refs):
    here = lax.axis_index("tm")
    blocks, (turn_ref, high_ref, low_ref) = refs[:planes], refs[planes : planes + 3]
    out_ref, x_ref, mid_ref, stage_ref, sem = refs[-5:]
    span = x_ref.shape[-1]
    groups, _, chunks, pieces, dets, width = stage_ref.shape
    per = span // n2
    for step, block in zip(farthest_first(planes), blocks):
        x_ref[here ^ step] = block[...]
    copies = []
    for chunk in range(chunks):
        for tile, lane in tiles(dets, n2):
            rows = slice(chunk * dets + tile.start, chunk * dets + tile.stop)

            def load(index):
                start = (index % per) * n2 + lane
                return x_ref[index // per, rows, start : start + LANES]

            parts = [(load(t1), -load(t1 + n1)) for t1 in range(n1)]
            for k1, (re, im) in enumerate(forward_butterflies(parts, 0.25)):
                cosine = turn_ref[0, k1 : k1 + 1, lane : lane + LANES]
                sine = turn_ref[1, k1 : k1 + 1, lane : lane + LANES]
                place = slice(k1 * dets + tile.start, k1 * dets + tile.stop)
                mid_ref[chunk, place, lane : lane + LANES] = re * cosine + im * sine
                mid_ref[chunk, place, n2 + lane : n2 + lane + LANES] = im * cosine - re * sine
        spectrum = product(split(mid_ref[chunk]), (high_ref[...], low_ref[...]))
        for plane in range(planes):
            value = spectrum[:, plane * width : (plane + 1) * width]
            stage_ref[:, plane, chunk] = value.reshape(groups, pieces, dets, width)
        copies.append(pltpu.make_async_copy(stage_ref.at[:, :, chunk], out_ref.at[:, :, chunk], sem.at[chunk]))
        copies[-1].start()
    for copy in copies:
        copy.wait()


def inverse_kernel(n1, n2, chunk, y_ref, turn_ref, high_ref, low_ref, *refs):
    here = lax.axis_index("tm")
    outs, (x_ref, mid_ref) = refs[:-2], refs[-2:]
    _, dets, span = x_ref.shape
    _, planes, _, _, _, width = y_ref.shape
    per = span // n2
    scale = 1.0 / (n1 * n2)
    bins = jnp.concatenate([y_ref[:, plane, chunk].reshape(n1 * dets, width) for plane in range(planes)], axis=1)
    mid_ref[...] = product(split(bins), (high_ref[...], low_ref[...]), ((1,), (1,)))
    for rows, lane in tiles(dets, n2):
        parts = []
        for k1 in range(n1):
            cosine = turn_ref[0, k1 : k1 + 1, lane : lane + LANES] * scale
            sine = turn_ref[1, k1 : k1 + 1, lane : lane + LANES] * scale
            place = slice(k1 * dets + rows.start, k1 * dets + rows.stop)
            re = mid_ref[place, lane : lane + LANES]
            im = mid_ref[place, n2 + lane : n2 + lane + LANES]
            parts.append((re * cosine - im * sine, im * cosine + re * sine))
        for t1, (re, im) in enumerate(inverse_butterflies(parts, 0.25)):
            for index, value in ((t1, re), (t1 + n1, -im)):
                start = (index % per) * n2 + lane
                x_ref[index // per, rows, start : start + LANES] = value
    for step, out in enumerate(outs):
        out[...] = x_ref[here ^ step]


def place_kernel(chunk, *refs):
    here = lax.axis_index("tm")
    out_ref, sem = refs[-2:]
    planes = out_ref.shape[0]
    copies = [
        pltpu.make_async_copy(block, out_ref.at[here ^ step, chunk], sem.at[step])
        for step, block in zip(half_first(planes), refs)
    ]
    for copy in copies:
        copy.start()
    for copy in copies:
        copy.wait()


def factor_kernel(factor_ref, high_ref, low_ref):
    here = lax.axis_index("det")
    shares, rows, _ = factor_ref.shape
    for share in range(shares):
        source = here ^ (2 * share if 2 * share < shares else 2 * share - shares + 1)
        place = pl.ds(pl.multiple_of(source * rows, rows), rows)
        high_ref[place], low_ref[place] = split(factor_ref[share])


def mix_kernel(x_ref, f_high, f_low, out_ref, x_mid):
    groups, planes, chunks, pieces, dets, width = out_ref.shape
    places = []
    for group, plane, chunk, piece in np.ndindex(groups, planes, chunks, pieces):
        start = ((group * planes + plane) * chunks + chunk) * dets
        rows, lanes = slice(start, start + dets), slice(piece * width, (piece + 1) * width)
        places.append(((group, plane, chunk, piece), (rows, lanes)))
    for source, target in places:
        x_mid[target] = x_ref[source]
    x_high, x_low = split(x_mid[...])
    half = f_high.shape[0] // 2
    for part in range(2):
        rows, reach = slice(part * half, (part + 1) * half), (part + 1) * half
        value = product((f_high[rows, :reach], f_low[rows, :reach]), (x_high[:reach], x_low[:reach]))
        for target, (place, lanes) in places:
            if place.start // half == part:
                out_ref[target] = value[place.start - part * half : place.stop - part * half, lanes]


def call(kernel, outs, scratch, flops, *args, spaces=None, out_space=pltpu.VMEM, aliases=None):
    spaces = spaces or [pltpu.VMEM] * len(args)
    count = sum(math.prod(arg.shape) * arg.dtype.itemsize for arg in (*args, *outs))
    return pl.pallas_call(
        kernel,
        out_shape=outs,
        in_specs=[pl.BlockSpec(memory_space=space) for space in spaces],
        out_specs=[pl.BlockSpec(memory_space=out_space)] * len(outs),
        scratch_shapes=[pltpu.VMEM(item, jnp.float32) if isinstance(item, tuple) else item for item in scratch],
        compiler_params=pltpu.CompilerParams(vmem_limit_bytes=VMEM_LIMIT),
        cost_estimate=pl.CostEstimate(flops=flops, bytes_accessed=count, transcendentals=0),
        input_output_aliases=aliases or {},
    )(*args)


def array(*shape, dtype=jnp.float32):
    return jax.ShapeDtypeStruct(shape, dtype)


def dma(count):
    return pltpu.SemaphoreType.DMA((count,))


def swap(value, axis, mask):
    return lax.ppermute(value, axis, [(place, place ^ mask) for place in range(lax.axis_size(axis))])


def farthest_first(planes):
    return list(reversed(range(planes)))


def half_first(planes):
    return sorted(range(1, planes), key=lambda step: 2 * step != planes) + [0]


def trade(parts, order):
    return [swap(parts[step], "tm", step) if step else parts[step] for step in order(len(parts))]


def plane_factor(factor, planes, groups):
    half = factor.shape[1] // 2
    upper = lax.axis_index("det") >= groups // 2
    mine = lax.dynamic_slice_in_dim(factor[0], jnp.where(upper, half, 0), half, 0)
    plane_of = {band_of(plane, planes): plane for plane in range(planes)}
    pairs = []
    for plane in range(planes):
        for group in range(groups):
            target = plane_of[min(group, groups - 1 - group)]
            pairs.append((plane * groups + group, target * groups + 2 * plane + (group >= groups // 2)))
    middle = factor.shape[2] // 2
    low = lax.ppermute(mine[:, :middle], ("tm", "det"), pairs)
    high = lax.ppermute(mine[:, middle:], ("tm", "det"), [pair for pair in pairs if 2 * (pair[0] // groups) >= planes])
    return low, high


def band_factor(sides, groups):
    share = jnp.concatenate(sides, axis=1)
    rows, columns = share.shape
    share = jnp.stack([share] + [swap(share, "det", mask) for mask in range(2, groups, 2)])
    share = jnp.concatenate([share, swap(share, "det", 1)])
    whole = array(groups * rows, columns, dtype=jnp.bfloat16)
    return call(factor_kernel, [whole, whole], [], FACTOR_WORK, share)


def bind(kernel, *static):
    return lambda *refs: kernel(*static, *refs)


def local(noise, factor):
    planes = lax.axis_size("tm")
    groups = lax.axis_size("det")
    rows, span = noise.shape
    own = rows // planes
    n2 = LANES // 2 * planes
    n1 = span * planes // 2 // n2
    pieces = n1 // groups
    chunks = CHUNKS if own % (8 * CHUNKS) == 0 else 1
    dets = own // chunks
    flops = 3 * 2 * n1 * own * (2 * n2) ** 2
    tables = (twiddles(n1, n2), *fourier_matrix(n2, planes))

    parts = call(
        slice_kernel, [array(own, span)] * planes, [dma(planes)], 0, noise.reshape(planes, own, span), spaces=[pl.ANY],
        out_space=pl.ANY,
    )
    layout = (groups, planes, chunks, pieces, dets, LANES)

    def exchange(value):
        value = value.reshape(groups * planes, pieces * own, LANES)
        return lax.all_to_all(value, ("det", "tm"), split_axis=0, concat_axis=0, tiled=True).reshape(layout)

    (spectrum,) = call(
        bind(forward_kernel, n1, n2, planes), [array(*layout)],
        [(planes, own, span), (chunks, n1 * dets, 2 * n2), layout, dma(chunks)], flops, *trade(parts, farthest_first), *tables, out_space=pl.ANY,
    )
    sides = plane_factor(factor, planes, groups)
    f_high, f_low = band_factor(sides, groups)

    count = f_high.shape[0]
    (mixed,) = call(
        mix_kernel, [array(*layout)], [(count, pieces * LANES)],
        2 * 3 * count * count * pieces * LANES, exchange(spectrum), f_high, f_low,
    )
    back = exchange(mixed)
    result = []
    for chunk in range(chunks):
        parts = call(
            bind(inverse_kernel, n1, n2, chunk), [array(dets, span)] * planes,
            [(planes, dets, span), (n1 * dets, 2 * n2)], flops // chunks, back, *tables,
        )
        result = call(
            bind(place_kernel, chunk), [array(planes, chunks, dets, span)], [dma(planes)], 0, *trade(parts, half_first), *result,
            spaces=[pl.ANY] * (planes + len(result)), out_space=pl.ANY, aliases={planes: 0} if result else None,
        )
    return result[0].reshape(rows, span)


def solution(mesh):
    in_specs = (P("det", "tm"), P("det", "tm", None))
    return jax.shard_map(local, mesh=mesh, in_specs=in_specs, out_specs=P("det", "tm"), check_vma=False)
```
